256 devices in a mesh: ctx: 16 (over x_lo, z), head: 4 (over y), dp: 4 (over x_hi, core).
Axes of the slice: x: 4 (x_hi: 2, x_lo: 2; x = x_hi * 2 + x_lo), y: 4, z: 8, core: 2. Of those that a mesh axis runs over, the one named last changes fastest.
Arguments:
- qkv: bfloat16 [3, 10240, 2560], P(None, ('dp', 'ctx'), 'head'), parts along dimension 1, may hold values from -200 to 200
- tangent: bfloat16 [3, 10240, 2560], P(None, ('dp', 'ctx'), 'head'), parts along dimension 1, may hold values from -6 to 6
- segments: int32 [10240], P(('dp', 'ctx')), parts along dimension 0, may hold values from 0 to 3, never falling along the last dimension, each value on 1 to 1600 neighbouring positions
- out_weight: bfloat16 [2560, 5120], P('head', 'ctx'), may hold values from -0.625 to 0.625
Outputs:
- output: bfloat16 [10240, 5120], P(('dp', 'ctx'), 'head'), parts along dimension 0
- output_tangent: bfloat16 [10240, 5120], P(('dp', 'ctx'), 'head'), parts along dimension 0
The draws below stay inside these ranges and needn't reach their ends.
There are 4 independent parts, one for each index of `dp`. The reference program is written for one: setup_inputs(seed, part) draws one part's arguments, and reference() takes and returns one part's arrays. A program takes and returns all parts, laid end to end along the dimension named above; an argument that names none is the same for every part. Nothing has to cross between parts.
Inputs may be any that keep to these rules, and one draw needn't show every extreme that they name: `segments`: numbers never fall along the sample; every number of 0 to 3 occurs; one video holds exactly 1600 tokens and none more.
All inputs are finite; a program needn't handle non-finite values.
Results may differ from the reference program's by a relative error of at most 0.017.
Values may be sent and summed in bfloat16 or wider, within the bound.
A program may use at most 64 MiB of HBM per device.

```python
import math
import jax
import jax.numpy as jnp
import numpy as np
from jax import lax

D = 5120
HD = 128
TOK_DEV = 160
SEGS = 4
HEADS = 20
SEQ = 2560
SEG_MOST = 1600


def draw_qkv(key, part):
    key = jax.random.fold_in(key, 7)
    keys = jax.random.split(key, 1)
    base = jnp.clip(jax.random.normal(keys[0], (3, SEQ, HEADS * HD), jnp.float32), -6.0, 6.0)
    lift = jnp.array([2.0, 1.0, 1.0], jnp.float32).reshape(3, 1, 1)
    return (base * lift).astype(jnp.bfloat16)


def shard_levels(key, shape, shards, smallest, high):
    loudness, own = 1.0, jax.random.fold_in(key, 6)
    for dim, parts in shards:
        steps = jnp.exp(jax.random.uniform(jax.random.fold_in(own, dim), (parts,), jnp.float32, smallest / len(shards), high / len(shards)))
        loudness = loudness * jnp.repeat(steps, shape[dim] // parts).reshape([-1 if axis == dim else 1 for axis in range(len(shape))])
    return loudness


def length_profile(amount, total, reach, slope):
    weights = [(1 << 20) // math.isqrt(standing ** slope) + 1 for standing in range(2, amount + 1)]
    spare, given = total - reach - (amount - 1), [1] * (amount - 1)
    while spare > 0:
        free = [i for i in range(amount - 1) if given[i] < reach]
        pool, budget = sum([weights[i] for i in free]), spare
        for i in free:
            more = min(reach - given[i], max(1, budget * weights[i] // pool), spare)
            given[i] = given[i] + more
            spare = spare - more
    return np.array([reach] + given)


def uneven(key, count, total, reach, slope):
    if count == 2:
        one = jax.random.randint(key, (), max(1, total - reach), min(reach, total - 1) + 1)
        return jnp.stack([one, total - one])
    tallies = jnp.asarray(length_profile(count, total, reach, slope), jnp.int32)
    twos = (count - 1) // 2
    source_of, receiver = tallies[1:1 + 2 * twos:2], tallies[2:2 + 2 * twos:2]
    margin = jnp.minimum(source_of - 1, reach - receiver)
    moved = jax.random.randint(jax.random.fold_in(key, 1), (twos,), 0, 1 << 20) % (margin + 1)
    tallies = tallies.at[1:1 + 2 * twos:2].set(source_of - moved).at[2:2 + 2 * twos:2].set(receiver + moved)
    return tallies[jax.random.permutation(jax.random.fold_in(key, 2), count)]


def scatter_about(rng, extent, scale, limit, cuts=(), kind=jnp.bfloat16):
    entries = scale * jax.random.normal(rng, extent, jnp.float32)
    if cuts:
        entries = entries * shard_levels(rng, extent, cuts, -0.22, 0.18)
    return jnp.clip(entries, -limit, limit).astype(kind)


def setup_inputs(seed: int = 0, part: int = 0) -> dict:
    seeds = jax.random.split(jax.random.key(seed), 5)
    part_splits = jax.random.split(jax.random.fold_in(seeds[4], part), 5)
    return {
        "qkv": draw_qkv(jax.random.fold_in(jax.random.fold_in(seeds[4], part), 71), part),
        "tangent": scatter_about(part_splits[1], (3, SEQ, HEADS * HD), 1.0, 6.0, ((1, 16), (2, 4))),
        "segments": jnp.searchsorted(jnp.cumsum(uneven(part_splits[2], SEGS, SEQ, SEG_MOST, 2)), jnp.arange(SEQ), side="right").astype(jnp.int32),
        "out_weight": scatter_about(seeds[3], (HEADS * HD, D), (HEADS * HD // 32) ** -0.5, 0.625, ((0, 4), (1, 16))),
    }


def block_attention(query, query_tan, keys, values, keys_tan, values_tan, seg_rows, seg_keys):
    scale = 1.0 / math.sqrt(HD)
    count = query.shape[0]
    total_keys = keys.shape[0]
    q_three = query.astype(jnp.float32).reshape(count, HEADS, HD)
    qt_three = query_tan.astype(jnp.float32).reshape(count, HEADS, HD)
    k_three = keys.astype(jnp.float32).reshape(total_keys, HEADS, HD)
    kt_three = keys_tan.astype(jnp.float32).reshape(total_keys, HEADS, HD)
    v_three = values.astype(jnp.float32).reshape(total_keys, HEADS, HD)
    vt_three = values_tan.astype(jnp.float32).reshape(total_keys, HEADS, HD)
    scores = jnp.einsum('qhd,khd->qhk', q_three, k_three) * scale
    scores_tan = (jnp.einsum('qhd,khd->qhk', qt_three, k_three) + jnp.einsum('qhd,khd->qhk', q_three, kt_three)) * scale
    same = (seg_rows[:, None] == seg_keys[None, :])[:, None, :]
    scores = jnp.where(same, scores, -1e+30)
    top = lax.optimization_barrier(jnp.max(scores, axis=2, keepdims=True))
    prob = jnp.where(same, jnp.exp(scores - top), 0.0)
    weighted = prob * scores_tan
    total = lax.optimization_barrier(jnp.sum(prob, axis=2))
    drift = lax.optimization_barrier(jnp.sum(weighted, axis=2))
    prob_b = lax.optimization_barrier(prob.astype(jnp.bfloat16)).astype(jnp.float32)
    weighted_b = lax.optimization_barrier(weighted.astype(jnp.bfloat16)).astype(jnp.float32)
    acc = jnp.einsum('qhk,khd->qhd', prob_b, v_three)
    acc_tan = jnp.einsum('qhk,khd->qhd', weighted_b, v_three) + jnp.einsum('qhk,khd->qhd', prob_b, vt_three)
    attn = acc / total[..., None]
    attn_tan = (acc_tan - (drift / total)[..., None] * acc) / total[..., None]
    return (attn.reshape(count, HEADS * HD).astype(jnp.bfloat16), attn_tan.reshape(count, HEADS * HD).astype(jnp.bfloat16))

def reference(qkv, tangent, segments, out_weight):
    blocks = SEQ // TOK_DEV

    def one_block(index):
        start = (index * TOK_DEV).astype(jnp.int32)
        query = lax.dynamic_slice_in_dim(qkv[0], start, TOK_DEV, 0)
        query_tan = lax.dynamic_slice_in_dim(tangent[0], start, TOK_DEV, 0)
        seg_rows = lax.dynamic_slice_in_dim(segments, start, TOK_DEV, 0)
        return block_attention(query, query_tan, qkv[1], qkv[2], tangent[1], tangent[2], seg_rows, segments)
    attn, attn_tan = lax.map(one_block, jnp.arange(blocks, dtype=jnp.int32))
    attn = attn.reshape(SEQ, HEADS * HD)
    attn_tan = attn_tan.reshape(SEQ, HEADS * HD)
    output = jnp.dot(attn, out_weight, preferred_element_type=jnp.float32).astype(jnp.bfloat16)
    output_tangent = jnp.dot(attn_tan, out_weight, preferred_element_type=jnp.float32).astype(jnp.bfloat16)
    return (output, output_tangent)
```

```python
import functools
import math

import jax
import jax.numpy as jnp
from jax import lax
from jax.experimental import pallas as pl
from jax.experimental.pallas import tpu as pltpu
from jax.sharding import PartitionSpec as P

HD = 128
HEADS = 5
BLOCKS = 16
ROWS = 160
SEQ = BLOCKS * ROWS
SLOTS = 6
SEGS = 4
TILE = 256
KTILES = SEQ // TILE
MESH = pl.DeviceIdType.MESH


def place_of(ctx):
    return lax.rem(ctx, 8) * 2 + ctx // 8


def ctx_of(place):
    return lax.rem(place, 2) * 8 + place // 2


def chunk_of(block):
    return (block >= 6).astype(jnp.int32) + (block >= 11).astype(jnp.int32)


def chunk_start(chunk):
    return chunk * 5 + jnp.minimum(chunk, 1)


def send_heads(
    qkv_ref, tan_ref, count_ref, kv_ref, q_ref, counts_ref,
    stage, local_sems, kv_send, kv_recv, q_send, q_recv, n_send, n_recv,
):
    ctx = lax.axis_index("ctx")
    me = place_of(ctx)

    def at(c):
        return {"ctx": c}

    barrier = pltpu.get_barrier_semaphore()
    for step in range(1, BLOCKS):
        pl.semaphore_signal(
            barrier, inc=1, device_id=at(lax.rem(ctx + step, BLOCKS)), device_id_type=MESH
        )
    for head in range(HEADS):
        cols = slice(head * HD, (head + 1) * HD)
        stage[head, 0, :, 0:HD] = qkv_ref[1, :, cols]
        stage[head, 0, :, HD:] = tan_ref[1, :, cols]
        stage[head, 1, :, 0:HD] = qkv_ref[2, :, cols]
        stage[head, 1, :, HD:] = tan_ref[2, :, cols]
        stage[head, 2, :, 0:HD] = tan_ref[0, :, cols]
        stage[head, 2, :, HD:] = qkv_ref[0, :, cols]
    pl.semaphore_wait(barrier, BLOCKS - 1)

    my_chunk = chunk_of(ctx)
    my_slot = ctx - chunk_start(my_chunk)
    rows = pl.ds(pl.multiple_of(ctx * ROWS, ROWS), ROWS)

    def kv_copy(step):
        place = lax.rem(me + step, BLOCKS)
        return place, pltpu.make_async_remote_copy(
            src_ref=stage.at[place // 3, 0:2],
            dst_ref=kv_ref.at[:, rows],
            send_sem=kv_send.at[place],
            recv_sem=kv_recv.at[ctx],
            device_id=at(ctx_of(place)),
            device_id_type=MESH,
        )

    def q_copy(head):
        place = head * 3 + my_chunk
        return place, pltpu.make_async_remote_copy(
            src_ref=stage.at[head, 2],
            dst_ref=q_ref.at[my_slot],
            send_sem=q_send.at[head],
            recv_sem=q_recv.at[my_slot],
            device_id=at(ctx_of(place)),
            device_id_type=MESH,
        )

    def n_copy(step):
        other = lax.rem(ctx + step, BLOCKS)
        return pltpu.make_async_remote_copy(
            src_ref=count_ref,
            dst_ref=counts_ref.at[ctx],
            send_sem=n_send.at[step],
            recv_sem=n_recv.at[ctx],
            device_id=at(other),
            device_id_type=MESH,
        )

    for step in range(1, BLOCKS):
        n_copy(step).start()
    for step in range(1, BLOCKS):
        place, copy = kv_copy(step)
        pl.when(place < 15)(copy.start)
    for head in range(HEADS):
        place, copy = q_copy(head)
        pl.when(place != me)(copy.start)

    own_n = pltpu.make_async_copy(count_ref, counts_ref.at[ctx], local_sems.at[0])
    own_kv = pltpu.make_async_copy(
        stage.at[lax.min(me // 3, HEADS - 1), 0:2], kv_ref.at[:, rows], local_sems.at[1]
    )
    own_q = pltpu.make_async_copy(
        stage.at[lax.min(me // 3, HEADS - 1), 2], q_ref.at[my_slot], local_sems.at[2]
    )
    own_n.start()
    working = me < 15
    chunk = lax.rem(me, 3)
    pl.when(working)(own_kv.start)
    mine = (my_chunk == chunk) & working
    pl.when(mine)(own_q.start)

    own_n.wait()
    pl.when(working)(own_kv.wait)
    pl.when(mine)(own_q.wait)

    for step in range(1, BLOCKS):
        n_copy(step).wait_send()
        place, copy = kv_copy(step)
        pl.when(place < 15)(copy.wait_send)
    for head in range(HEADS):
        place, copy = q_copy(head)
        pl.when(place != me)(copy.wait_send)

    for step in range(1, BLOCKS):
        other = lax.rem(ctx + step, BLOCKS)
        other_rows = pl.ds(pl.multiple_of(other * ROWS, ROWS), ROWS)
        pltpu.make_async_copy(count_ref, counts_ref.at[other], n_recv.at[other]).wait()

        @pl.when(working)
        def _():
            pltpu.make_async_copy(
                stage.at[0, 0:2], kv_ref.at[:, other_rows], kv_recv.at[other]
            ).wait()

    first = chunk_start(chunk)
    for slot in range(SLOTS):
        block = first + slot

        @pl.when(working & (slot < 5 + (chunk == 0).astype(jnp.int32)) & (block != ctx))
        def _():
            pltpu.make_async_copy(stage.at[0, 2], q_ref.at[slot], q_recv.at[slot]).wait()


def attention(counts_ref, kv_ref, q_ref, out_ref, s_ref, st_ref):
    me = place_of(lax.axis_index("ctx"))
    first = chunk_start(lax.rem(me, 3))
    scale = 1.0 / math.sqrt(HD)
    bounds = [counts_ref[v] for v in range(SEGS - 1)]

    def of_position(position, values):
        result = values[SEGS - 1]
        for v in range(SEGS - 2, -1, -1):
            result = jnp.where(position < bounds[v], values[v], result)
        return result

    starts = [jnp.int32(0)] + bounds
    ends = bounds + [jnp.int32(SEQ)]

    @pl.loop(0, 5 + (lax.rem(me, 3) == 0).astype(jnp.int32))
    def _(slot):
        top_row = jnp.minimum(first + slot, BLOCKS - 1) * ROWS
        low = of_position(top_row, starts) // TILE
        high = (of_position(top_row + ROWS - 1, ends) + TILE - 1) // TILE
        position = top_row + lax.broadcasted_iota(jnp.int32, (ROWS, TILE), 0)
        start = of_position(position, starts)
        end = of_position(position, ends)
        column = lax.broadcasted_iota(jnp.int32, (ROWS, TILE), 1)
        query = q_ref[slot, :, HD:]
        both = q_ref[slot]

        def same(tile):
            keys = column + tile * TILE
            return (keys >= start) & (keys < end)

        def first_pass(tile, top):
            keys = pl.ds(pl.multiple_of(tile * TILE, TILE), TILE)
            s = lax.dot_general(
                query, kv_ref[0, keys, 0:HD], (((1,), (1,)), ((), ())),
                preferred_element_type=jnp.float32,
            ) * scale
            s = jnp.where(same(tile), s, -1e30)
            s_ref[tile] = s
            st_ref[tile] = lax.dot_general(
                both, kv_ref[0, keys], (((1,), (1,)), ((), ())),
                preferred_element_type=jnp.float32,
            ) * scale
            return jnp.maximum(top, s)

        top = lax.fori_loop(low, high, first_pass, jnp.full((ROWS, TILE), -1e30, jnp.float32))
        top = jnp.max(top, axis=1, keepdims=True)

        def second_pass(tile, carry):
            total, drift, acc, acc_tan = carry
            keys = pl.ds(pl.multiple_of(tile * TILE, TILE), TILE)
            prob = jnp.where(same(tile), jnp.exp(s_ref[tile] - top), 0.0)
            weighted = prob * st_ref[tile]
            total = total + prob
            drift = drift + weighted
            acc = acc + jnp.dot(
                prob.astype(jnp.bfloat16), kv_ref[1, keys], preferred_element_type=jnp.float32
            )
            acc_tan = acc_tan + jnp.dot(
                weighted.astype(jnp.bfloat16), kv_ref[1, keys, 0:HD],
                preferred_element_type=jnp.float32,
            )
            return total, drift, acc, acc_tan

        zero = jnp.zeros((ROWS, TILE), jnp.float32)
        total, drift, acc, acc_tan = lax.fori_loop(
            low, high, second_pass, (zero, zero, jnp.zeros((ROWS, 2 * HD), jnp.float32),
                                     jnp.zeros((ROWS, HD), jnp.float32))
        )
        total = jnp.sum(total, axis=1, keepdims=True)
        drift = jnp.sum(drift, axis=1, keepdims=True)
        plain = acc[:, 0:HD]
        out_ref[slot, 0] = (plain / total).astype(jnp.bfloat16)
        out_ref[slot, 1] = (
            (acc[:, HD:] + acc_tan - (drift / total) * plain) / total
        ).astype(jnp.bfloat16)


def return_heads(part_ref, attn_ref, landing, local_sem, send_sems, recv_sems):
    ctx = lax.axis_index("ctx")
    me = place_of(ctx)

    def at(c):
        return {"ctx": c}

    barrier = pltpu.get_barrier_semaphore()
    for step in range(1, BLOCKS):
        pl.semaphore_signal(
            barrier, inc=1, device_id=at(lax.rem(ctx + step, BLOCKS)), device_id_type=MESH
        )
    pl.semaphore_wait(barrier, BLOCKS - 1)

    head = me // 3
    chunk = lax.rem(me, 3)
    first = chunk_start(chunk)
    working = me < 15

    def copy_of(slot):
        block = lax.min(first + slot, BLOCKS - 1)
        live = working & (slot < 5 + (chunk == 0).astype(jnp.int32))
        safe_head = lax.min(head, HEADS - 1)
        return block, live, pltpu.make_async_remote_copy(
            src_ref=part_ref.at[slot],
            dst_ref=landing.at[safe_head],
            send_sem=send_sems.at[slot],
            recv_sem=recv_sems.at[safe_head],
            device_id=at(block),
            device_id_type=MESH,
        ), pltpu.make_async_copy(part_ref.at[slot], landing.at[safe_head], local_sem)

    for slot in range(SLOTS):
        block, live, copy, own = copy_of(slot)
        pl.when(live & (block != ctx))(copy.start)

        @pl.when(live & (block == ctx))
        def _():
            own.start()
            own.wait()

    for slot in range(SLOTS):
        block, live, copy, own = copy_of(slot)
        pl.when(live & (block != ctx))(copy.wait_send)

    my_chunk = chunk_of(ctx)
    for h in range(HEADS):
        place = h * 3 + my_chunk

        @pl.when(place != me)
        def _():
            pltpu.make_async_copy(part_ref.at[0], landing.at[h], recv_sems.at[h]).wait()

        attn_ref[:, :, h * HD:(h + 1) * HD] = landing[h]


def local(qkv, tangent, segments, out_weight):
    vmem = pl.BlockSpec(memory_space=pltpu.VMEM)
    hbm = pl.BlockSpec(memory_space=pl.ANY)
    dma = pltpu.SemaphoreType.DMA
    weights = lax.all_gather(out_weight, "ctx", axis=1, tiled=True)
    below = jnp.sum(
        (segments[:, None] < jnp.arange(1, 129, dtype=jnp.int32)[None, :]).astype(jnp.int32), axis=0
    )
    count = jnp.broadcast_to(below[None, :], (8, 128))
    kv, query, counts = pl.pallas_call(
        send_heads,
        out_shape=(
            jax.ShapeDtypeStruct((2, SEQ, 2 * HD), jnp.bfloat16),
            jax.ShapeDtypeStruct((SLOTS, ROWS, 2 * HD), jnp.bfloat16),
            jax.ShapeDtypeStruct((BLOCKS, 8, 128), jnp.int32),
        ),
        in_specs=[vmem] * 3,
        out_specs=(hbm, hbm, hbm),
        scratch_shapes=[
            pltpu.VMEM((HEADS, 3, ROWS, 2 * HD), jnp.bfloat16),
            dma((3,)), dma((BLOCKS,)), dma((BLOCKS,)), dma((HEADS,)), dma((SLOTS,)),
            dma((BLOCKS,)), dma((BLOCKS,)),
        ],
        compiler_params=pltpu.CompilerParams(
            collective_id=0, has_side_effects=True, vmem_limit_bytes=24 * 2**20
        ),
        name="send_heads",
    )(qkv, tangent, count)
    bounds = jnp.sum(counts[:, 0, 0:8], axis=0)
    part = pl.pallas_call(
        attention,
        out_shape=jax.ShapeDtypeStruct((SLOTS, 2, ROWS, HD), jnp.bfloat16),
        in_specs=[pl.BlockSpec(memory_space=pltpu.SMEM), vmem, vmem],
        out_specs=vmem,
        scratch_shapes=[
            pltpu.VMEM((KTILES, ROWS, TILE), jnp.float32),
            pltpu.VMEM((KTILES, ROWS, TILE), jnp.float32),
        ],
        compiler_params=pltpu.CompilerParams(vmem_limit_bytes=32 * 2**20),
        name="attention",
    )(bounds, kv, query)
    attn = pl.pallas_call(
        return_heads,
        out_shape=jax.ShapeDtypeStruct((2, ROWS, HEADS * HD), jnp.bfloat16),
        in_specs=[vmem],
        out_specs=vmem,
        scratch_shapes=[
            pltpu.VMEM((HEADS, 2, ROWS, HD), jnp.bfloat16),
            dma, dma((SLOTS,)), dma((HEADS,)),
        ],
        compiler_params=pltpu.CompilerParams(
            collective_id=1, has_side_effects=True, vmem_limit_bytes=16 * 2**20
        ),
        name="return_heads",
    )(part)
    terms = jnp.einsum("srw,wc->src", attn, weights, preferred_element_type=jnp.float32)
    summed = lax.psum_scatter(
        terms.astype(jnp.bfloat16), "head", scatter_dimension=2, tiled=True
    )
    return (summed[0], summed[1])


def solution(mesh):
    return jax.shard_map(
        local,
        mesh=mesh,
        in_specs=(
            P(None, ("dp", "ctx"), "head"),
            P(None, ("dp", "ctx"), "head"),
            P(("dp", "ctx")),
            P("head", "ctx"),
        ),
        out_specs=(P(("dp", "ctx"), "head"), P(("dp", "ctx"), "head")),
        check_vma=False,
    )
```

```python
import functools
import math

import jax
import jax.numpy as jnp
from jax import lax
from jax.experimental import pallas as pl
from jax.experimental.pallas import tpu as pltpu
from jax.sharding import PartitionSpec as P

HD = 128
HEADS = 5
BLOCKS = 16
ROWS = 160
SEQ = BLOCKS * ROWS
SLOTS = 6
SEGS = 4
TILE = 256
KTILES = SEQ // TILE
MESH = pl.DeviceIdType.MESH


def place_of(ctx):
    return lax.rem(ctx, 8) * 2 + ctx // 8


def ctx_of(place):
    return lax.rem(place, 2) * 8 + place // 2


def chunk_of(block):
    return (block >= 6).astype(jnp.int32) + (block >= 11).astype(jnp.int32)


def chunk_start(chunk):
    return chunk * 5 + jnp.minimum(chunk, 1)


def signal_if(condition, semaphore, device):
    @pl.when(condition)
    def _():
        pl.semaphore_signal(semaphore, inc=1, device_id=device, device_id_type=MESH)


class Weights:
    def __init__(self, shard_ref, weight_ref, local_sem, *sems):
        self.shard, self.weight, self.local_sem = shard_ref, weight_ref, local_sem
        (self.y_send, self.y_recv, self.z_send, self.z_recv,
         self.x_send, self.x_recv, self.c_send, self.c_recv) = sems
        self.ctx, self.y, dp = lax.axis_index("ctx"), lax.axis_index("head"), lax.axis_index("dp")
        self.x_lo, self.z = self.ctx // 8, lax.rem(self.ctx, 8)
        self.x_hi, self.core = dp // 2, lax.rem(dp, 2)
        self.x = self.x_hi * 2 + self.x_lo
        self.active = lax.rem(self.z, 2) == self.core
        self.parity = lax.rem(self.z // 4 + self.y, 2)

    def device(self, x=None, z=None, y=None, core=None):
        x = self.x if x is None else x
        z = self.z if z is None else z
        y = self.y if y is None else y
        core = self.core if core is None else core
        return {"ctx": lax.rem(x, 2) * 8 + z, "head": y, "dp": (x // 2) * 2 + core}

    def first_target(self, same):
        y = self.x_lo * 2 + self.z // 4
        x = self.x if same else self.x_hi * 2 + 1 - self.x_lo
        z = lax.rem(self.z + 4 * lax.rem(self.y, 2), 8)
        is_me = (x == self.x) & (y == self.y) & (z == self.z)
        return x, z, y, is_me

    def first_source(self, half):
        y = 2 * half + self.parity
        x = self.x_hi * 2 + self.y // 2
        z = lax.rem(self.z + 4 * self.parity, 8)
        is_me = (x == self.x) & (y == self.y) & (z == self.z)
        return x, z, y, is_me

    def greet(self, barrier):
        for half in range(2):
            x, z, y, is_me = self.first_source(half)
            signal_if(self.active & jnp.logical_not(is_me), barrier, self.device(x, z, y))
        for step in range(1, 4):
            signal_if(True, barrier, self.device(x=lax.rem(self.x + step, 4)))
        signal_if(True, barrier, self.device(core=1 - self.core))

    def greetings(self):
        count = jnp.int32(4)
        for same in (True, False):
            is_me = self.first_target(same)[3]
            count = count + (self.active & jnp.logical_not(is_me)).astype(jnp.int32)
        return count

    def piece(self, zq, parity, x):
        return self.weight.at[zq, parity, x]

    def landed(self, ref, sem):
        pltpu.make_async_copy(ref, ref, sem).wait()

    def remote(self, src, dst, send, recv, device):
        return pltpu.make_async_remote_copy(
            src_ref=src, dst_ref=dst, send_sem=send, recv_sem=recv, device_id=device,
            device_id_type=MESH,
        )

    def first(self, index):
        x, z, y, is_me = self.first_target(index == 0)
        dst = self.weight.at[lax.rem(self.z, 4), lax.rem(self.y, 2), x, self.y // 2]
        far = self.remote(
            self.shard.at[x], dst, self.y_send.at[index], self.y_recv.at[self.y // 2],
            self.device(x, z, y),
        )
        return is_me, far, dst

    def over_y(self):
        for index in range(2):
            is_me, far, dst = self.first(index)
            pl.when(self.active & jnp.logical_not(is_me))(far.start)

            @pl.when(self.active & is_me)
            def _():
                x = self.first_target(index == 0)[0]
                pltpu.make_async_copy(self.shard.at[x], dst, self.local_sem).start()

    def second(self, step):
        mine = self.piece(lax.rem(self.z, 4), self.parity, self.x)
        return self.remote(
            mine, mine, self.z_send.at[step], self.z_recv.at[self.z // 2],
            self.device(z=lax.rem(self.z + step, 8)),
        )

    def over_z(self):
        @pl.when(self.active)
        def _():
            for index in range(2):
                is_me, far, dst = self.first(index)
                pl.when(jnp.logical_not(is_me))(far.wait_send)
            for half in range(2):
                is_me = self.first_source(half)[3]
                dst = self.weight.at[lax.rem(self.z, 4), self.parity, self.x, half]

                @pl.when(is_me)
                def _():
                    self.landed(dst, self.local_sem)

                @pl.when(jnp.logical_not(is_me))
                def _():
                    self.landed(dst, self.y_recv.at[half])
            for step in (1, 7, 2, 6, 3, 5, 4):
                self.second(step).start()

    def from_z(self, index):
        z = 2 * index + self.core
        return z, lax.rem(z, 4), lax.rem(z // 4 + self.y, 2)

    def order(self, step):
        return lax.rem(self.z // 2 + step, 4)

    def third(self, index, step):
        z, zq, parity = self.from_z(index)
        mine = self.piece(zq, parity, self.x)
        return self.remote(
            mine, mine, self.x_send.at[step - 1, index], self.x_recv.at[self.x, index],
            self.device(x=lax.rem(self.x + step, 4)),
        )

    def fourth(self, index, x):
        z, zq, parity = self.from_z(index)
        mine = self.piece(zq, parity, x)
        return self.remote(
            mine, mine, self.c_send.at[x, index], self.c_recv.at[x, index],
            self.device(core=1 - self.core),
        )

    def over_x(self):
        for turn in range(4):
            index = self.order(turn)
            z, zq, parity = self.from_z(index)

            @pl.when(z != self.z)
            def _():
                self.landed(self.piece(zq, parity, self.x), self.z_recv.at[index])
            for step in (1, 3, 2):
                self.third(index, step).start()
            self.fourth(index, self.x).start()

    def over_cores(self):
        for step in (1, 3, 2):
            x = lax.rem(self.x + step, 4)
            for turn in range(4):
                index = self.order(turn)
                z, zq, parity = self.from_z(index)
                self.landed(self.piece(zq, parity, x), self.x_recv.at[x, index])
                self.fourth(index, x).start()

        @pl.when(self.active)
        def _():
            for step in range(1, 8):
                self.second(step).wait_send()
        for index in range(4):
            for step in range(1, 4):
                self.third(index, step).wait_send()
        for x in range(4):
            for index in range(4):
                self.fourth(index, x).wait_send()
                z = 2 * index + 1 - self.core
                other = self.piece(lax.rem(z, 4), lax.rem(z // 4 + self.y, 2), x)
                self.landed(other, self.c_recv.at[x, index])


def send_heads(
    qkv_ref, tan_ref, count_ref, shard_ref, kv_ref, q_ref, counts_ref, weight_ref,
    stage, local_sems, kv_send, kv_recv, q_send, q_recv, n_send, n_recv,
    y_send, y_recv, z_send, z_recv, x_send, x_recv, c_send, c_recv,
):
    ctx = lax.axis_index("ctx")
    me = place_of(ctx)
    weights = Weights(
        shard_ref, weight_ref, local_sems.at[3],
        y_send, y_recv, z_send, z_recv, x_send, x_recv, c_send, c_recv,
    )

    def at(c):
        return {"ctx": c}

    barrier = pltpu.get_barrier_semaphore()
    for step in range(1, BLOCKS):
        pl.semaphore_signal(
            barrier, inc=1, device_id=at(lax.rem(ctx + step, BLOCKS)), device_id_type=MESH
        )
    weights.greet(barrier)
    for head in range(HEADS):
        cols = slice(head * HD, (head + 1) * HD)
        stage[head, 0, :, 0:HD] = qkv_ref[1, :, cols]
        stage[head, 0, :, HD:] = tan_ref[1, :, cols]
        stage[head, 1, :, 0:HD] = qkv_ref[2, :, cols]
        stage[head, 1, :, HD:] = tan_ref[2, :, cols]
        stage[head, 2, :, 0:HD] = tan_ref[0, :, cols]
        stage[head, 2, :, HD:] = qkv_ref[0, :, cols]
    pl.semaphore_wait(barrier, BLOCKS - 1 + weights.greetings())
    weights.over_y()

    my_chunk = chunk_of(ctx)
    my_slot = ctx - chunk_start(my_chunk)
    rows = pl.ds(pl.multiple_of(ctx * ROWS, ROWS), ROWS)

    def kv_copy(step):
        place = lax.rem(me + step, BLOCKS)
        return place, pltpu.make_async_remote_copy(
            src_ref=stage.at[place // 3, 0:2],
            dst_ref=kv_ref.at[:, rows],
            send_sem=kv_send.at[place],
            recv_sem=kv_recv.at[ctx],
            device_id=at(ctx_of(place)),
            device_id_type=MESH,
        )

    def q_copy(head):
        place = head * 3 + my_chunk
        return place, pltpu.make_async_remote_copy(
            src_ref=stage.at[head, 2],
            dst_ref=q_ref.at[my_slot],
            send_sem=q_send.at[head],
            recv_sem=q_recv.at[my_slot],
            device_id=at(ctx_of(place)),
            device_id_type=MESH,
        )

    def n_copy(step):
        other = lax.rem(ctx + step, BLOCKS)
        return pltpu.make_async_remote_copy(
            src_ref=count_ref,
            dst_ref=counts_ref.at[ctx],
            send_sem=n_send.at[step],
            recv_sem=n_recv.at[ctx],
            device_id=at(other),
            device_id_type=MESH,
        )

    for step in range(1, BLOCKS):
        n_copy(step).start()
    for head in range(HEADS):
        place, copy = q_copy(head)
        pl.when(place != me)(copy.start)
    weights.over_z()
    for step in range(1, BLOCKS):
        place, copy = kv_copy(step)
        pl.when(place < 15)(copy.start)

    own_n = pltpu.make_async_copy(count_ref, counts_ref.at[ctx], local_sems.at[0])
    own_kv = pltpu.make_async_copy(
        stage.at[lax.min(me // 3, HEADS - 1), 0:2], kv_ref.at[:, rows], local_sems.at[1]
    )
    own_q = pltpu.make_async_copy(
        stage.at[lax.min(me // 3, HEADS - 1), 2], q_ref.at[my_slot], local_sems.at[2]
    )
    own_n.start()
    working = me < 15
    chunk = lax.rem(me, 3)
    pl.when(working)(own_kv.start)
    mine = (my_chunk == chunk) & working
    pl.when(mine)(own_q.start)

    weights.over_x()
    weights.over_cores()

    own_n.wait()
    pl.when(working)(own_kv.wait)
    pl.when(mine)(own_q.wait)

    for step in range(1, BLOCKS):
        n_copy(step).wait_send()
        place, copy = kv_copy(step)
        pl.when(place < 15)(copy.wait_send)
    for head in range(HEADS):
        place, copy = q_copy(head)
        pl.when(place != me)(copy.wait_send)

    for step in range(1, BLOCKS):
        other = lax.rem(ctx + step, BLOCKS)
        other_rows = pl.ds(pl.multiple_of(other * ROWS, ROWS), ROWS)
        pltpu.make_async_copy(count_ref, counts_ref.at[other], n_recv.at[other]).wait()

        @pl.when(working)
        def _():
            pltpu.make_async_copy(
                stage.at[0, 0:2], kv_ref.at[:, other_rows], kv_recv.at[other]
            ).wait()

    first = chunk_start(chunk)
    for slot in range(SLOTS):
        block = first + slot

        @pl.when(working & (slot < 5 + (chunk == 0).astype(jnp.int32)) & (block != ctx))
        def _():
            pltpu.make_async_copy(stage.at[0, 2], q_ref.at[slot], q_recv.at[slot]).wait()


def attention(counts_ref, kv_ref, q_ref, out_ref, s_ref, st_ref):
    me = place_of(lax.axis_index("ctx"))
    first = chunk_start(lax.rem(me, 3))
    scale = 1.0 / math.sqrt(HD)
    bounds = [counts_ref[v] for v in range(SEGS - 1)]

    def of_position(position, values):
        result = values[SEGS - 1]
        for v in range(SEGS - 2, -1, -1):
            result = jnp.where(position < bounds[v], values[v], result)
        return result

    starts = [jnp.int32(0)] + bounds
    ends = bounds + [jnp.int32(SEQ)]

    @pl.loop(0, 5 + (lax.rem(me, 3) == 0).astype(jnp.int32))
    def _(slot):
        top_row = jnp.minimum(first + slot, BLOCKS - 1) * ROWS
        low = of_position(top_row, starts) // TILE
        high = (of_position(top_row + ROWS - 1, ends) + TILE - 1) // TILE
        position = top_row + lax.broadcasted_iota(jnp.int32, (ROWS, TILE), 0)
        start = of_position(position, starts)
        end = of_position(position, ends)
        column = lax.broadcasted_iota(jnp.int32, (ROWS, TILE), 1)
        query = q_ref[slot, :, HD:]
        both = q_ref[slot]

        def same(tile):
            keys = column + tile * TILE
            return (keys >= start) & (keys < end)

        def first_pass(tile, top):
            keys = pl.ds(pl.multiple_of(tile * TILE, TILE), TILE)
            s = lax.dot_general(
                query, kv_ref[0, keys, 0:HD], (((1,), (1,)), ((), ())),
                preferred_element_type=jnp.float32,
            ) * scale
            s = jnp.where(same(tile), s, -1e30)
            s_ref[tile] = s
            st_ref[tile] = lax.dot_general(
                both, kv_ref[0, keys], (((1,), (1,)), ((), ())),
                preferred_element_type=jnp.float32,
            ) * scale
            return jnp.maximum(top, s)

        top = lax.fori_loop(low, high, first_pass, jnp.full((ROWS, TILE), -1e30, jnp.float32))
        top = jnp.max(top, axis=1, keepdims=True)

        def second_pass(tile, carry):
            total, drift, acc, acc_tan = carry
            keys = pl.ds(pl.multiple_of(tile * TILE, TILE), TILE)
            prob = jnp.where(same(tile), jnp.exp(s_ref[tile] - top), 0.0)
            weighted = prob * st_ref[tile]
            total = total + prob
            drift = drift + weighted
            acc = acc + jnp.dot(
                prob.astype(jnp.bfloat16), kv_ref[1, keys], preferred_element_type=jnp.float32
            )
            acc_tan = acc_tan + jnp.dot(
                weighted.astype(jnp.bfloat16), kv_ref[1, keys, 0:HD],
                preferred_element_type=jnp.float32,
            )
            return total, drift, acc, acc_tan

        zero = jnp.zeros((ROWS, TILE), jnp.float32)
        total, drift, acc, acc_tan = lax.fori_loop(
            low, high, second_pass, (zero, zero, jnp.zeros((ROWS, 2 * HD), jnp.float32),
                                     jnp.zeros((ROWS, HD), jnp.float32))
        )
        total = jnp.sum(total, axis=1, keepdims=True)
        drift = jnp.sum(drift, axis=1, keepdims=True)
        plain = acc[:, 0:HD]
        out_ref[slot, 0] = (plain / total).astype(jnp.bfloat16)
        out_ref[slot, 1] = (
            (acc[:, HD:] + acc_tan - (drift / total) * plain) / total
        ).astype(jnp.bfloat16)


def project(
    part_ref, weight_ref, out_ref, out_tan_ref,
    landing, rows_ref, main, packed, rest, acc,
    local_sem, w_sems, send_sems, recv_sems, y_send, y_recv,
):
    ctx = lax.axis_index("ctx")
    y = lax.axis_index("head")
    me = place_of(ctx)

    def at(c):
        return {"ctx": c}

    barrier = pltpu.get_barrier_semaphore()
    for step in range(1, BLOCKS):
        signal_if(True, barrier, at(lax.rem(ctx + step, BLOCKS)))
    for step in range(1, 4):
        signal_if(True, barrier, {"head": lax.rem(y + step, 4)})

    moves = []
    for quarter, first, count, group, row in (
        (0, 0, 400, 0, 0), (1, 0, 240, 0, 400), (1, 240, 160, 1, 0),
        (2, 0, 400, 1, 160), (3, 0, 80, 1, 560), (3, 80, 320, 2, 0),
    ):
        for zq in range(4):
            for parity in range(2):
                dst = (
                    packed.at[zq, parity] if group == 2 else
                    main.at[zq, parity, :, row:row + count, group * HD:(group + 1) * HD]
                )
                moves.append(pltpu.make_async_copy(
                    weight_ref.at[zq, parity, quarter, :, first:first + count], dst,
                    w_sems.at[len(moves)],
                ))
    for move in moves:
        move.start()
    pl.semaphore_wait(barrier, BLOCKS - 1 + 3)

    head = me // 3
    chunk = lax.rem(me, 3)
    first = chunk_start(chunk)
    working = me < 15

    def copy_of(slot):
        block = lax.min(first + slot, BLOCKS - 1)
        live = working & (slot < 5 + (chunk == 0).astype(jnp.int32))
        safe_head = lax.min(head, HEADS - 1)
        return block, live, pltpu.make_async_remote_copy(
            src_ref=part_ref.at[slot],
            dst_ref=landing.at[y, safe_head],
            send_sem=send_sems.at[slot],
            recv_sem=recv_sems.at[safe_head],
            device_id=at(block),
            device_id_type=MESH,
        ), landing.at[y, safe_head]

    for slot in range(SLOTS):
        block, live, copy, own = copy_of(slot)
        pl.when(live & (block != ctx))(copy.start)

        @pl.when(live & (block == ctx))
        def _():
            local = pltpu.make_async_copy(part_ref.at[slot], own, local_sem)
            local.start()
            local.wait()

    for move in moves:
        move.wait()
    for zq in range(4):
        for parity in range(2):
            for half in range(2):
                for side in range(2):
                    rest[parity, half, side * 320:(side + 1) * 320, zq * 64:(zq + 1) * 64] = (
                        packed[zq, parity, half, :, side * 64:(side + 1) * 64]
                    )

    my_chunk = chunk_of(ctx)

    def to_y(h, step):
        return pltpu.make_async_remote_copy(
            src_ref=landing.at[y, h],
            dst_ref=landing.at[y, h],
            send_sem=y_send.at[h, step - 1],
            recv_sem=y_recv.at[y, h],
            device_id={"head": lax.rem(y + step, 4)},
            device_id_type=MESH,
        )

    for h in range(HEADS):
        @pl.when(h * 3 + my_chunk != me)
        def _():
            pltpu.make_async_copy(part_ref.at[0], landing.at[y, h], recv_sems.at[h]).wait()
        for step in (2, 1, 3):
            to_y(h, step).start()

    for turn, step in enumerate((0, 1, 3, 2)):
        other = lax.rem(y + step, 4)
        for h in range(HEADS):
            if step:
                pltpu.make_async_copy(part_ref.at[0], landing.at[other, h], y_recv.at[other, h]).wait()
            for kind in range(2):
                rows_ref[kind * ROWS:(kind + 1) * ROWS, h * HD:(h + 1) * HD] = landing[other, h, kind]
        parity, half = lax.rem(other, 2), other // 2
        for zq in range(5):
            weight = main[zq, parity, half] if zq < 4 else rest[parity, half]
            term = jnp.dot(rows_ref[...], weight, preferred_element_type=jnp.float32)
            acc[zq] = term if turn == 0 else acc[zq] + term

    for zq in range(4):
        for kind, ref in enumerate((out_ref, out_tan_ref)):
            rows = slice(kind * ROWS, (kind + 1) * ROWS)
            ref[:, zq * 320:zq * 320 + 256] = acc[zq, rows].astype(jnp.bfloat16)
            ref[:, zq * 320 + 256:(zq + 1) * 320] = (
                acc[4, rows, zq * 64:(zq + 1) * 64].astype(jnp.bfloat16)
            )

    for slot in range(SLOTS):
        block, live, copy, own = copy_of(slot)
        pl.when(live & (block != ctx))(copy.wait_send)
    for h in range(HEADS):
        for step in range(1, 4):
            to_y(h, step).wait_send()


def local(qkv, tangent, segments, out_weight):
    vmem = pl.BlockSpec(memory_space=pltpu.VMEM)
    hbm = pl.BlockSpec(memory_space=pl.ANY)
    dma = pltpu.SemaphoreType.DMA
    shard = jnp.concatenate(
        [out_weight[:, 0:128], out_weight[:, 128:256],
         jnp.concatenate([out_weight[0:320, 256:], out_weight[320:, 256:]], axis=1)], axis=0
    ).reshape(4, 400, 128)
    below = jnp.sum(
        (segments[:, None] < jnp.arange(1, 129, dtype=jnp.int32)[None, :]).astype(jnp.int32), axis=0
    )
    count = jnp.broadcast_to(below[None, :], (8, 128))
    kv, query, counts, weights = pl.pallas_call(
        send_heads,
        out_shape=(
            jax.ShapeDtypeStruct((2, SEQ, 2 * HD), jnp.bfloat16),
            jax.ShapeDtypeStruct((SLOTS, ROWS, 2 * HD), jnp.bfloat16),
            jax.ShapeDtypeStruct((BLOCKS, 8, 128), jnp.int32),
            jax.ShapeDtypeStruct((4, 2, 4, 2, 400, 128), jnp.bfloat16),
        ),
        in_specs=[vmem] * 4,
        out_specs=(hbm, hbm, hbm, hbm),
        scratch_shapes=[
            pltpu.VMEM((HEADS, 3, ROWS, 2 * HD), jnp.bfloat16),
            dma((4,)), dma((BLOCKS,)), dma((BLOCKS,)), dma((HEADS,)), dma((SLOTS,)),
            dma((BLOCKS,)), dma((BLOCKS,)),
            dma((2,)), dma((2,)), dma((8,)), dma((4,)), dma((3, 4)), dma((4, 4)), dma((4, 4)), dma((4, 4)),
        ],
        compiler_params=pltpu.CompilerParams(
            collective_id=0, has_side_effects=True, vmem_limit_bytes=24 * 2**20
        ),
        name="send_heads",
    )(qkv, tangent, count, shard)
    bounds = jnp.sum(counts[:, 0, 0:8], axis=0)
    part = pl.pallas_call(
        attention,
        out_shape=jax.ShapeDtypeStruct((SLOTS, 2, ROWS, HD), jnp.bfloat16),
        in_specs=[pl.BlockSpec(memory_space=pltpu.SMEM), vmem, vmem],
        out_specs=vmem,
        scratch_shapes=[
            pltpu.VMEM((KTILES, ROWS, TILE), jnp.float32),
            pltpu.VMEM((KTILES, ROWS, TILE), jnp.float32),
        ],
        compiler_params=pltpu.CompilerParams(vmem_limit_bytes=32 * 2**20),
        name="attention",
    )(bounds, kv, query)
    return pl.pallas_call(
        project,
        out_shape=(jax.ShapeDtypeStruct((ROWS, 1280), jnp.bfloat16),) * 2,
        in_specs=[vmem, hbm],
        out_specs=(vmem, vmem),
        scratch_shapes=[
            pltpu.VMEM((4, HEADS, 2, ROWS, HD), jnp.bfloat16),
            pltpu.VMEM((2 * ROWS, HEADS * HD), jnp.bfloat16),
            pltpu.VMEM((4, 2, 2, 640, 256), jnp.bfloat16),
            pltpu.VMEM((4, 2, 2, 320, 128), jnp.bfloat16),
            pltpu.VMEM((2, 2, 640, 256), jnp.bfloat16),
            pltpu.VMEM((5, 2 * ROWS, 256), jnp.float32),
            dma, dma((48,)), dma((SLOTS,)), dma((HEADS,)), dma((HEADS, 3)), dma((4, HEADS)),
        ],
        compiler_params=pltpu.CompilerParams(
            collective_id=1, has_side_effects=True, vmem_limit_bytes=32 * 2**20
        ),
        name="project",
    )(part, weights)


def solution(mesh):
    return jax.shard_map(
        local,
        mesh=mesh,
        in_specs=(
            P(None, ("dp", "ctx"), "head"),
            P(None, ("dp", "ctx"), "head"),
            P(("dp", "ctx")),
            P("head", "ctx"),
        ),
        out_specs=(P(("dp", "ctx"), "head"), P(("dp", "ctx"), "head")),
        check_vma=False,
    )
```

```python
import functools
import math

import jax
import jax.numpy as jnp
from jax import lax
from jax.experimental import pallas as pl
from jax.experimental.pallas import tpu as pltpu
from jax.sharding import PartitionSpec as P

HD = 128
HEADS = 5
BLOCKS = 16
ROWS = 160
SEQ = BLOCKS * ROWS
SLOTS = 6
SEGS = 4
TILE = 256
PART = 480


def several(kind, first, last):
    return [(kind, turn) for turn in range(first, last)]


ORDERS = (
    several("X", 0, 1) + several("K", 0, 2) + several("X", 1, 3) + several("K", 2, 4) + several("X", 3, 4)
    + several("D", 0, 3) + several("I", 0, 4) + several("D", 3, 8) + several("R", 0, 8),
    several("O", 0, 4),
    several("F", 0, 4),
    [],
)
KTILES = SEQ // TILE
MESH = pl.DeviceIdType.MESH


def role_of(x_lo, core):
    return x_lo * 2 + core


def chunk_of(block):
    return (block >= 6).astype(jnp.int32) + (block >= 11).astype(jnp.int32)


def chunk_start(chunk):
    return chunk * 5 + jnp.minimum(chunk, 1)


def work_of(x_lo, z, core):
    role = role_of(x_lo, core)
    first = jnp.where(role == 3, 4 * (z // 2), chunk_start(role))
    count = jnp.where(role == 3, 4, 5 + (role == 0).astype(jnp.int32))
    return first, count


def worker_of(head, block, core):
    if head == HEADS - 1:
        return 1, 2 * (block // 4) + core, 1
    role = chunk_of(block)
    return role // 2, 2 * head + core, lax.rem(role, 2)


def signal_if(condition, semaphore, device):
    @pl.when(condition)
    def _():
        pl.semaphore_signal(semaphore, inc=1, device_id=device, device_id_type=MESH)


class Both:
    def __init__(self, copies):
        self.copies = copies

    def start(self):
        for copy in self.copies:
            copy.start()

    def wait_send(self):
        for copy in self.copies:
            copy.wait_send()


class Weights:
    def __init__(self, shard_ref, tail_ref, main_ref, packed_ref, local_sems, *sems):
        self.shard, self.tail, self.local_sems = shard_ref, tail_ref, local_sems
        self.main, self.packed = main_ref, packed_ref
        (self.y_send, self.y_recv, self.z_send, self.z_recv,
         self.x_send, self.x_recv, self.c_send, self.c_recv) = sems
        self.ctx, self.y, dp = lax.axis_index("ctx"), lax.axis_index("head"), lax.axis_index("dp")
        self.x_lo, self.z = self.ctx // 8, lax.rem(self.ctx, 8)
        self.x_hi, self.core = dp // 2, lax.rem(dp, 2)
        self.x = self.x_hi * 2 + self.x_lo
        self.inner = self.x_hi * 2 + 1 - self.x_lo
        self.outer = lax.rem(self.x + 3 + 2 * self.x_lo, 4)
        self.far = lax.rem(self.x + 2, 4)
        self.active = lax.rem(self.z, 2) == self.core
        self.parity = lax.rem(self.z // 4 + self.y, 2)

    def prepare(self):
        for quarter in range(4):
            for side in range(2):
                row = quarter * 160 + side * 80
                self.tail[quarter * 80:(quarter + 1) * 80, side * 64:(side + 1) * 64] = (
                    self.shard[row:row + 80, 256:320]
                )

    def device(self, x=None, z=None, y=None, core=None):
        x = self.x if x is None else x
        z = self.z if z is None else z
        y = self.y if y is None else y
        core = self.core if core is None else core
        return {"ctx": lax.rem(x, 2) * 8 + z, "head": y, "dp": (x // 2) * 2 + core}

    def first_target(self, same):
        y = self.x_lo * 2 + self.z // 4
        x = self.x if same else self.x_hi * 2 + 1 - self.x_lo
        z = lax.rem(self.z + 4 * lax.rem(self.y, 2), 8)
        is_me = (x == self.x) & (y == self.y) & (z == self.z)
        return x, z, y, is_me

    def first_source(self, half):
        y = 2 * half + self.parity
        x = self.x_hi * 2 + self.y // 2
        z = lax.rem(self.z + 4 * self.parity, 8)
        is_me = (x == self.x) & (y == self.y) & (z == self.z)
        return x, z, y, is_me

    def greet(self, barrier):
        for half in range(2):
            x, z, y, is_me = self.first_source(half)
            signal_if(self.active & jnp.logical_not(is_me), barrier, self.device(x, z, y))
        for x in (self.inner, self.outer):
            signal_if(True, barrier, self.device(x=x))
        signal_if(True, barrier, self.device(core=1 - self.core))
        for step in (1, 7):
            signal_if(True, barrier, self.device(z=lax.rem(self.z + step, 8)))

    def greetings(self):
        count = jnp.int32(5)
        for same in (True, False):
            is_me = self.first_target(same)[3]
            count = count + (self.active & jnp.logical_not(is_me)).astype(jnp.int32)
        return count

    def rows(self, quarter):
        return (
            pl.ds(pl.multiple_of(quarter * 160, 160), 160),
            pl.ds(pl.multiple_of(quarter * 80, 80), 80),
        )

    def piece(self, zq, parity, x):
        wide, narrow = self.rows(x)
        return self.main.at[zq, parity, :, wide], self.packed.at[zq, parity, :, narrow]

    def landed(self, refs, sems):
        for i, ref in enumerate(refs):
            pltpu.make_async_copy(ref, ref, sems.at[i]).wait()

    def remote(self, srcs, dsts, send, recv, device):
        return Both([
            pltpu.make_async_remote_copy(
                src_ref=src, dst_ref=dst, send_sem=send.at[i], recv_sem=recv.at[i],
                device_id=device, device_id_type=MESH,
            ) for i, (src, dst) in enumerate(zip(srcs, dsts))
        ])

    def first(self, index):
        x, z, y, is_me = self.first_target(index == 0)
        wide, narrow = self.rows(x)
        zq, parity, half = lax.rem(self.z, 4), lax.rem(self.y, 2), self.y // 2
        srcs = self.shard.at[wide, 0:256], self.tail.at[narrow]
        dsts = self.main.at[zq, parity, half, wide], self.packed.at[zq, parity, half, narrow]
        far = self.remote(
            srcs, dsts, self.y_send.at[index], self.y_recv.at[half], self.device(x, z, y)
        )
        return is_me, far, srcs, dsts

    def over_y(self):
        for index in range(2):
            is_me, far, srcs, dsts = self.first(index)
            pl.when(self.active & jnp.logical_not(is_me))(far.start)

            @pl.when(self.active & is_me)
            def _():
                for i in range(2):
                    pltpu.make_async_copy(srcs[i], dsts[i], self.local_sems.at[i]).start()

    def second(self, turn, back):
        z, zq, parity = self.from_z(self.order(turn))
        mine = self.piece(zq, parity, self.x)
        return self.remote(
            mine, mine, self.z_send.at[turn, int(back)], self.z_recv.at[z // 2],
            self.device(z=lax.rem(self.z + (7 if back else 1), 8)),
        )

    def seconds(self):
        passive = jnp.logical_not(self.active)
        return (
            (0, True, self.second(0, False)), (0, self.active, self.second(0, True)),
            (1, self.active, self.second(1, False)), (1, passive, self.second(1, True)),
            (2, passive, self.second(2, False)), (2, self.active, self.second(2, True)),
        )

    def over_z(self):
        @pl.when(self.active)
        def _():
            for index in range(2):
                is_me, far, srcs, dsts = self.first(index)
                pl.when(jnp.logical_not(is_me))(far.wait_send)
            for half in range(2):
                is_me = self.first_source(half)[3]
                wide, narrow = self.rows(self.x)
                zq = lax.rem(self.z, 4)
                dst = (
                    self.main.at[zq, self.parity, half, wide],
                    self.packed.at[zq, self.parity, half, narrow],
                )

                @pl.when(is_me)
                def _():
                    self.landed(dst, self.local_sems)

                @pl.when(jnp.logical_not(is_me))
                def _():
                    self.landed(dst, self.y_recv.at[half])

    def from_z(self, index):
        z = 2 * index + self.core
        return z, lax.rem(z, 4), lax.rem(z // 4 + self.y, 2)

    def order(self, turn):
        step = jnp.where(self.active, (0, 6, 2, 4)[turn], (7, 1, 5, 3)[turn])
        return lax.rem(self.z + step, 8) // 2

    def third(self, index, hop):
        z, zq, parity = self.from_z(index)
        owner = self.inner if hop == 2 else self.x
        mine = self.piece(zq, parity, owner)
        return self.remote(
            mine, mine, self.x_send.at[hop, index], self.x_recv.at[owner, index],
            self.device(x=self.outer if hop else self.inner),
        )

    def fourth(self, index, x):
        z, zq, parity = self.from_z(index)
        mine = self.piece(zq, parity, x)
        return self.remote(
            mine, mine, self.c_send.at[x, index], self.c_recv.at[x, index],
            self.device(core=1 - self.core),
        )

    def start_x(self, turn):
        index = self.order(turn)
        z, zq, parity = self.from_z(index)

        @pl.when(z != self.z)
        def _():
            self.landed(self.piece(zq, parity, self.x), self.z_recv.at[index])
        for other, live, copy in self.seconds():
            if other == turn:
                pl.when(live)(copy.start)
        self.third(index, 0).start()
        self.third(index, 1).start()
        self.fourth(index, self.x).start()

    def pass_on(self, x, turn):
        index = self.order(turn)
        z, zq, parity = self.from_z(index)
        self.landed(self.piece(zq, parity, x), self.x_recv.at[x, index])
        if x is self.inner:
            self.third(index, 2).start()
        self.fourth(index, x).start()

    def arrive(self):
        for x in range(4):
            for index in range(4):
                z = 2 * index + 1 - self.core
                other = self.piece(lax.rem(z, 4), lax.rem(z // 4 + self.y, 2), x)
                self.landed(other, self.c_recv.at[x, index])

    def finish(self):
        for turn, live, copy in self.seconds():
            pl.when(live)(copy.wait_send)
        for index in range(4):
            for hop in range(3):
                self.third(index, hop).wait_send()
        for x in range(4):
            for index in range(4):
                self.fourth(index, x).wait_send()


def layer(
    qkv_hbm, tan_hbm, count_ref, shard_hbm, both_ref,
    qkv_ref, tan_ref, shard_ref, in_sems, stage, kv_ref, q_ref, counts_ref, kt_ref, s_ref, st_ref, top_ref, sum_ref, acc_ref, part_ref,
    tail, main, packed, rest, landing, rows_ref, total_ref,
    local_sems, kv_send, kv_recv, q_send, q_recv, n_send, n_recv, f_send,
    y_send, y_recv, z_send, z_recv, x_send, x_recv, c_send, c_recv,
    back_send, back_recv, g_send, g_recv,
):
    ctx, dp, y = lax.axis_index("ctx"), lax.axis_index("dp"), lax.axis_index("head")
    x_lo, z, x_hi, core = ctx // 8, lax.rem(ctx, 8), dp // 2, lax.rem(dp, 2)
    sample = lax.rem(z, 2)
    role = role_of(x_lo, core)
    first, count = work_of(x_lo, z, core)
    weights = Weights(
        shard_ref, tail, main, packed, local_sems.at[pl.ds(4, 2)],
        y_send, y_recv, z_send, z_recv, x_send, x_recv, c_send, c_recv,
    )

    def at(other_x, other_z, other_core):
        return {"ctx": other_x * 8 + other_z, "dp": x_hi * 2 + other_core}

    def is_me(other_x, other_z, other_core):
        return (other_x == x_lo) & (other_z == z) & (other_core == core)

    def remote(src, dst, send, recv, device):
        return pltpu.make_async_remote_copy(
            src_ref=src, dst_ref=dst, send_sem=send, recv_sem=recv, device_id=at(*device),
            device_id_type=MESH,
        )

    def rows_of(block):
        return pl.ds(pl.multiple_of(block * ROWS, ROWS), ROWS)

    loads = [
        pltpu.make_async_copy(src, dst, in_sems.at[i]) for i, (src, dst) in enumerate(
            ((qkv_hbm, qkv_ref), (tan_hbm, tan_ref), (shard_hbm, shard_ref))
        )
    ]
    for load in loads:
        load.start()
    barrier = pltpu.get_barrier_semaphore()
    for other_x in range(2):
        for step in range(8):
            source = (other_x, lax.rem(z + step, 8), sample)
            signal_if(jnp.logical_not(is_me(*source)), barrier, at(*source))
    for mate in ((1 - x_lo, z, core), (x_lo, z, 1 - core), (1 - x_lo, z, 1 - core)):
        signal_if(True, barrier, at(*mate))
    weights.greet(barrier)
    workers = [worker_of(h, ctx, core) for h in range(HEADS)]
    for worker in workers:
        signal_if(jnp.logical_not(is_me(*worker)), barrier, at(*worker))
    for step in range(1, 4):
        signal_if(True, barrier, {"head": lax.rem(y + step, 4)})
    own_block = (core == sample) & (first <= ctx) & (ctx < first + count)
    for load in loads:
        load.wait()
    weights.prepare()
    for slot in (4, 5):
        @pl.when(slot >= count)
        def _():
            q_ref[slot * ROWS:(slot + 1) * ROWS] = jnp.zeros((ROWS, 2 * HD), jnp.bfloat16)
    for head in range(HEADS):
        cols = slice(head * HD, (head + 1) * HD)
        stage[head, 0, :, 0:HD] = qkv_ref[1, :, cols]
        stage[head, 0, :, HD:] = tan_ref[1, :, cols]
        stage[head, 1, :, 0:HD] = qkv_ref[2, :, cols]
        stage[head, 1, :, HD:] = tan_ref[2, :, cols]
        stage[head, 2, :, 0:HD] = tan_ref[0, :, cols]
        stage[head, 2, :, HD:] = qkv_ref[0, :, cols]
    pl.semaphore_wait(
        barrier,
        22 - (core == sample).astype(jnp.int32) + weights.greetings()
        + count - own_block.astype(jnp.int32),
    )
    weights.over_y()

    sends = []

    def send(device, src, dst, send_sem, recv_sem, local_sem):
        mine = is_me(*device)
        far = remote(src, dst, send_sem, recv_sem, device)
        pl.when(jnp.logical_not(mine))(far.start)

        @pl.when(mine)
        def _():
            pltpu.make_async_copy(src, dst, local_sem).start()
        sends.append((jnp.logical_not(mine), far))

    for other_x in range(2):
        for step in range(4):
            device = (other_x, 2 * lax.rem(z // 2 + step, 4) + core)
            for other_core in range(2):
                send(
                    device + (other_core,), count_ref, counts_ref.at[ctx],
                    n_send.at[other_x, step, other_core], n_recv.at[ctx], local_sems.at[0],
                )
    for head in range(HEADS):
        slot = lax.rem(ctx, 4) if head == 4 else ctx - chunk_start(chunk_of(ctx))
        send(
            worker_of(head, ctx, core), stage.at[head, 2], q_ref.at[rows_of(slot)],
            q_send.at[head], q_recv.at[slot], local_sems.at[2],
        )
    weights.over_z()
    def send_keys(step):
        turn = lax.rem(z // 2 + (0, 1, 3, 2)[step], 4)
        slice_z = 2 * turn + core
        send(
            (x_lo, slice_z, jnp.where(x_lo == 0, core, 0)), stage.at[turn, 0:2],
            kv_ref.at[:, rows_of(ctx)], kv_send.at[0, step], kv_recv.at[ctx], local_sems.at[1],
        )
        send(
            (1, slice_z, 1), stage.at[HEADS - 1, 0:2],
            kv_ref.at[:, rows_of(ctx)], kv_send.at[1, step], kv_recv.at[ctx], local_sems.at[1],
        )

    entry = (x_lo == 0) & (core == sample)
    third = role == 2

    def forward(block, mate, index):
        dst = kv_ref.at[:, rows_of(block)]
        return remote(dst, dst, f_send.at[block, index], kv_recv.at[block], mate)

    def forwards(direct, block):
        to_core = (entry, forward(block, (0, z, 1 - core), 0))
        if direct:
            to_x = forward(block, (1 - x_lo, z, jnp.where(entry, 0, sample)), 1)
            return [to_core, (entry | third, to_x)]
        return [to_core]

    def arrived(block, ref, own_sem, sem):
        mine = (block == ctx) & (core == sample)

        @pl.when(mine)
        def _():
            pltpu.make_async_copy(ref, ref, own_sem).wait()

        @pl.when(jnp.logical_not(mine))
        def _():
            pltpu.make_async_copy(ref, ref, sem).wait()

    def pass_keys(direct, step):
        block = (x_lo if direct else 1 - x_lo) * 8 + lax.rem(z + step, 8)
        arrived(block, kv_ref.at[:, rows_of(block)], local_sems.at[1], kv_recv.at[block])
        for live, copy in forwards(direct, block):
            pl.when(live)(copy.start)

    near = (0, 1, 7, 2, 6, 3, 5, 4)

    def events(order):
        for kind, turn in order:
            if kind in "DR":
                pass_keys(kind == "D", near[turn])
            elif kind == "X":
                weights.start_x(turn)
            elif kind == "K":
                send_keys(turn)
            else:
                x = {"I": weights.inner, "O": weights.outer, "F": weights.far}[kind]
                weights.pass_on(x, turn)

    events(ORDERS[0])
    for direct in (True, False):
        for step in range(8):
            block = (x_lo if direct else 1 - x_lo) * 8 + lax.rem(z + step, 8)
            arrived(block, counts_ref.at[block], local_sems.at[0], n_recv.at[block])
    for slot in range(SLOTS):
        @pl.when(slot < count)
        def _():
            arrived(first + slot, q_ref.at[rows_of(slot)], local_sems.at[2], q_recv.at[slot])

    def back(slot):
        block = lax.min(first + slot, BLOCKS - 1)
        head = jnp.where(role == 3, HEADS - 1, z // 2)
        own = (block == ctx) & (core == sample)
        dst = landing.at[y, head]
        far = pltpu.make_async_remote_copy(
            src_ref=part_ref.at[slot], dst_ref=dst, send_sem=back_send.at[slot],
            recv_sem=back_recv.at[head], device_id={"ctx": block, "dp": x_hi * 2 + sample},
            device_id_type=MESH,
        )
        return (slot < count) & own, (slot < count) & jnp.logical_not(own), far, dst

    scale = 1.0 / math.sqrt(HD)
    power = scale / math.log(2.0)
    below = jnp.sum(counts_ref[...], axis=0)
    bounds = [below[0:1, v:v + 1] for v in range(SEGS - 1)]

    def of_position(position, values):
        result = values[SEGS - 1]
        for v in range(SEGS - 2, -1, -1):
            result = jnp.where(position < bounds[v], values[v], result)
        return result

    starts = [jnp.zeros((1, 1), jnp.int32)] + bounds
    ends = bounds + [jnp.full((1, 1), SEQ, jnp.int32)]

    @pl.loop(0, KTILES)
    def _(tile):
        keys = pl.ds(pl.multiple_of(tile * TILE, TILE), TILE)
        kt_ref[tile] = kv_ref[0, keys].T

    for part in range(2):
        position = (first + 3 * part) * ROWS + lax.broadcasted_iota(jnp.int32, (PART, 1), 0)
        start = of_position(position, starts)
        end = of_position(position, ends)
        column = lax.broadcasted_iota(jnp.int32, (1, TILE), 1)
        rows = slice(part * PART, (part + 1) * PART)
        top_ref[...] = jnp.full((PART, TILE), -1e30, jnp.float32)
        sum_ref[...] = jnp.zeros_like(sum_ref)
        acc_ref[...] = jnp.zeros_like(acc_ref)

        @pl.loop(0, KTILES)
        def _(tile):
            s = jnp.dot(
                q_ref[rows, HD:], kt_ref[tile, 0:HD], preferred_element_type=jnp.float32
            )
            place = column + tile * TILE
            s = jnp.where((place >= start) & (place < end), s, -1e30)
            s_ref[tile] = s
            st_ref[tile] = jnp.dot(
                q_ref[rows, :], kt_ref[tile], preferred_element_type=jnp.float32
            )
            top_ref[...] = jnp.maximum(top_ref[...], s)

        top = jnp.max(top_ref[...], axis=1, keepdims=True)

        @pl.loop(0, KTILES)
        def _(tile):
            keys = pl.ds(pl.multiple_of(tile * TILE, TILE), TILE)
            prob = jnp.exp2((s_ref[tile] - top) * power)
            weighted = prob * st_ref[tile]
            sum_ref[0] += prob
            sum_ref[1] += weighted
            acc_ref[:, 0:2 * HD] += jnp.dot(
                prob.astype(jnp.bfloat16), kv_ref[1, keys], preferred_element_type=jnp.float32
            )
            acc_ref[:, 2 * HD:] += jnp.dot(
                weighted.astype(jnp.bfloat16), kv_ref[1, keys, 0:HD],
                preferred_element_type=jnp.float32,
            )

        inverse = 1.0 / jnp.sum(sum_ref[0], axis=1, keepdims=True)
        drift = jnp.sum(sum_ref[1], axis=1, keepdims=True) * scale
        plain = acc_ref[:, 0:HD] * inverse
        turned = (acc_ref[:, HD:2 * HD] + acc_ref[:, 2 * HD:] * scale - drift * plain) * inverse
        for slot in range(3):
            piece = slice(slot * ROWS, (slot + 1) * ROWS)
            part_ref[part * 3 + slot, 0] = plain[piece].astype(jnp.bfloat16)
            part_ref[part * 3 + slot, 1] = turned[piece].astype(jnp.bfloat16)
        for slot in range(part * 3, part * 3 + 3):
            own, live, far, dst = back(slot)
            pl.when(live)(far.start)

            @pl.when(own)
            def _():
                pltpu.make_async_copy(part_ref.at[slot], dst, local_sems.at[3]).start()
        events(ORDERS[1 + part])

    def to_y(owner, h, step, index):
        piece = landing.at[owner, h]
        return pltpu.make_async_remote_copy(
            src_ref=piece, dst_ref=piece, send_sem=g_send.at[h, index],
            recv_sem=g_recv.at[owner, h], device_id={"head": lax.rem(y + step, 4)}, device_id_type=MESH,
        )

    def gathers(h):
        owner, step = (3, 1) if h < 3 else (1, 3)
        return (
            to_y(y, h, 1, 0), to_y(y, h, 3, 1), to_y(lax.rem(y + owner, 4), h, step, 2),
        )

    for h in range(HEADS):
        mine = is_me(*workers[h])

        @pl.when(mine)
        def _():
            pltpu.make_async_copy(part_ref.at[0], landing.at[y, h], local_sems.at[3]).wait()

        @pl.when(jnp.logical_not(mine))
        def _():
            pltpu.make_async_copy(part_ref.at[0], landing.at[y, h], back_recv.at[h]).wait()
        for copy in gathers(h)[0:2]:
            copy.start()

    events(ORDERS[3])
    weights.arrive()
    for zq in range(4):
        for parity in range(2):
            for half in range(2):
                for quarter in range(4):
                    for side in range(2):
                        row = quarter * 160 + side * 80
                        rest[parity, half, row:row + 80, zq * 64:(zq + 1) * 64] = packed[
                            zq, parity, half, quarter * 80:(quarter + 1) * 80, side * 64:(side + 1) * 64
                        ]

    def gathered(step, h):
        other = lax.rem(y + step, 4)
        pltpu.make_async_copy(part_ref.at[0], landing.at[other, h], g_recv.at[other, h]).wait()

    for turn, step in enumerate((0, 1, 3, 2)):
        other = lax.rem(y + step, 4)
        if turn == 1:
            for h in range(HEADS):
                gathered(1, h)
                if h < 3:
                    gathered(3, h)
                gathers(h)[2].start()
        for h in range(HEADS):
            if step == 2 or (step == 3 and h >= 3):
                gathered(step, h)
            for kind in range(2):
                rows_ref[kind * ROWS:(kind + 1) * ROWS, h * HD:(h + 1) * HD] = landing[other, h, kind]
        parity, half = lax.rem(other, 2), other // 2
        for zq in range(5):
            weight = main[zq, parity, half] if zq < 4 else rest[parity, half]
            term = jnp.dot(rows_ref[...], weight, preferred_element_type=jnp.float32)
            total_ref[zq] = term if turn == 0 else total_ref[zq] + term

    for zq in range(4):
        for kind in range(2):
            rows = slice(kind * ROWS, (kind + 1) * ROWS)
            both_ref[kind, :, zq * 320:zq * 320 + 256] = total_ref[zq, rows].astype(jnp.bfloat16)
            both_ref[kind, :, zq * 320 + 256:(zq + 1) * 320] = (
                total_ref[4, rows, zq * 64:(zq + 1) * 64].astype(jnp.bfloat16)
            )

    for direct in (True, False):
        for step in range(8):
            block = (x_lo if direct else 1 - x_lo) * 8 + lax.rem(z + step, 8)
            for live, copy in forwards(direct, block):
                pl.when(live)(copy.wait_send)
    for live, copy in sends:
        pl.when(live)(copy.wait_send)
    for slot in range(SLOTS):
        own, live, far, dst = back(slot)
        pl.when(live)(far.wait_send)
    for h in range(HEADS):
        for copy in gathers(h):
            copy.wait_send()
    weights.finish()


def local(qkv, tangent, segments, out_weight):
    vmem = pl.BlockSpec(memory_space=pltpu.VMEM)
    dma = pltpu.SemaphoreType.DMA
    below = jnp.sum(
        (segments[:, None] < jnp.arange(1, 129, dtype=jnp.int32)[None, :]).astype(jnp.int32), axis=0
    )
    count = jnp.broadcast_to(below[None, :], (8, 128))
    bf16, f32 = jnp.bfloat16, jnp.float32
    hbm = pl.BlockSpec(memory_space=pl.ANY)
    both = pl.pallas_call(
        layer,
        out_shape=jax.ShapeDtypeStruct((2, ROWS, 1280), bf16),
        in_specs=[hbm, hbm, vmem, hbm],
        out_specs=vmem,
        scratch_shapes=[
            pltpu.VMEM((3, ROWS, HEADS * HD), bf16),
            pltpu.VMEM((3, ROWS, HEADS * HD), bf16),
            pltpu.VMEM((640, 320), bf16),
            dma((3,)),
            pltpu.VMEM((HEADS, 3, ROWS, 2 * HD), bf16),
            pltpu.VMEM((2, SEQ, 2 * HD), bf16),
            pltpu.VMEM((SLOTS * ROWS, 2 * HD), bf16),
            pltpu.VMEM((BLOCKS, 8, 128), jnp.int32),
            pltpu.VMEM((KTILES, 2 * HD, TILE), bf16),
            pltpu.VMEM((KTILES, PART, TILE), f32),
            pltpu.VMEM((KTILES, PART, TILE), f32),
            pltpu.VMEM((PART, TILE), f32),
            pltpu.VMEM((2, PART, TILE), f32),
            pltpu.VMEM((PART, 3 * HD), f32),
            pltpu.VMEM((SLOTS, 2, ROWS, HD), bf16),
            pltpu.VMEM((320, 128), bf16),
            pltpu.VMEM((4, 2, 2, 640, 256), bf16),
            pltpu.VMEM((4, 2, 2, 320, 128), bf16),
            pltpu.VMEM((2, 2, 640, 256), bf16),
            pltpu.VMEM((4, HEADS, 2, ROWS, HD), bf16),
            pltpu.VMEM((2 * ROWS, HEADS * HD), bf16),
            pltpu.VMEM((5, 2 * ROWS, 256), f32),
            dma((6,)), dma((2, 4)), dma((BLOCKS,)), dma((HEADS,)), dma((SLOTS,)),
            dma((2, 4, 2)), dma((BLOCKS,)), dma((BLOCKS, 2)),
            dma((2, 2)), dma((2, 2)), dma((3, 2, 2)), dma((4, 2)),
            dma((3, 4, 2)), dma((4, 4, 2)), dma((4, 4, 2)), dma((4, 4, 2)),
            dma((SLOTS,)), dma((HEADS,)), dma((HEADS, 3)), dma((4, HEADS)),
        ],
        compiler_params=pltpu.CompilerParams(
            collective_id=0, has_side_effects=True, vmem_limit_bytes=56 * 2**20
        ),
        name="layer",
    )(qkv, tangent, count, out_weight)
    return both[0], both[1]


def solution(mesh):
    return jax.shard_map(
        local,
        mesh=mesh,
        in_specs=(
            P(None, ("dp", "ctx"), "head"),
            P(None, ("dp", "ctx"), "head"),
            P(("dp", "ctx")),
            P("head", "ctx"),
        ),
        out_specs=(P(("dp", "ctx"), "head"), P(("dp", "ctx"), "head")),
        check_vma=False,
    )
```

```python
import functools
import math

import jax
import jax.numpy as jnp
from jax import lax
from jax.experimental import pallas as pl
from jax.experimental.pallas import tpu as pltpu
from jax.sharding import PartitionSpec as P

HD = 128
HEADS = 5
BLOCKS = 16
ROWS = 160
SEQ = BLOCKS * ROWS
SLOTS = 6
SEGS = 4
TILE = 512
PART = 480


def several(kind, first, last):
    return [(kind, turn) for turn in range(first, last)]


ORDERS = (
    several("X", 0, 1) + several("K", 0, 2) + several("X", 1, 3) + several("K", 2, 4) + several("X", 3, 4)
    + several("D", 0, 3) + several("I", 0, 4) + several("D", 3, 8) + several("R", 0, 8),
    several("O", 0, 4),
    several("F", 0, 4),
    [],
)
KTILES = SEQ // TILE
MESH = pl.DeviceIdType.MESH


def role_of(x_lo, core):
    return x_lo * 2 + core


def chunk_of(block):
    return (block >= 6).astype(jnp.int32) + (block >= 11).astype(jnp.int32)


def chunk_start(chunk):
    return chunk * 5 + jnp.minimum(chunk, 1)


def work_of(x_lo, z, core):
    role = role_of(x_lo, core)
    first = jnp.where(role == 3, 4 * (z // 2), chunk_start(role))
    count = jnp.where(role == 3, 4, 5 + (role == 0).astype(jnp.int32))
    return first, count


def worker_of(head, block, core):
    if head == HEADS - 1:
        return 1, 2 * (block // 4) + core, 1
    role = chunk_of(block)
    return role // 2, 2 * head + core, lax.rem(role, 2)


def fold(op, values):
    parts = [values[:, i:i + 128] for i in range(0, values.shape[1], 128)]
    while len(parts) > 1:
        parts = [op(a, b) for a, b in zip(parts[0::2], parts[1::2])]
    return parts[0]


def signal_if(condition, semaphore, device):
    @pl.when(condition)
    def _():
        pl.semaphore_signal(semaphore, inc=1, device_id=device, device_id_type=MESH)


class Both:
    def __init__(self, copies):
        self.copies = copies

    def start(self):
        for copy in self.copies:
            copy.start()

    def wait_send(self):
        for copy in self.copies:
            copy.wait_send()


class Weights:
    def __init__(self, shard_ref, tail_ref, main_ref, packed_ref, local_sems, *sems):
        self.shard, self.tail, self.local_sems = shard_ref, tail_ref, local_sems
        self.main, self.packed = main_ref, packed_ref
        (self.y_send, self.y_recv, self.z_send, self.z_recv,
         self.x_send, self.x_recv, self.c_send, self.c_recv) = sems
        self.ctx, self.y, dp = lax.axis_index("ctx"), lax.axis_index("head"), lax.axis_index("dp")
        self.x_lo, self.z = self.ctx // 8, lax.rem(self.ctx, 8)
        self.x_hi, self.core = dp // 2, lax.rem(dp, 2)
        self.x = self.x_hi * 2 + self.x_lo
        self.inner = self.x_hi * 2 + 1 - self.x_lo
        self.outer = lax.rem(self.x + 3 + 2 * self.x_lo, 4)
        self.far = lax.rem(self.x + 2, 4)
        self.active = lax.rem(self.z, 2) == self.core
        self.parity = lax.rem(self.z // 4 + self.y, 2)

    def prepare(self):
        for quarter in range(4):
            for side in range(2):
                row = quarter * 160 + side * 80
                self.tail[quarter * 80:(quarter + 1) * 80, side * 64:(side + 1) * 64] = (
                    self.shard[row:row + 80, 256:320]
                )

    def device(self, x=None, z=None, y=None, core=None):
        x = self.x if x is None else x
        z = self.z if z is None else z
        y = self.y if y is None else y
        core = self.core if core is None else core
        return {"ctx": lax.rem(x, 2) * 8 + z, "head": y, "dp": (x // 2) * 2 + core}

    def first_target(self, same):
        y = self.x_lo * 2 + self.z // 4
        x = self.x if same else self.x_hi * 2 + 1 - self.x_lo
        z = lax.rem(self.z + 4 * lax.rem(self.y, 2), 8)
        is_me = (x == self.x) & (y == self.y) & (z == self.z)
        return x, z, y, is_me

    def first_source(self, half):
        y = 2 * half + self.parity
        x = self.x_hi * 2 + self.y // 2
        z = lax.rem(self.z + 4 * self.parity, 8)
        is_me = (x == self.x) & (y == self.y) & (z == self.z)
        return x, z, y, is_me

    def greet(self, barrier):
        for half in range(2):
            x, z, y, is_me = self.first_source(half)
            signal_if(self.active & jnp.logical_not(is_me), barrier, self.device(x, z, y))
        for x in (self.inner, self.outer):
            signal_if(True, barrier, self.device(x=x))
        signal_if(True, barrier, self.device(core=1 - self.core))
        for step in (1, 7):
            signal_if(True, barrier, self.device(z=lax.rem(self.z + step, 8)))

    def greetings(self):
        count = jnp.int32(5)
        for same in (True, False):
            is_me = self.first_target(same)[3]
            count = count + (self.active & jnp.logical_not(is_me)).astype(jnp.int32)
        return count

    def rows(self, quarter):
        return (
            pl.ds(pl.multiple_of(quarter * 160, 160), 160),
            pl.ds(pl.multiple_of(quarter * 80, 80), 80),
        )

    def piece(self, zq, parity, x):
        wide, narrow = self.rows(x)
        return self.main.at[zq, parity, :, wide], self.packed.at[zq, parity, :, narrow]

    def landed(self, refs, sems):
        for i, ref in enumerate(refs):
            pltpu.make_async_copy(ref, ref, sems.at[i]).wait()

    def remote(self, srcs, dsts, send, recv, device):
        return Both([
            pltpu.make_async_remote_copy(
                src_ref=src, dst_ref=dst, send_sem=send.at[i], recv_sem=recv.at[i],
                device_id=device, device_id_type=MESH,
            ) for i, (src, dst) in enumerate(zip(srcs, dsts))
        ])

    def first(self, index):
        x, z, y, is_me = self.first_target(index == 0)
        wide, narrow = self.rows(x)
        zq, parity, half = lax.rem(self.z, 4), lax.rem(self.y, 2), self.y // 2
        srcs = self.shard.at[wide, 0:256], self.tail.at[narrow]
        dsts = self.main.at[zq, parity, half, wide], self.packed.at[zq, parity, half, narrow]
        far = self.remote(
            srcs, dsts, self.y_send.at[index], self.y_recv.at[half], self.device(x, z, y)
        )
        return is_me, far, srcs, dsts

    def over_y(self):
        for index in range(2):
            is_me, far, srcs, dsts = self.first(index)
            pl.when(self.active & jnp.logical_not(is_me))(far.start)

            @pl.when(self.active & is_me)
            def _():
                for i in range(2):
                    pltpu.make_async_copy(srcs[i], dsts[i], self.local_sems.at[i]).start()

    def second(self, turn, back):
        z, zq, parity = self.from_z(self.order(turn))
        mine = self.piece(zq, parity, self.x)
        return self.remote(
            mine, mine, self.z_send.at[turn, int(back)], self.z_recv.at[z // 2],
            self.device(z=lax.rem(self.z + (7 if back else 1), 8)),
        )

    def seconds(self):
        passive = jnp.logical_not(self.active)
        return (
            (0, True, self.second(0, False)), (0, self.active, self.second(0, True)),
            (1, self.active, self.second(1, False)), (1, passive, self.second(1, True)),
            (2, passive, self.second(2, False)), (2, self.active, self.second(2, True)),
        )

    def over_z(self):
        @pl.when(self.active)
        def _():
            for index in range(2):
                is_me, far, srcs, dsts = self.first(index)
                pl.when(jnp.logical_not(is_me))(far.wait_send)
            for half in range(2):
                is_me = self.first_source(half)[3]
                wide, narrow = self.rows(self.x)
                zq = lax.rem(self.z, 4)
                dst = (
                    self.main.at[zq, self.parity, half, wide],
                    self.packed.at[zq, self.parity, half, narrow],
                )

                @pl.when(is_me)
                def _():
                    self.landed(dst, self.local_sems)

                @pl.when(jnp.logical_not(is_me))
                def _():
                    self.landed(dst, self.y_recv.at[half])

    def from_z(self, index):
        z = 2 * index + self.core
        return z, lax.rem(z, 4), lax.rem(z // 4 + self.y, 2)

    def order(self, turn):
        step = jnp.where(self.active, (0, 6, 2, 4)[turn], (7, 1, 5, 3)[turn])
        return lax.rem(self.z + step, 8) // 2

    def third(self, index, hop):
        z, zq, parity = self.from_z(index)
        owner = self.inner if hop == 2 else self.x
        mine = self.piece(zq, parity, owner)
        return self.remote(
            mine, mine, self.x_send.at[hop, index], self.x_recv.at[owner, index],
            self.device(x=self.outer if hop else self.inner),
        )

    def fourth(self, index, x):
        z, zq, parity = self.from_z(index)
        mine = self.piece(zq, parity, x)
        return self.remote(
            mine, mine, self.c_send.at[x, index], self.c_recv.at[x, index],
            self.device(core=1 - self.core),
        )

    def start_x(self, turn):
        index = self.order(turn)
        z, zq, parity = self.from_z(index)

        @pl.when(z != self.z)
        def _():
            self.landed(self.piece(zq, parity, self.x), self.z_recv.at[index])
        for other, live, copy in self.seconds():
            if other == turn:
                pl.when(live)(copy.start)
        self.third(index, 0).start()
        self.third(index, 1).start()
        self.fourth(index, self.x).start()

    def pass_on(self, x, turn):
        index = self.order(turn)
        z, zq, parity = self.from_z(index)
        self.landed(self.piece(zq, parity, x), self.x_recv.at[x, index])
        if x is self.inner:
            self.third(index, 2).start()
        self.fourth(index, x).start()

    def arrive(self):
        for x in range(4):
            for index in range(4):
                z = 2 * index + 1 - self.core
                other = self.piece(lax.rem(z, 4), lax.rem(z // 4 + self.y, 2), x)
                self.landed(other, self.c_recv.at[x, index])

    def finish(self):
        for turn, live, copy in self.seconds():
            pl.when(live)(copy.wait_send)
        for index in range(4):
            for hop in range(3):
                self.third(index, hop).wait_send()
        for x in range(4):
            for index in range(4):
                self.fourth(index, x).wait_send()


def layer(
    qkv_hbm, tan_hbm, seg_ref, turned_hbm, both_ref,
    qkv_ref, tan_ref, turned_ref, shard_ref, count_ref, in_sems, stage, kv_ref, q_ref, counts_ref, kt_ref, s_ref, st_ref, top_ref, sum_ref, acc_ref, part_ref,
    tail, main, packed, rest, landing, rows_ref, total_ref,
    local_sems, kv_send, kv_recv, q_send, q_recv, n_send, n_recv, f_send,
    y_send, y_recv, z_send, z_recv, x_send, x_recv, c_send, c_recv,
    back_send, back_recv, g_send, g_recv,
):
    ctx, dp, y = lax.axis_index("ctx"), lax.axis_index("dp"), lax.axis_index("head")
    x_lo, z, x_hi, core = ctx // 8, lax.rem(ctx, 8), dp // 2, lax.rem(dp, 2)
    sample = lax.rem(z, 2)
    role = role_of(x_lo, core)
    first, count = work_of(x_lo, z, core)
    weights = Weights(
        shard_ref, tail, main, packed, local_sems.at[pl.ds(4, 2)],
        y_send, y_recv, z_send, z_recv, x_send, x_recv, c_send, c_recv,
    )

    def at(other_x, other_z, other_core):
        return {"ctx": other_x * 8 + other_z, "dp": x_hi * 2 + other_core}

    def is_me(other_x, other_z, other_core):
        return (other_x == x_lo) & (other_z == z) & (other_core == core)

    def remote(src, dst, send, recv, device):
        return pltpu.make_async_remote_copy(
            src_ref=src, dst_ref=dst, send_sem=send, recv_sem=recv, device_id=at(*device),
            device_id_type=MESH,
        )

    def rows_of(block):
        return pl.ds(pl.multiple_of(block * ROWS, ROWS), ROWS)

    loads = [
        pltpu.make_async_copy(src, dst, in_sems.at[i]) for i, (src, dst) in enumerate(
            ((qkv_hbm, qkv_ref), (tan_hbm, tan_ref), (turned_hbm, turned_ref))
        )
    ]
    for load in loads:
        load.start()
    barrier = pltpu.get_barrier_semaphore()
    for other_x in range(2):
        for step in range(8):
            source = (other_x, lax.rem(z + step, 8), sample)
            signal_if(jnp.logical_not(is_me(*source)), barrier, at(*source))
    for mate in ((1 - x_lo, z, core), (x_lo, z, 1 - core), (1 - x_lo, z, 1 - core)):
        signal_if(True, barrier, at(*mate))
    weights.greet(barrier)
    workers = [worker_of(h, ctx, core) for h in range(HEADS)]
    for worker in workers:
        signal_if(jnp.logical_not(is_me(*worker)), barrier, at(*worker))
    for step in range(1, 4):
        signal_if(True, barrier, {"head": lax.rem(y + step, 4)})
    own_block = (core == sample) & (first <= ctx) & (ctx < first + count)
    lane = lax.broadcasted_iota(jnp.int32, (8, 128), 1)
    tally = jnp.zeros((8, 128), jnp.int32)
    for v in range(SEGS - 1):
        below = jnp.sum((seg_ref[...] <= v).astype(jnp.int32), axis=1, keepdims=True)
        tally = jnp.where(lane == v, below, tally)
    count_ref[...] = tally
    for load in loads:
        load.wait()
    shard_ref[...] = turned_ref[...].T
    weights.prepare()
    for slot in (4, 5):
        @pl.when(slot >= count)
        def _():
            q_ref[slot * ROWS:(slot + 1) * ROWS] = jnp.zeros((ROWS, 2 * HD), jnp.bfloat16)
    for head in range(HEADS):
        cols = slice(head * HD, (head + 1) * HD)
        stage[head, 0, :, 0:HD] = qkv_ref[1, :, cols]
        stage[head, 0, :, HD:] = tan_ref[1, :, cols]
        stage[head, 1, :, 0:HD] = qkv_ref[2, :, cols]
        stage[head, 1, :, HD:] = tan_ref[2, :, cols]
        stage[head, 2, :, 0:HD] = tan_ref[0, :, cols]
        stage[head, 2, :, HD:] = qkv_ref[0, :, cols]
    pl.semaphore_wait(
        barrier,
        22 - (core == sample).astype(jnp.int32) + weights.greetings()
        + count - own_block.astype(jnp.int32),
    )
    weights.over_y()

    sends = []

    def send(device, src, dst, send_sem, recv_sem, local_sem):
        mine = is_me(*device)
        far = remote(src, dst, send_sem, recv_sem, device)
        pl.when(jnp.logical_not(mine))(far.start)

        @pl.when(mine)
        def _():
            pltpu.make_async_copy(src, dst, local_sem).start()
        sends.append((jnp.logical_not(mine), far))

    for other_x in range(2):
        for step in range(4):
            device = (other_x, 2 * lax.rem(z // 2 + step, 4) + core)
            for other_core in range(2):
                send(
                    device + (other_core,), count_ref, counts_ref.at[ctx],
                    n_send.at[other_x, step, other_core], n_recv.at[ctx], local_sems.at[0],
                )
    for head in range(HEADS):
        slot = lax.rem(ctx, 4) if head == 4 else ctx - chunk_start(chunk_of(ctx))
        send(
            worker_of(head, ctx, core), stage.at[head, 2], q_ref.at[rows_of(slot)],
            q_send.at[head], q_recv.at[slot], local_sems.at[2],
        )
    weights.over_z()
    def send_keys(step):
        turn = lax.rem(z // 2 + (0, 1, 3, 2)[step], 4)
        slice_z = 2 * turn + core
        send(
            (x_lo, slice_z, jnp.where(x_lo == 0, core, 0)), stage.at[turn, 0:2],
            kv_ref.at[:, rows_of(ctx)], kv_send.at[0, step], kv_recv.at[ctx], local_sems.at[1],
        )
        send(
            (1, slice_z, 1), stage.at[HEADS - 1, 0:2],
            kv_ref.at[:, rows_of(ctx)], kv_send.at[1, step], kv_recv.at[ctx], local_sems.at[1],
        )

    entry = (x_lo == 0) & (core == sample)
    third = role == 2

    def forward(block, mate, index):
        dst = kv_ref.at[:, rows_of(block)]
        return remote(dst, dst, f_send.at[block, index], kv_recv.at[block], mate)

    def forwards(direct, block):
        to_core = (entry, forward(block, (0, z, 1 - core), 0))
        if direct:
            to_x = forward(block, (1 - x_lo, z, jnp.where(entry, 0, sample)), 1)
            return [to_core, (entry | third, to_x)]
        return [to_core]

    def arrived(block, ref, own_sem, sem):
        mine = (block == ctx) & (core == sample)

        @pl.when(mine)
        def _():
            pltpu.make_async_copy(ref, ref, own_sem).wait()

        @pl.when(jnp.logical_not(mine))
        def _():
            pltpu.make_async_copy(ref, ref, sem).wait()

    def pass_keys(direct, step):
        block = (x_lo if direct else 1 - x_lo) * 8 + lax.rem(z + step, 8)
        arrived(block, kv_ref.at[:, rows_of(block)], local_sems.at[1], kv_recv.at[block])
        for live, copy in forwards(direct, block):
            pl.when(live)(copy.start)

    near = (0, 1, 7, 2, 6, 3, 5, 4)

    def events(order):
        for kind, turn in order:
            if kind in "DR":
                pass_keys(kind == "D", near[turn])
            elif kind == "X":
                weights.start_x(turn)
            elif kind == "K":
                send_keys(turn)
            else:
                x = {"I": weights.inner, "O": weights.outer, "F": weights.far}[kind]
                weights.pass_on(x, turn)

    events(ORDERS[0])
    for direct in (True, False):
        for step in range(8):
            block = (x_lo if direct else 1 - x_lo) * 8 + lax.rem(z + step, 8)
            arrived(block, counts_ref.at[block], local_sems.at[0], n_recv.at[block])
    for slot in range(SLOTS):
        @pl.when(slot < count)
        def _():
            arrived(first + slot, q_ref.at[rows_of(slot)], local_sems.at[2], q_recv.at[slot])

    def back(slot):
        block = lax.min(first + slot, BLOCKS - 1)
        head = jnp.where(role == 3, HEADS - 1, z // 2)
        own = (block == ctx) & (core == sample)
        dst = landing.at[y, head]
        far = pltpu.make_async_remote_copy(
            src_ref=part_ref.at[slot], dst_ref=dst, send_sem=back_send.at[slot],
            recv_sem=back_recv.at[head], device_id={"ctx": block, "dp": x_hi * 2 + sample},
            device_id_type=MESH,
        )
        return (slot < count) & own, (slot < count) & jnp.logical_not(own), far, dst

    scale = 1.0 / math.sqrt(HD)
    power = scale / math.log(2.0)
    below = jnp.sum(counts_ref[...], axis=0)
    bounds = [below[0:1, v:v + 1] for v in range(SEGS - 1)]

    def of_position(position, values):
        result = values[SEGS - 1]
        for v in range(SEGS - 2, -1, -1):
            result = jnp.where(position < bounds[v], values[v], result)
        return result

    starts = [jnp.zeros((1, 1), jnp.int32)] + bounds
    ends = bounds + [jnp.full((1, 1), SEQ, jnp.int32)]

    @pl.loop(0, KTILES)
    def _(tile):
        keys = pl.ds(pl.multiple_of(tile * TILE, TILE), TILE)
        kt_ref[tile] = kv_ref[0, keys].T

    for part in range(2):
        position = (first + 3 * part) * ROWS + lax.broadcasted_iota(jnp.int32, (PART, 1), 0)
        start = of_position(position, starts)
        end = of_position(position, ends)
        column = lax.broadcasted_iota(jnp.int32, (1, TILE), 1)
        rows = slice(part * PART, (part + 1) * PART)
        top_ref[...] = jnp.full_like(top_ref, -1e30)
        sum_ref[...] = jnp.zeros_like(sum_ref)
        acc_ref[...] = jnp.zeros_like(acc_ref)

        @pl.loop(0, KTILES)
        def _(tile):
            s = jnp.dot(
                q_ref[rows, HD:], kt_ref[tile, 0:HD], preferred_element_type=jnp.float32
            )
            place = column + tile * TILE
            s = jnp.where((place >= start) & (place < end), s, -1e30)
            s_ref[tile] = s
            st_ref[tile] = jnp.dot(
                q_ref[rows, :], kt_ref[tile], preferred_element_type=jnp.float32
            )
            top_ref[...] = jnp.maximum(top_ref[...], fold(jnp.maximum, s))

        top = jnp.max(top_ref[...], axis=1, keepdims=True)

        @pl.loop(0, KTILES)
        def _(tile):
            keys = pl.ds(pl.multiple_of(tile * TILE, TILE), TILE)
            prob = jnp.exp2((s_ref[tile] - top) * power)
            weighted = prob * st_ref[tile]
            sum_ref[0] += fold(jnp.add, prob)
            sum_ref[1] += fold(jnp.add, weighted)
            acc_ref[:, 0:2 * HD] += jnp.dot(
                prob.astype(jnp.bfloat16), kv_ref[1, keys], preferred_element_type=jnp.float32
            )
            acc_ref[:, 2 * HD:] += jnp.dot(
                weighted.astype(jnp.bfloat16), kv_ref[1, keys, 0:HD],
                preferred_element_type=jnp.float32,
            )

        inverse = 1.0 / jnp.sum(sum_ref[0], axis=1, keepdims=True)
        drift = jnp.sum(sum_ref[1], axis=1, keepdims=True) * scale
        plain = acc_ref[:, 0:HD] * inverse
        turned = (acc_ref[:, HD:2 * HD] + acc_ref[:, 2 * HD:] * scale - drift * plain) * inverse
        for slot in range(3):
            piece = slice(slot * ROWS, (slot + 1) * ROWS)
            part_ref[part * 3 + slot, 0] = plain[piece].astype(jnp.bfloat16)
            part_ref[part * 3 + slot, 1] = turned[piece].astype(jnp.bfloat16)
        for slot in range(part * 3, part * 3 + 3):
            own, live, far, dst = back(slot)
            pl.when(live)(far.start)

            @pl.when(own)
            def _():
                pltpu.make_async_copy(part_ref.at[slot], dst, local_sems.at[3]).start()
        events(ORDERS[1 + part])

    def to_y(owner, h, step, index):
        piece = landing.at[owner, h]
        return pltpu.make_async_remote_copy(
            src_ref=piece, dst_ref=piece, send_sem=g_send.at[h, index],
            recv_sem=g_recv.at[owner, h], device_id={"head": lax.rem(y + step, 4)}, device_id_type=MESH,
        )

    def gathers(h):
        owner, step = (3, 1) if h < 3 else (1, 3)
        return (
            to_y(y, h, 1, 0), to_y(y, h, 3, 1), to_y(lax.rem(y + owner, 4), h, step, 2),
        )

    for h in range(HEADS):
        mine = is_me(*workers[h])

        @pl.when(mine)
        def _():
            pltpu.make_async_copy(part_ref.at[0], landing.at[y, h], local_sems.at[3]).wait()

        @pl.when(jnp.logical_not(mine))
        def _():
            pltpu.make_async_copy(part_ref.at[0], landing.at[y, h], back_recv.at[h]).wait()
        for copy in gathers(h)[0:2]:
            copy.start()

    events(ORDERS[3])
    weights.arrive()
    for zq in range(4):
        for parity in range(2):
            for half in range(2):
                for quarter in range(4):
                    for side in range(2):
                        row = quarter * 160 + side * 80
                        rest[parity, half, row:row + 80, zq * 64:(zq + 1) * 64] = packed[
                            zq, parity, half, quarter * 80:(quarter + 1) * 80, side * 64:(side + 1) * 64
                        ]

    def gathered(step, h):
        other = lax.rem(y + step, 4)
        pltpu.make_async_copy(part_ref.at[0], landing.at[other, h], g_recv.at[other, h]).wait()

    for turn, step in enumerate((0, 1, 3, 2)):
        other = lax.rem(y + step, 4)
        if turn == 1:
            for h in range(HEADS):
                gathered(1, h)
                if h < 3:
                    gathered(3, h)
                gathers(h)[2].start()
        for h in range(HEADS):
            if step == 2 or (step == 3 and h >= 3):
                gathered(step, h)
            for kind in range(2):
                rows_ref[kind * ROWS:(kind + 1) * ROWS, h * HD:(h + 1) * HD] = landing[other, h, kind]
        parity, half = lax.rem(other, 2), other // 2
        for zq in range(5):
            weight = main[zq, parity, half] if zq < 4 else rest[parity, half]
            term = jnp.dot(rows_ref[...], weight, preferred_element_type=jnp.float32)
            total_ref[zq] = term if turn == 0 else total_ref[zq] + term

    for zq in range(4):
        for kind in range(2):
            rows = slice(kind * ROWS, (kind + 1) * ROWS)
            both_ref[kind, :, zq * 320:zq * 320 + 256] = total_ref[zq, rows].astype(jnp.bfloat16)
            both_ref[kind, :, zq * 320 + 256:(zq + 1) * 320] = (
                total_ref[4, rows, zq * 64:(zq + 1) * 64].astype(jnp.bfloat16)
            )

    for direct in (True, False):
        for step in range(8):
            block = (x_lo if direct else 1 - x_lo) * 8 + lax.rem(z + step, 8)
            for live, copy in forwards(direct, block):
                pl.when(live)(copy.wait_send)
    for live, copy in sends:
        pl.when(live)(copy.wait_send)
    for slot in range(SLOTS):
        own, live, far, dst = back(slot)
        pl.when(live)(far.wait_send)
    for h in range(HEADS):
        for copy in gathers(h):
            copy.wait_send()
    weights.finish()


def local(qkv, tangent, segments, out_weight):
    vmem = pl.BlockSpec(memory_space=pltpu.VMEM)
    dma = pltpu.SemaphoreType.DMA
    bf16, f32 = jnp.bfloat16, jnp.float32
    hbm = pl.BlockSpec(memory_space=pl.ANY)
    both = pl.pallas_call(
        layer,
        out_shape=jax.ShapeDtypeStruct((2, ROWS, 1280), bf16),
        in_specs=[hbm, hbm, vmem, hbm],
        out_specs=vmem,
        scratch_shapes=[
            pltpu.VMEM((3, ROWS, HEADS * HD), bf16),
            pltpu.VMEM((3, ROWS, HEADS * HD), bf16),
            pltpu.VMEM((320, 640), bf16),
            pltpu.VMEM((640, 320), bf16),
            pltpu.VMEM((8, 128), jnp.int32),
            dma((3,)),
            pltpu.VMEM((HEADS, 3, ROWS, 2 * HD), bf16),
            pltpu.VMEM((2, SEQ, 2 * HD), bf16),
            pltpu.VMEM((SLOTS * ROWS, 2 * HD), bf16),
            pltpu.VMEM((BLOCKS, 8, 128), jnp.int32),
            pltpu.VMEM((KTILES, 2 * HD, TILE), bf16),
            pltpu.VMEM((KTILES, PART, TILE), f32),
            pltpu.VMEM((KTILES, PART, TILE), f32),
            pltpu.VMEM((PART, 128), f32),
            pltpu.VMEM((2, PART, 128), f32),
            pltpu.VMEM((PART, 3 * HD), f32),
            pltpu.VMEM((SLOTS, 2, ROWS, HD), bf16),
            pltpu.VMEM((320, 128), bf16),
            pltpu.VMEM((4, 2, 2, 640, 256), bf16),
            pltpu.VMEM((4, 2, 2, 320, 128), bf16),
            pltpu.VMEM((2, 2, 640, 256), bf16),
            pltpu.VMEM((4, HEADS, 2, ROWS, HD), bf16),
            pltpu.VMEM((2 * ROWS, HEADS * HD), bf16),
            pltpu.VMEM((5, 2 * ROWS, 256), f32),
            dma((6,)), dma((2, 4)), dma((BLOCKS,)), dma((HEADS,)), dma((SLOTS,)),
            dma((2, 4, 2)), dma((BLOCKS,)), dma((BLOCKS, 2)),
            dma((2, 2)), dma((2, 2)), dma((3, 2, 2)), dma((4, 2)),
            dma((3, 4, 2)), dma((4, 4, 2)), dma((4, 4, 2)), dma((4, 4, 2)),
            dma((SLOTS,)), dma((HEADS,)), dma((HEADS, 3)), dma((4, HEADS)),
        ],
        compiler_params=pltpu.CompilerParams(
            collective_id=0, has_side_effects=True, vmem_limit_bytes=56 * 2**20
        ),
        name="layer",
    )(qkv, tangent, segments.reshape(1, ROWS), out_weight.T)
    return both[0], both[1]


def solution(mesh):
    return jax.shard_map(
        local,
        mesh=mesh,
        in_specs=(
            P(None, ("dp", "ctx"), "head"),
            P(None, ("dp", "ctx"), "head"),
            P(("dp", "ctx")),
            P("head", "ctx"),
        ),
        out_specs=(P(("dp", "ctx"), "head"), P(("dp", "ctx"), "head")),
        check_vma=False,
    )
```

```python
import functools
import math

import jax
import jax.numpy as jnp
from jax import lax
from jax.experimental import pallas as pl
from jax.experimental.pallas import tpu as pltpu
from jax.sharding import PartitionSpec as P

HD = 128
HEADS = 5
BLOCKS = 16
ROWS = 160
SEQ = BLOCKS * ROWS
SLOTS = 6
SEGS = 4
TILE = 512
PART = 480


def several(kind, first, last):
    return [(kind, turn) for turn in range(first, last)]


ORDERS = (
    several("X", 0, 1) + several("K", 0, 2) + several("X", 1, 3) + several("K", 2, 4) + several("X", 3, 4)
    + several("D", 0, 3) + several("I", 0, 4) + several("D", 3, 8) + several("R", 0, 8),
    several("O", 0, 4),
    several("F", 0, 4),
    [],
)
KTILES = SEQ // TILE
MESH = pl.DeviceIdType.MESH


def role_of(x_lo, core):
    return x_lo * 2 + core


def chunk_of(block):
    return (block >= 6).astype(jnp.int32) + (block >= 11).astype(jnp.int32)


def chunk_start(chunk):
    return chunk * 5 + jnp.minimum(chunk, 1)


def work_of(x_lo, z, core):
    role = role_of(x_lo, core)
    first = jnp.where(role == 3, 4 * (z // 2), chunk_start(role))
    count = jnp.where(role == 3, 4, 5 + (role == 0).astype(jnp.int32))
    return first, count


def worker_of(head, block, core):
    if head == HEADS - 1:
        return 1, 2 * (block // 4) + core, 1
    role = chunk_of(block)
    return role // 2, 2 * head + core, lax.rem(role, 2)


def fold(op, values):
    parts = [values[:, i:i + 128] for i in range(0, values.shape[1], 128)]
    while len(parts) > 1:
        parts = [op(a, b) for a, b in zip(parts[0::2], parts[1::2])]
    return parts[0]


def signal_if(condition, semaphore, device):
    @pl.when(condition)
    def _():
        pl.semaphore_signal(semaphore, inc=1, device_id=device, device_id_type=MESH)


class Both:
    def __init__(self, copies):
        self.copies = copies

    def start(self):
        for copy in self.copies:
            copy.start()

    def wait_send(self):
        for copy in self.copies:
            copy.wait_send()


class Weights:
    def __init__(self, shard_ref, tail_ref, main_ref, packed_ref, local_sems, *sems):
        self.shard, self.tail, self.local_sems = shard_ref, tail_ref, local_sems
        self.main, self.packed = main_ref, packed_ref
        (self.y_send, self.y_recv, self.z_send, self.z_recv,
         self.x_send, self.x_recv, self.c_send, self.c_recv) = sems
        self.ctx, self.y, dp = lax.axis_index("ctx"), lax.axis_index("head"), lax.axis_index("dp")
        self.x_lo, self.z = self.ctx // 8, lax.rem(self.ctx, 8)
        self.x_hi, self.core = dp // 2, lax.rem(dp, 2)
        self.x = self.x_hi * 2 + self.x_lo
        self.inner = self.x_hi * 2 + 1 - self.x_lo
        self.outer = lax.rem(self.x + 3 + 2 * self.x_lo, 4)
        self.far = lax.rem(self.x + 2, 4)
        self.active = lax.rem(self.z, 2) == self.core
        self.parity = lax.rem(self.z // 4 + self.y, 2)

    def prepare(self):
        for quarter in range(4):
            for side in range(2):
                row = quarter * 160 + side * 80
                self.tail[quarter * 80:(quarter + 1) * 80, side * 64:(side + 1) * 64] = (
                    self.shard[row:row + 80, 256:320]
                )

    def device(self, x=None, z=None, y=None, core=None):
        x = self.x if x is None else x
        z = self.z if z is None else z
        y = self.y if y is None else y
        core = self.core if core is None else core
        return {"ctx": lax.rem(x, 2) * 8 + z, "head": y, "dp": (x // 2) * 2 + core}

    def first_target(self, same):
        y = self.x_lo * 2 + self.z // 4
        x = self.x if same else self.x_hi * 2 + 1 - self.x_lo
        z = lax.rem(self.z + 4 * lax.rem(self.y, 2), 8)
        is_me = (x == self.x) & (y == self.y) & (z == self.z)
        return x, z, y, is_me

    def first_source(self, half):
        y = 2 * half + self.parity
        x = self.x_hi * 2 + self.y // 2
        z = lax.rem(self.z + 4 * self.parity, 8)
        is_me = (x == self.x) & (y == self.y) & (z == self.z)
        return x, z, y, is_me

    def greet(self, barrier):
        for half in range(2):
            x, z, y, is_me = self.first_source(half)
            signal_if(self.active & jnp.logical_not(is_me), barrier, self.device(x, z, y))
        for x in (self.inner, self.outer):
            signal_if(True, barrier, self.device(x=x))
        signal_if(True, barrier, self.device(core=1 - self.core))
        for step in (1, 7):
            signal_if(True, barrier, self.device(z=lax.rem(self.z + step, 8)))

    def greetings(self):
        count = jnp.int32(5)
        for same in (True, False):
            is_me = self.first_target(same)[3]
            count = count + (self.active & jnp.logical_not(is_me)).astype(jnp.int32)
        return count

    def rows(self, quarter):
        return (
            pl.ds(pl.multiple_of(quarter * 160, 160), 160),
            pl.ds(pl.multiple_of(quarter * 80, 80), 80),
        )

    def piece(self, zq, parity, x):
        wide, narrow = self.rows(x)
        return self.main.at[zq, parity, :, wide], self.packed.at[zq, parity, :, narrow]

    def landed(self, refs, sems):
        for i, ref in enumerate(refs):
            pltpu.make_async_copy(ref, ref, sems.at[i]).wait()

    def remote(self, srcs, dsts, send, recv, device):
        return Both([
            pltpu.make_async_remote_copy(
                src_ref=src, dst_ref=dst, send_sem=send.at[i], recv_sem=recv.at[i],
                device_id=device, device_id_type=MESH,
            ) for i, (src, dst) in enumerate(zip(srcs, dsts))
        ])

    def first(self, index):
        x, z, y, is_me = self.first_target(index == 0)
        wide, narrow = self.rows(x)
        zq, parity, half = lax.rem(self.z, 4), lax.rem(self.y, 2), self.y // 2
        srcs = self.shard.at[wide, 0:256], self.tail.at[narrow]
        dsts = self.main.at[zq, parity, half, wide], self.packed.at[zq, parity, half, narrow]
        far = self.remote(
            srcs, dsts, self.y_send.at[index], self.y_recv.at[half], self.device(x, z, y)
        )
        return is_me, far, srcs, dsts

    def over_y(self):
        for index in range(2):
            is_me, far, srcs, dsts = self.first(index)
            pl.when(self.active & jnp.logical_not(is_me))(far.start)

            @pl.when(self.active & is_me)
            def _():
                for i in range(2):
                    pltpu.make_async_copy(srcs[i], dsts[i], self.local_sems.at[i]).start()

    def second(self, turn, back):
        z, zq, parity = self.from_z(self.order(turn))
        mine = self.piece(zq, parity, self.x)
        return self.remote(
            mine, mine, self.z_send.at[turn, int(back)], self.z_recv.at[z // 2],
            self.device(z=lax.rem(self.z + (7 if back else 1), 8)),
        )

    def seconds(self):
        passive = jnp.logical_not(self.active)
        return (
            (0, True, self.second(0, False)), (0, self.active, self.second(0, True)),
            (1, self.active, self.second(1, False)), (1, passive, self.second(1, True)),
            (2, passive, self.second(2, False)), (2, self.active, self.second(2, True)),
        )

    def over_z(self):
        @pl.when(self.active)
        def _():
            for index in range(2):
                is_me, far, srcs, dsts = self.first(index)
                pl.when(jnp.logical_not(is_me))(far.wait_send)
            for half in range(2):
                is_me = self.first_source(half)[3]
                wide, narrow = self.rows(self.x)
                zq = lax.rem(self.z, 4)
                dst = (
                    self.main.at[zq, self.parity, half, wide],
                    self.packed.at[zq, self.parity, half, narrow],
                )

                @pl.when(is_me)
                def _():
                    self.landed(dst, self.local_sems)

                @pl.when(jnp.logical_not(is_me))
                def _():
                    self.landed(dst, self.y_recv.at[half])

    def from_z(self, index):
        z = 2 * index + self.core
        return z, lax.rem(z, 4), lax.rem(z // 4 + self.y, 2)

    def order(self, turn):
        step = jnp.where(self.active, (0, 6, 2, 4)[turn], (7, 1, 5, 3)[turn])
        return lax.rem(self.z + step, 8) // 2

    def third(self, index, hop):
        z, zq, parity = self.from_z(index)
        owner = self.inner if hop == 2 else self.x
        mine = self.piece(zq, parity, owner)
        return self.remote(
            mine, mine, self.x_send.at[hop, index], self.x_recv.at[owner, index],
            self.device(x=self.outer if hop else self.inner),
        )

    def fourth(self, index, x):
        z, zq, parity = self.from_z(index)
        mine = self.piece(zq, parity, x)
        return self.remote(
            mine, mine, self.c_send.at[x, index], self.c_recv.at[x, index],
            self.device(core=1 - self.core),
        )

    def start_x(self, turn):
        index = self.order(turn)
        z, zq, parity = self.from_z(index)

        @pl.when(z != self.z)
        def _():
            self.landed(self.piece(zq, parity, self.x), self.z_recv.at[index])
        for other, live, copy in self.seconds():
            if other == turn:
                pl.when(live)(copy.start)
        self.third(index, 0).start()
        self.third(index, 1).start()
        self.fourth(index, self.x).start()

    def pass_on(self, x, turn):
        index = self.order(turn)
        z, zq, parity = self.from_z(index)
        self.landed(self.piece(zq, parity, x), self.x_recv.at[x, index])
        if x is self.inner:
            self.third(index, 2).start()
        self.fourth(index, x).start()

    def arrive(self):
        for x in range(4):
            for index in range(4):
                z = 2 * index + 1 - self.core
                other = self.piece(lax.rem(z, 4), lax.rem(z // 4 + self.y, 2), x)
                self.landed(other, self.c_recv.at[x, index])

    def finish(self):
        for turn, live, copy in self.seconds():
            pl.when(live)(copy.wait_send)
        for index in range(4):
            for hop in range(3):
                self.third(index, hop).wait_send()
        for x in range(4):
            for index in range(4):
                self.fourth(index, x).wait_send()


def layer(
    qkv_hbm, tan_hbm, seg_ref, turned_hbm, both_ref,
    qkv_ref, tan_ref, turned_ref, shard_ref, count_ref, in_sems, stage, kv_ref, q_ref, counts_ref, kt_ref, s_ref, st_ref, top_ref, sum_ref, acc_ref, part_ref,
    tail, main, packed, rest, landing, rows_ref, total_ref,
    local_sems, kv_send, kv_recv, q_send, q_recv, n_send, n_recv, f_send,
    y_send, y_recv, z_send, z_recv, x_send, x_recv, c_send, c_recv,
    back_send, back_recv, g_send, g_recv,
):
    ctx, dp, y = lax.axis_index("ctx"), lax.axis_index("dp"), lax.axis_index("head")
    x_lo, z, x_hi, core = ctx // 8, lax.rem(ctx, 8), dp // 2, lax.rem(dp, 2)
    sample = lax.rem(z, 2)
    role = role_of(x_lo, core)
    first, count = work_of(x_lo, z, core)
    weights = Weights(
        shard_ref, tail, main, packed, local_sems.at[pl.ds(4, 2)],
        y_send, y_recv, z_send, z_recv, x_send, x_recv, c_send, c_recv,
    )

    def at(other_x, other_z, other_core):
        return {"ctx": other_x * 8 + other_z, "dp": x_hi * 2 + other_core}

    def is_me(other_x, other_z, other_core):
        return (other_x == x_lo) & (other_z == z) & (other_core == core)

    def remote(src, dst, send, recv, device):
        return pltpu.make_async_remote_copy(
            src_ref=src, dst_ref=dst, send_sem=send, recv_sem=recv, device_id=at(*device),
            device_id_type=MESH,
        )

    def rows_of(block):
        return pl.ds(pl.multiple_of(block * ROWS, ROWS), ROWS)

    loads = [
        pltpu.make_async_copy(src, dst, in_sems.at[i]) for i, (src, dst) in enumerate(
            ((qkv_hbm, qkv_ref), (tan_hbm, tan_ref), (turned_hbm, turned_ref))
        )
    ]
    for load in loads:
        load.start()
    barrier = pltpu.get_barrier_semaphore()
    for other_x in range(2):
        for step in range(8):
            source = (other_x, lax.rem(z + step, 8), sample)
            signal_if(jnp.logical_not(is_me(*source)), barrier, at(*source))
    for mate in ((1 - x_lo, z, core), (x_lo, z, 1 - core), (1 - x_lo, z, 1 - core)):
        signal_if(True, barrier, at(*mate))
    weights.greet(barrier)
    workers = [worker_of(h, ctx, core) for h in range(HEADS)]
    for worker in workers:
        signal_if(jnp.logical_not(is_me(*worker)), barrier, at(*worker))
    for step in range(1, 4):
        signal_if(True, barrier, {"head": lax.rem(y + step, 4)})
    for step in (2, 6):
        signal_if(role == 3, barrier, at(1, lax.rem(z + step, 8), 1))
    own_block = (core == sample) & (first <= ctx) & (ctx < first + count)
    lane = lax.broadcasted_iota(jnp.int32, (8, 128), 1)
    tally = jnp.zeros((8, 128), jnp.int32)
    for v in range(SEGS - 1):
        below = jnp.sum((seg_ref[...] <= v).astype(jnp.int32), axis=1, keepdims=True)
        tally = jnp.where(lane == v, below, tally)
    count_ref[...] = tally
    for load in loads:
        load.wait()
    shard_ref[...] = turned_ref[...].T
    weights.prepare()
    for slot in (4, 5):
        @pl.when(slot >= count)
        def _():
            q_ref[slot * ROWS:(slot + 1) * ROWS] = jnp.zeros((ROWS, 2 * HD), jnp.bfloat16)
    for head in range(HEADS):
        cols = slice(head * HD, (head + 1) * HD)
        stage[head, 0, :, 0:HD] = qkv_ref[1, :, cols]
        stage[head, 0, :, HD:] = tan_ref[1, :, cols]
        stage[head, 1, :, 0:HD] = qkv_ref[2, :, cols]
        stage[head, 1, :, HD:] = tan_ref[2, :, cols]
        stage[head, 2, :, 0:HD] = tan_ref[0, :, cols]
        stage[head, 2, :, HD:] = qkv_ref[0, :, cols]
    pl.semaphore_wait(
        barrier,
        22 - (core == sample).astype(jnp.int32) + weights.greetings()
        + count - own_block.astype(jnp.int32) + 2 * (role == 3).astype(jnp.int32),
    )
    weights.over_y()

    sends = []

    def send(device, src, dst, send_sem, recv_sem, local_sem, live=True):
        mine = is_me(*device)
        far = remote(src, dst, send_sem, recv_sem, device)
        away = live & jnp.logical_not(mine)
        pl.when(away)(far.start)

        @pl.when(mine)
        def _():
            pltpu.make_async_copy(src, dst, local_sem).start()
        sends.append((away, far))

    for other_x in range(2):
        for step in range(4):
            device = (other_x, 2 * lax.rem(z // 2 + step, 4) + core)
            for other_core in range(2):
                send(
                    device + (other_core,), count_ref, counts_ref.at[ctx],
                    n_send.at[other_x, step, other_core], n_recv.at[ctx], local_sems.at[0],
                )
    for head in range(HEADS):
        slot = lax.rem(ctx, 4) if head == 4 else ctx - chunk_start(chunk_of(ctx))
        send(
            worker_of(head, ctx, core), stage.at[head, 2], q_ref.at[rows_of(slot)],
            q_send.at[head], q_recv.at[slot], local_sems.at[2],
        )
    weights.over_z()
    def send_keys(step):
        turn = lax.rem(z // 2 + (0, 1, 3, 2)[step], 4)
        slice_z = 2 * turn + core
        send(
            (x_lo, slice_z, jnp.where(x_lo == 0, core, 0)), stage.at[turn, 0:2],
            kv_ref.at[:, rows_of(ctx)], kv_send.at[0, step], kv_recv.at[ctx], local_sems.at[1],
        )
        steps = lax.rem(slice_z - z + 8, 8)
        send(
            (1, slice_z, 1), stage.at[HEADS - 1, 0:2], kv_ref.at[:, rows_of(ctx)],
            kv_send.at[1, step], kv_recv.at[ctx], local_sems.at[1], (steps <= 2) | (steps >= 6),
        )

    entry = (x_lo == 0) & (core == sample)
    third = role == 2

    def forward(block, mate, index):
        dst = kv_ref.at[:, rows_of(block)]
        return remote(dst, dst, f_send.at[block, index], kv_recv.at[block], mate)

    def forwards(direct, block):
        to_core = (entry, forward(block, (0, z, 1 - core), 0))
        if direct:
            to_x = forward(block, (1 - x_lo, z, jnp.where(entry, 0, sample)), 1)
            return [to_core, (entry | third, to_x)]
        return [to_core]

    def arrived(block, ref, own_sem, sem):
        mine = (block == ctx) & (core == sample)

        @pl.when(mine)
        def _():
            pltpu.make_async_copy(ref, ref, own_sem).wait()

        @pl.when(jnp.logical_not(mine))
        def _():
            pltpu.make_async_copy(ref, ref, sem).wait()

    chain = {6: 2, 7: 2, 1: 6}

    def on(block, step):
        dst = kv_ref.at[:, rows_of(block)]
        return remote(
            dst, dst, f_send.at[block, 0], kv_recv.at[block], (1, lax.rem(z + chain[step], 8), 1)
        )

    def pass_keys(direct, step):
        block = (x_lo if direct else 1 - x_lo) * 8 + lax.rem(z + step, 8)

        @pl.when(role != 3)
        def _():
            arrived(block, kv_ref.at[:, rows_of(block)], local_sems.at[1], kv_recv.at[block])
            for live, copy in forwards(direct, block):
                pl.when(live)(copy.start)

        if direct:
            @pl.when(role == 3)
            def _():
                for other_x in range(2):
                    block = other_x * 8 + lax.rem(z + step, 8)
                    ref = kv_ref.at[:, rows_of(block)]
                    arrived(block, ref, local_sems.at[1], kv_recv.at[block])
                    if step in chain:
                        on(block, step).start()

    near = (0, 1, 7, 2, 6, 3, 5, 4)

    def events(order):
        for kind, turn in order:
            if kind in "DR":
                pass_keys(kind == "D", near[turn])
            elif kind == "X":
                weights.start_x(turn)
            elif kind == "K":
                send_keys(turn)
            else:
                x = {"I": weights.inner, "O": weights.outer, "F": weights.far}[kind]
                weights.pass_on(x, turn)

    events(ORDERS[0])
    for direct in (True, False):
        for step in range(8):
            block = (x_lo if direct else 1 - x_lo) * 8 + lax.rem(z + step, 8)
            arrived(block, counts_ref.at[block], local_sems.at[0], n_recv.at[block])
    for slot in range(SLOTS):
        @pl.when(slot < count)
        def _():
            arrived(first + slot, q_ref.at[rows_of(slot)], local_sems.at[2], q_recv.at[slot])

    def back(slot):
        block = lax.min(first + slot, BLOCKS - 1)
        head = jnp.where(role == 3, HEADS - 1, z // 2)
        own = (block == ctx) & (core == sample)
        dst = landing.at[y, head]
        far = pltpu.make_async_remote_copy(
            src_ref=part_ref.at[slot], dst_ref=dst, send_sem=back_send.at[slot],
            recv_sem=back_recv.at[head], device_id={"ctx": block, "dp": x_hi * 2 + sample},
            device_id_type=MESH,
        )
        return (slot < count) & own, (slot < count) & jnp.logical_not(own), far, dst

    scale = 1.0 / math.sqrt(HD)
    power = scale / math.log(2.0)
    below = jnp.sum(counts_ref[...], axis=0)
    bounds = [below[0:1, v:v + 1] for v in range(SEGS - 1)]

    def of_position(position, values):
        result = values[SEGS - 1]
        for v in range(SEGS - 2, -1, -1):
            result = jnp.where(position < bounds[v], values[v], result)
        return result

    starts = [jnp.zeros((1, 1), jnp.int32)] + bounds
    ends = bounds + [jnp.full((1, 1), SEQ, jnp.int32)]

    @pl.loop(0, KTILES)
    def _(tile):
        keys = pl.ds(pl.multiple_of(tile * TILE, TILE), TILE)
        kt_ref[tile] = kv_ref[0, keys].T

    for part in range(2):
        position = (first + 3 * part) * ROWS + lax.broadcasted_iota(jnp.int32, (PART, 1), 0)
        start = of_position(position, starts)
        end = of_position(position, ends)
        column = lax.broadcasted_iota(jnp.int32, (1, TILE), 1)
        rows = slice(part * PART, (part + 1) * PART)
        top_ref[...] = jnp.full_like(top_ref, -1e30)
        sum_ref[...] = jnp.zeros_like(sum_ref)
        acc_ref[...] = jnp.zeros_like(acc_ref)

        @pl.loop(0, KTILES)
        def _(tile):
            s = jnp.dot(
                q_ref[rows, HD:], kt_ref[tile, 0:HD], preferred_element_type=jnp.float32
            )
            place = column + tile * TILE
            s = jnp.where((place >= start) & (place < end), s, -1e30)
            s_ref[tile] = s
            st_ref[tile] = jnp.dot(
                q_ref[rows, :], kt_ref[tile], preferred_element_type=jnp.float32
            )
            top_ref[...] = jnp.maximum(top_ref[...], fold(jnp.maximum, s))

        top = jnp.max(top_ref[...], axis=1, keepdims=True)

        @pl.loop(0, KTILES)
        def _(tile):
            keys = pl.ds(pl.multiple_of(tile * TILE, TILE), TILE)
            prob = jnp.exp2((s_ref[tile] - top) * power)
            weighted = prob * st_ref[tile]
            sum_ref[0] += fold(jnp.add, prob)
            sum_ref[1] += fold(jnp.add, weighted)
            acc_ref[:, 0:2 * HD] += jnp.dot(
                prob.astype(jnp.bfloat16), kv_ref[1, keys], preferred_element_type=jnp.float32
            )
            acc_ref[:, 2 * HD:] += jnp.dot(
                weighted.astype(jnp.bfloat16), kv_ref[1, keys, 0:HD],
                preferred_element_type=jnp.float32,
            )

        inverse = 1.0 / jnp.sum(sum_ref[0], axis=1, keepdims=True)
        drift = jnp.sum(sum_ref[1], axis=1, keepdims=True) * scale
        plain = acc_ref[:, 0:HD] * inverse
        turned = (acc_ref[:, HD:2 * HD] + acc_ref[:, 2 * HD:] * scale - drift * plain) * inverse
        for slot in range(3):
            piece = slice(slot * ROWS, (slot + 1) * ROWS)
            part_ref[part * 3 + slot, 0] = plain[piece].astype(jnp.bfloat16)
            part_ref[part * 3 + slot, 1] = turned[piece].astype(jnp.bfloat16)
        for slot in range(part * 3, part * 3 + 3):
            own, live, far, dst = back(slot)
            pl.when(live)(far.start)

            @pl.when(own)
            def _():
                pltpu.make_async_copy(part_ref.at[slot], dst, local_sems.at[3]).start()
        events(ORDERS[1 + part])

    def to_y(owner, h, step, index):
        piece = landing.at[owner, h]
        return pltpu.make_async_remote_copy(
            src_ref=piece, dst_ref=piece, send_sem=g_send.at[h, index],
            recv_sem=g_recv.at[owner, h], device_id={"head": lax.rem(y + step, 4)}, device_id_type=MESH,
        )

    def gathers(h):
        owner, step = (3, 1) if h < 3 else (1, 3)
        return (
            to_y(y, h, 1, 0), to_y(y, h, 3, 1), to_y(lax.rem(y + owner, 4), h, step, 2),
        )

    for h in range(HEADS):
        mine = is_me(*workers[h])

        @pl.when(mine)
        def _():
            pltpu.make_async_copy(part_ref.at[0], landing.at[y, h], local_sems.at[3]).wait()

        @pl.when(jnp.logical_not(mine))
        def _():
            pltpu.make_async_copy(part_ref.at[0], landing.at[y, h], back_recv.at[h]).wait()
        for copy in gathers(h)[0:2]:
            copy.start()

    events(ORDERS[3])
    weights.arrive()
    for zq in range(4):
        for parity in range(2):
            for half in range(2):
                for quarter in range(4):
                    for side in range(2):
                        row = quarter * 160 + side * 80
                        rest[parity, half, row:row + 80, zq * 64:(zq + 1) * 64] = packed[
                            zq, parity, half, quarter * 80:(quarter + 1) * 80, side * 64:(side + 1) * 64
                        ]

    def gathered(step, h):
        other = lax.rem(y + step, 4)
        pltpu.make_async_copy(part_ref.at[0], landing.at[other, h], g_recv.at[other, h]).wait()

    for turn, step in enumerate((0, 1, 3, 2)):
        other = lax.rem(y + step, 4)
        if turn == 1:
            for h in range(HEADS):
                gathered(1, h)
                if h < 3:
                    gathered(3, h)
                gathers(h)[2].start()
        for h in range(HEADS):
            if step == 2 or (step == 3 and h >= 3):
                gathered(step, h)
            for kind in range(2):
                rows_ref[kind * ROWS:(kind + 1) * ROWS, h * HD:(h + 1) * HD] = landing[other, h, kind]
        parity, half = lax.rem(other, 2), other // 2
        for zq in range(5):
            weight = main[zq, parity, half] if zq < 4 else rest[parity, half]
            term = jnp.dot(rows_ref[...], weight, preferred_element_type=jnp.float32)
            total_ref[zq] = term if turn == 0 else total_ref[zq] + term

    for zq in range(4):
        for kind in range(2):
            rows = slice(kind * ROWS, (kind + 1) * ROWS)
            both_ref[kind, :, zq * 320:zq * 320 + 256] = total_ref[zq, rows].astype(jnp.bfloat16)
            both_ref[kind, :, zq * 320 + 256:(zq + 1) * 320] = (
                total_ref[4, rows, zq * 64:(zq + 1) * 64].astype(jnp.bfloat16)
            )

    for direct in (True, False):
        for step in range(8):
            block = (x_lo if direct else 1 - x_lo) * 8 + lax.rem(z + step, 8)
            for live, copy in forwards(direct, block):
                pl.when(live)(copy.wait_send)
    @pl.when(role == 3)
    def _():
        for step in chain:
            for other_x in range(2):
                on(other_x * 8 + lax.rem(z + step, 8), step).wait_send()
    for live, copy in sends:
        pl.when(live)(copy.wait_send)
    for slot in range(SLOTS):
        own, live, far, dst = back(slot)
        pl.when(live)(far.wait_send)
    for h in range(HEADS):
        for copy in gathers(h):
            copy.wait_send()
    weights.finish()


def local(qkv, tangent, segments, out_weight):
    vmem = pl.BlockSpec(memory_space=pltpu.VMEM)
    dma = pltpu.SemaphoreType.DMA
    bf16, f32 = jnp.bfloat16, jnp.float32
    hbm = pl.BlockSpec(memory_space=pl.ANY)
    both = pl.pallas_call(
        layer,
        out_shape=jax.ShapeDtypeStruct((2, ROWS, 1280), bf16),
        in_specs=[hbm, hbm, vmem, hbm],
        out_specs=vmem,
        scratch_shapes=[
            pltpu.VMEM((3, ROWS, HEADS * HD), bf16),
            pltpu.VMEM((3, ROWS, HEADS * HD), bf16),
            pltpu.VMEM((320, 640), bf16),
            pltpu.VMEM((640, 320), bf16),
            pltpu.VMEM((8, 128), jnp.int32),
            dma((3,)),
            pltpu.VMEM((HEADS, 3, ROWS, 2 * HD), bf16),
            pltpu.VMEM((2, SEQ, 2 * HD), bf16),
            pltpu.VMEM((SLOTS * ROWS, 2 * HD), bf16),
            pltpu.VMEM((BLOCKS, 8, 128), jnp.int32),
            pltpu.VMEM((KTILES, 2 * HD, TILE), bf16),
            pltpu.VMEM((KTILES, PART, TILE), f32),
            pltpu.VMEM((KTILES, PART, TILE), f32),
            pltpu.VMEM((PART, 128), f32),
            pltpu.VMEM((2, PART, 128), f32),
            pltpu.VMEM((PART, 3 * HD), f32),
            pltpu.VMEM((SLOTS, 2, ROWS, HD), bf16),
            pltpu.VMEM((320, 128), bf16),
            pltpu.VMEM((4, 2, 2, 640, 256), bf16),
            pltpu.VMEM((4, 2, 2, 320, 128), bf16),
            pltpu.VMEM((2, 2, 640, 256), bf16),
            pltpu.VMEM((4, HEADS, 2, ROWS, HD), bf16),
            pltpu.VMEM((2 * ROWS, HEADS * HD), bf16),
            pltpu.VMEM((5, 2 * ROWS, 256), f32),
            dma((6,)), dma((2, 4)), dma((BLOCKS,)), dma((HEADS,)), dma((SLOTS,)),
            dma((2, 4, 2)), dma((BLOCKS,)), dma((BLOCKS, 2)),
            dma((2, 2)), dma((2, 2)), dma((3, 2, 2)), dma((4, 2)),
            dma((3, 4, 2)), dma((4, 4, 2)), dma((4, 4, 2)), dma((4, 4, 2)),
            dma((SLOTS,)), dma((HEADS,)), dma((HEADS, 3)), dma((4, HEADS)),
        ],
        compiler_params=pltpu.CompilerParams(
            collective_id=0, has_side_effects=True, vmem_limit_bytes=56 * 2**20
        ),
        name="layer",
    )(qkv, tangent, segments.reshape(1, ROWS), out_weight.T)
    return both[0], both[1]


def solution(mesh):
    return jax.shard_map(
        local,
        mesh=mesh,
        in_specs=(
            P(None, ("dp", "ctx"), "head"),
            P(None, ("dp", "ctx"), "head"),
            P(("dp", "ctx")),
            P("head", "ctx"),
        ),
        out_specs=(P(("dp", "ctx"), "head"), P(("dp", "ctx"), "head")),
        check_vma=False,
    )
```

```python
import functools
import math

import jax
import jax.numpy as jnp
from jax import lax
from jax.experimental import pallas as pl
from jax.experimental.pallas import tpu as pltpu
from jax.sharding import PartitionSpec as P

HD = 128
HEADS = 5
BLOCKS = 16
ROWS = 160
SEQ = BLOCKS * ROWS
SLOTS = 6
SEGS = 4
TILE = 512
PART = 480


def several(kind, first, last):
    return [(kind, turn) for turn in range(first, last)]


ORDERS = (
    several("X", 0, 1) + several("K", 0, 2) + several("X", 1, 3) + several("K", 2, 4) + several("D", 0, 1)
    + several("X", 3, 4) + several("D", 1, 4) + several("I", 0, 4) + several("D", 4, 8) + several("R", 0, 8),
    several("O", 0, 4),
    several("F", 0, 4),
    [],
)
KTILES = SEQ // TILE
MESH = pl.DeviceIdType.MESH


def role_of(x_lo, core):
    return x_lo * 2 + core


def chunk_of(block):
    return (block >= 6).astype(jnp.int32) + (block >= 11).astype(jnp.int32)


def chunk_start(chunk):
    return chunk * 5 + jnp.minimum(chunk, 1)


def work_of(x_lo, z, core):
    role = role_of(x_lo, core)
    first = jnp.where(role == 3, 4 * (z // 2), chunk_start(role))
    count = jnp.where(role == 3, 4, 5 + (role == 0).astype(jnp.int32))
    return first, count


def worker_of(head, block, core):
    if head == HEADS - 1:
        return 1, 2 * (block // 4) + core, 1
    role = chunk_of(block)
    return role // 2, 2 * head + core, lax.rem(role, 2)


def fold(op, values):
    parts = [values[:, i:i + 128] for i in range(0, values.shape[1], 128)]
    while len(parts) > 1:
        parts = [op(a, b) for a, b in zip(parts[0::2], parts[1::2])]
    return parts[0]


def signal_if(condition, semaphore, device):
    @pl.when(condition)
    def _():
        pl.semaphore_signal(semaphore, inc=1, device_id=device, device_id_type=MESH)


class Both:
    def __init__(self, copies):
        self.copies = copies

    def start(self):
        for copy in self.copies:
            copy.start()

    def wait_send(self):
        for copy in self.copies:
            copy.wait_send()


class Weights:
    def __init__(self, shard_ref, tail_ref, main_ref, packed_ref, local_sems, *sems):
        self.shard, self.tail, self.local_sems = shard_ref, tail_ref, local_sems
        self.main, self.packed = main_ref, packed_ref
        (self.y_send, self.y_recv, self.z_send, self.z_recv,
         self.x_send, self.x_recv, self.c_send, self.c_recv) = sems
        self.ctx, self.y, dp = lax.axis_index("ctx"), lax.axis_index("head"), lax.axis_index("dp")
        self.x_lo, self.z = self.ctx // 8, lax.rem(self.ctx, 8)
        self.x_hi, self.core = dp // 2, lax.rem(dp, 2)
        self.x = self.x_hi * 2 + self.x_lo
        self.inner = self.x_hi * 2 + 1 - self.x_lo
        self.outer = lax.rem(self.x + 3 + 2 * self.x_lo, 4)
        self.far = lax.rem(self.x + 2, 4)
        self.active = lax.rem(self.z, 2) == self.core
        self.parity = lax.rem(self.z // 4 + self.y, 2)

    def prepare(self):
        for quarter in range(4):
            for side in range(2):
                row = quarter * 160 + side * 80
                self.tail[quarter * 80:(quarter + 1) * 80, side * 64:(side + 1) * 64] = (
                    self.shard[row:row + 80, 256:320]
                )

    def device(self, x=None, z=None, y=None, core=None):
        x = self.x if x is None else x
        z = self.z if z is None else z
        y = self.y if y is None else y
        core = self.core if core is None else core
        return {"ctx": lax.rem(x, 2) * 8 + z, "head": y, "dp": (x // 2) * 2 + core}

    def first_target(self, same):
        y = self.x_lo * 2 + self.z // 4
        x = self.x if same else self.x_hi * 2 + 1 - self.x_lo
        z = lax.rem(self.z + 4 * lax.rem(self.y, 2), 8)
        is_me = (x == self.x) & (y == self.y) & (z == self.z)
        return x, z, y, is_me

    def first_source(self, half):
        y = 2 * half + self.parity
        x = self.x_hi * 2 + self.y // 2
        z = lax.rem(self.z + 4 * self.parity, 8)
        is_me = (x == self.x) & (y == self.y) & (z == self.z)
        return x, z, y, is_me

    def greet(self, barrier):
        for half in range(2):
            x, z, y, is_me = self.first_source(half)
            signal_if(self.active & jnp.logical_not(is_me), barrier, self.device(x, z, y))
        for x in (self.inner, self.outer):
            signal_if(True, barrier, self.device(x=x))
        signal_if(True, barrier, self.device(core=1 - self.core))
        for step in (1, 7):
            signal_if(True, barrier, self.device(z=lax.rem(self.z + step, 8)))

    def greetings(self):
        count = jnp.int32(5)
        for same in (True, False):
            is_me = self.first_target(same)[3]
            count = count + (self.active & jnp.logical_not(is_me)).astype(jnp.int32)
        return count

    def rows(self, quarter):
        return (
            pl.ds(pl.multiple_of(quarter * 160, 160), 160),
            pl.ds(pl.multiple_of(quarter * 80, 80), 80),
        )

    def piece(self, zq, parity, x):
        wide, narrow = self.rows(x)
        return self.main.at[zq, parity, :, wide], self.packed.at[zq, parity, :, narrow]

    def landed(self, refs, sems):
        for i, ref in enumerate(refs):
            pltpu.make_async_copy(ref, ref, sems.at[i]).wait()

    def remote(self, srcs, dsts, send, recv, device):
        return Both([
            pltpu.make_async_remote_copy(
                src_ref=src, dst_ref=dst, send_sem=send.at[i], recv_sem=recv.at[i],
                device_id=device, device_id_type=MESH,
            ) for i, (src, dst) in enumerate(zip(srcs, dsts))
        ])

    def first(self, index):
        x, z, y, is_me = self.first_target(index == 0)
        wide, narrow = self.rows(x)
        zq, parity, half = lax.rem(self.z, 4), lax.rem(self.y, 2), self.y // 2
        srcs = self.shard.at[wide, 0:256], self.tail.at[narrow]
        dsts = self.main.at[zq, parity, half, wide], self.packed.at[zq, parity, half, narrow]
        far = self.remote(
            srcs, dsts, self.y_send.at[index], self.y_recv.at[half], self.device(x, z, y)
        )
        return is_me, far, srcs, dsts

    def over_y(self):
        for index in range(2):
            is_me, far, srcs, dsts = self.first(index)
            pl.when(self.active & jnp.logical_not(is_me))(far.start)

            @pl.when(self.active & is_me)
            def _():
                for i in range(2):
                    pltpu.make_async_copy(srcs[i], dsts[i], self.local_sems.at[i]).start()

    def second(self, turn, back):
        z, zq, parity = self.from_z(self.order(turn))
        mine = self.piece(zq, parity, self.x)
        return self.remote(
            mine, mine, self.z_send.at[turn, int(back)], self.z_recv.at[z // 2],
            self.device(z=lax.rem(self.z + (7 if back else 1), 8)),
        )

    def seconds(self):
        passive = jnp.logical_not(self.active)
        return (
            (0, True, self.second(0, False)), (0, self.active, self.second(0, True)),
            (1, self.active, self.second(1, False)), (1, passive, self.second(1, True)),
            (2, passive, self.second(2, False)), (2, self.active, self.second(2, True)),
        )

    def over_z(self):
        @pl.when(self.active)
        def _():
            for index in range(2):
                is_me, far, srcs, dsts = self.first(index)
                pl.when(jnp.logical_not(is_me))(far.wait_send)
            for half in range(2):
                is_me = self.first_source(half)[3]
                wide, narrow = self.rows(self.x)
                zq = lax.rem(self.z, 4)
                dst = (
                    self.main.at[zq, self.parity, half, wide],
                    self.packed.at[zq, self.parity, half, narrow],
                )

                @pl.when(is_me)
                def _():
                    self.landed(dst, self.local_sems)

                @pl.when(jnp.logical_not(is_me))
                def _():
                    self.landed(dst, self.y_recv.at[half])

    def from_z(self, index):
        z = 2 * index + self.core
        return z, lax.rem(z, 4), lax.rem(z // 4 + self.y, 2)

    def order(self, turn):
        step = jnp.where(self.active, (0, 6, 2, 4)[turn], (7, 1, 5, 3)[turn])
        return lax.rem(self.z + step, 8) // 2

    def third(self, index, hop):
        z, zq, parity = self.from_z(index)
        owner = self.inner if hop == 2 else self.x
        mine = self.piece(zq, parity, owner)
        return self.remote(
            mine, mine, self.x_send.at[hop, index], self.x_recv.at[owner, index],
            self.device(x=self.outer if hop else self.inner),
        )

    def fourth(self, index, x):
        z, zq, parity = self.from_z(index)
        mine = self.piece(zq, parity, x)
        return self.remote(
            mine, mine, self.c_send.at[x, index], self.c_recv.at[x, index],
            self.device(core=1 - self.core),
        )

    def start_x(self, turn):
        index = self.order(turn)
        z, zq, parity = self.from_z(index)

        @pl.when(z != self.z)
        def _():
            self.landed(self.piece(zq, parity, self.x), self.z_recv.at[index])
        for other, live, copy in self.seconds():
            if other == turn:
                pl.when(live)(copy.start)
        self.third(index, 0).start()
        self.third(index, 1).start()
        self.fourth(index, self.x).start()

    def pass_on(self, x, turn):
        index = self.order(turn)
        z, zq, parity = self.from_z(index)
        self.landed(self.piece(zq, parity, x), self.x_recv.at[x, index])
        if x is self.inner:
            self.third(index, 2).start()
        self.fourth(index, x).start()

    def arrive(self):
        for x in range(4):
            for index in range(4):
                z = 2 * index + 1 - self.core
                other = self.piece(lax.rem(z, 4), lax.rem(z // 4 + self.y, 2), x)
                self.landed(other, self.c_recv.at[x, index])

    def finish(self):
        for turn, live, copy in self.seconds():
            pl.when(live)(copy.wait_send)
        for index in range(4):
            for hop in range(3):
                self.third(index, hop).wait_send()
        for x in range(4):
            for index in range(4):
                self.fourth(index, x).wait_send()


def layer(
    qkv_hbm, tan_hbm, seg_ref, turned_hbm, both_ref,
    qkv_ref, tan_ref, turned_ref, shard_ref, count_ref, in_sems, stage, kv_ref, q_ref, counts_ref, kt_ref, s_ref, st_ref, top_ref, sum_ref, acc_ref, part_ref,
    tail, main, packed, rest, landing, rows_ref, total_ref,
    local_sems, kv_send, kv_recv, q_send, q_recv, n_send, n_recv, f_send,
    y_send, y_recv, z_send, z_recv, x_send, x_recv, c_send, c_recv,
    back_send, back_recv, g_send, g_recv,
):
    ctx, dp, y = lax.axis_index("ctx"), lax.axis_index("dp"), lax.axis_index("head")
    x_lo, z, x_hi, core = ctx // 8, lax.rem(ctx, 8), dp // 2, lax.rem(dp, 2)
    sample = lax.rem(z, 2)
    role = role_of(x_lo, core)
    first, count = work_of(x_lo, z, core)
    weights = Weights(
        shard_ref, tail, main, packed, local_sems.at[pl.ds(4, 2)],
        y_send, y_recv, z_send, z_recv, x_send, x_recv, c_send, c_recv,
    )

    def at(other_x, other_z, other_core):
        return {"ctx": other_x * 8 + other_z, "dp": x_hi * 2 + other_core}

    def is_me(other_x, other_z, other_core):
        return (other_x == x_lo) & (other_z == z) & (other_core == core)

    def remote(src, dst, send, recv, device):
        return pltpu.make_async_remote_copy(
            src_ref=src, dst_ref=dst, send_sem=send, recv_sem=recv, device_id=at(*device),
            device_id_type=MESH,
        )

    def rows_of(block):
        return pl.ds(pl.multiple_of(block * ROWS, ROWS), ROWS)

    loads = [
        pltpu.make_async_copy(src, dst, in_sems.at[i]) for i, (src, dst) in enumerate(
            ((qkv_hbm, qkv_ref), (tan_hbm, tan_ref), (turned_hbm, turned_ref))
        )
    ]
    for load in loads:
        load.start()
    barrier = pltpu.get_barrier_semaphore()
    for other_x in range(2):
        for step in range(8):
            source = (other_x, lax.rem(z + step, 8), sample)
            signal_if(jnp.logical_not(is_me(*source)), barrier, at(*source))
    for mate in ((1 - x_lo, z, core), (x_lo, z, 1 - core), (1 - x_lo, z, 1 - core)):
        signal_if(True, barrier, at(*mate))
    weights.greet(barrier)
    workers = [worker_of(h, ctx, core) for h in range(HEADS)]
    for worker in workers:
        signal_if(jnp.logical_not(is_me(*worker)), barrier, at(*worker))
    for step in range(1, 4):
        signal_if(True, barrier, {"head": lax.rem(y + step, 4)})
    for step in (2, 6):
        signal_if(role == 3, barrier, at(1, lax.rem(z + step, 8), 1))
    own_block = (core == sample) & (first <= ctx) & (ctx < first + count)
    lane = lax.broadcasted_iota(jnp.int32, (8, 128), 1)
    tally = jnp.zeros((8, 128), jnp.int32)
    for v in range(SEGS - 1):
        below = jnp.sum((seg_ref[...] <= v).astype(jnp.int32), axis=1, keepdims=True)
        tally = jnp.where(lane == v, below, tally)
    count_ref[...] = tally
    for load in loads:
        load.wait()
    shard_ref[...] = turned_ref[...].T
    weights.prepare()
    for slot in (4, 5):
        @pl.when(slot >= count)
        def _():
            q_ref[slot * ROWS:(slot + 1) * ROWS] = jnp.zeros((ROWS, 2 * HD), jnp.bfloat16)
    for head in range(HEADS):
        cols = slice(head * HD, (head + 1) * HD)
        stage[head, 0, :, 0:HD] = qkv_ref[1, :, cols]
        stage[head, 0, :, HD:] = tan_ref[1, :, cols]
        stage[head, 1, :, 0:HD] = qkv_ref[2, :, cols]
        stage[head, 1, :, HD:] = tan_ref[2, :, cols]
        stage[head, 2, :, 0:HD] = tan_ref[0, :, cols]
        stage[head, 2, :, HD:] = qkv_ref[0, :, cols]
    pl.semaphore_wait(
        barrier,
        22 - (core == sample).astype(jnp.int32) + weights.greetings()
        + count - own_block.astype(jnp.int32) + 2 * (role == 3).astype(jnp.int32),
    )
    weights.over_y()

    sends = []

    def send(device, src, dst, send_sem, recv_sem, local_sem, live=True):
        mine = is_me(*device)
        far = remote(src, dst, send_sem, recv_sem, device)
        away = live & jnp.logical_not(mine)
        pl.when(away)(far.start)

        @pl.when(mine)
        def _():
            pltpu.make_async_copy(src, dst, local_sem).start()
        sends.append((away, far))

    for other_x in range(2):
        for step in range(4):
            device = (other_x, 2 * lax.rem(z // 2 + step, 4) + core)
            for other_core in range(2):
                send(
                    device + (other_core,), count_ref, counts_ref.at[ctx],
                    n_send.at[other_x, step, other_core], n_recv.at[ctx], local_sems.at[0],
                )
    for head in range(HEADS):
        slot = lax.rem(ctx, 4) if head == 4 else ctx - chunk_start(chunk_of(ctx))
        send(
            worker_of(head, ctx, core), stage.at[head, 2], q_ref.at[rows_of(slot)],
            q_send.at[head], q_recv.at[slot], local_sems.at[2],
        )
    weights.over_z()
    def send_keys(step):
        turn = lax.rem(z // 2 + (0, 1, 3, 2)[step], 4)
        slice_z = 2 * turn + core
        send(
            (x_lo, slice_z, jnp.where(x_lo == 0, core, 0)), stage.at[turn, 0:2],
            kv_ref.at[:, rows_of(ctx)], kv_send.at[0, step], kv_recv.at[ctx], local_sems.at[1],
        )
        steps = lax.rem(slice_z - z + 8, 8)
        send(
            (1, slice_z, 1), stage.at[HEADS - 1, 0:2], kv_ref.at[:, rows_of(ctx)],
            kv_send.at[1, step], kv_recv.at[ctx], local_sems.at[1], (steps <= 2) | (steps >= 6),
        )

    entry = (x_lo == 0) & (core == sample)
    third = role == 2

    def forward(block, mate, index):
        dst = kv_ref.at[:, rows_of(block)]
        return remote(dst, dst, f_send.at[block, index], kv_recv.at[block], mate)

    def forwards(direct, block):
        to_core = (entry, forward(block, (0, z, 1 - core), 0))
        if direct:
            to_x = forward(block, (1 - x_lo, z, jnp.where(entry, 0, sample)), 1)
            return [to_core, (entry | third, to_x)]
        return [to_core]

    def arrived(block, ref, own_sem, sem):
        mine = (block == ctx) & (core == sample)

        @pl.when(mine)
        def _():
            pltpu.make_async_copy(ref, ref, own_sem).wait()

        @pl.when(jnp.logical_not(mine))
        def _():
            pltpu.make_async_copy(ref, ref, sem).wait()

    chain = {6: 2, 7: 2, 1: 6}

    def on(block, step):
        dst = kv_ref.at[:, rows_of(block)]
        return remote(
            dst, dst, f_send.at[block, 0], kv_recv.at[block], (1, lax.rem(z + chain[step], 8), 1)
        )

    def pass_keys(direct, step):
        block = (x_lo if direct else 1 - x_lo) * 8 + lax.rem(z + step, 8)

        @pl.when(role != 3)
        def _():
            arrived(block, kv_ref.at[:, rows_of(block)], local_sems.at[1], kv_recv.at[block])
            for live, copy in forwards(direct, block):
                pl.when(live)(copy.start)

        if direct:
            @pl.when(role == 3)
            def _():
                for other_x in range(2):
                    block = other_x * 8 + lax.rem(z + step, 8)
                    ref = kv_ref.at[:, rows_of(block)]
                    arrived(block, ref, local_sems.at[1], kv_recv.at[block])
                    if step in chain:
                        on(block, step).start()

    near = (0, 1, 7, 2, 6, 3, 5, 4)

    def events(order):
        for kind, turn in order:
            if kind in "DR":
                pass_keys(kind == "D", near[turn])
            elif kind == "X":
                weights.start_x(turn)
            elif kind == "K":
                send_keys(turn)
            else:
                x = {"I": weights.inner, "O": weights.outer, "F": weights.far}[kind]
                weights.pass_on(x, turn)

    events(ORDERS[0])
    for direct in (True, False):
        for step in range(8):
            block = (x_lo if direct else 1 - x_lo) * 8 + lax.rem(z + step, 8)
            arrived(block, counts_ref.at[block], local_sems.at[0], n_recv.at[block])
    for slot in range(SLOTS):
        @pl.when(slot < count)
        def _():
            arrived(first + slot, q_ref.at[rows_of(slot)], local_sems.at[2], q_recv.at[slot])

    def back(slot):
        block = lax.min(first + slot, BLOCKS - 1)
        head = jnp.where(role == 3, HEADS - 1, z // 2)
        own = (block == ctx) & (core == sample)
        dst = landing.at[y, head]
        far = pltpu.make_async_remote_copy(
            src_ref=part_ref.at[slot], dst_ref=dst, send_sem=back_send.at[slot],
            recv_sem=back_recv.at[head], device_id={"ctx": block, "dp": x_hi * 2 + sample},
            device_id_type=MESH,
        )
        return (slot < count) & own, (slot < count) & jnp.logical_not(own), far, dst

    scale = 1.0 / math.sqrt(HD)
    power = scale / math.log(2.0)
    below = jnp.sum(counts_ref[...], axis=0)
    bounds = [below[0:1, v:v + 1] for v in range(SEGS - 1)]

    def of_position(position, values):
        result = values[SEGS - 1]
        for v in range(SEGS - 2, -1, -1):
            result = jnp.where(position < bounds[v], values[v], result)
        return result

    starts = [jnp.zeros((1, 1), jnp.int32)] + bounds
    ends = bounds + [jnp.full((1, 1), SEQ, jnp.int32)]

    @pl.loop(0, KTILES)
    def _(tile):
        keys = pl.ds(pl.multiple_of(tile * TILE, TILE), TILE)
        kt_ref[tile] = kv_ref[0, keys].T

    for part in range(2):
        position = (first + 3 * part) * ROWS + lax.broadcasted_iota(jnp.int32, (PART, 1), 0)
        start = of_position(position, starts)
        end = of_position(position, ends)
        column = lax.broadcasted_iota(jnp.int32, (1, TILE), 1)
        rows = slice(part * PART, (part + 1) * PART)
        top_ref[...] = jnp.full_like(top_ref, -1e30)
        sum_ref[...] = jnp.zeros_like(sum_ref)
        acc_ref[...] = jnp.zeros_like(acc_ref)

        @pl.loop(0, KTILES)
        def _(tile):
            s = jnp.dot(
                q_ref[rows, HD:], kt_ref[tile, 0:HD], preferred_element_type=jnp.float32
            )
            place = column + tile * TILE
            s = jnp.where((place >= start) & (place < end), s, -1e30)
            s_ref[tile] = s
            st_ref[tile] = jnp.dot(
                q_ref[rows, :], kt_ref[tile], preferred_element_type=jnp.float32
            )
            top_ref[...] = jnp.maximum(top_ref[...], fold(jnp.maximum, s))

        top = jnp.max(top_ref[...], axis=1, keepdims=True)

        @pl.loop(0, KTILES)
        def _(tile):
            keys = pl.ds(pl.multiple_of(tile * TILE, TILE), TILE)
            prob = jnp.exp2((s_ref[tile] - top) * power)
            weighted = prob * st_ref[tile]
            sum_ref[0] += fold(jnp.add, prob)
            sum_ref[1] += fold(jnp.add, weighted)
            acc_ref[:, 0:2 * HD] += jnp.dot(
                prob.astype(jnp.bfloat16), kv_ref[1, keys], preferred_element_type=jnp.float32
            )
            acc_ref[:, 2 * HD:] += jnp.dot(
                weighted.astype(jnp.bfloat16), kv_ref[1, keys, 0:HD],
                preferred_element_type=jnp.float32,
            )

        inverse = 1.0 / jnp.sum(sum_ref[0], axis=1, keepdims=True)
        drift = jnp.sum(sum_ref[1], axis=1, keepdims=True) * scale
        plain = acc_ref[:, 0:HD] * inverse
        turned = (acc_ref[:, HD:2 * HD] + acc_ref[:, 2 * HD:] * scale - drift * plain) * inverse
        for slot in range(3):
            piece = slice(slot * ROWS, (slot + 1) * ROWS)
            part_ref[part * 3 + slot, 0] = plain[piece].astype(jnp.bfloat16)
            part_ref[part * 3 + slot, 1] = turned[piece].astype(jnp.bfloat16)
        for slot in range(part * 3, part * 3 + 3):
            own, live, far, dst = back(slot)
            pl.when(live)(far.start)

            @pl.when(own)
            def _():
                pltpu.make_async_copy(part_ref.at[slot], dst, local_sems.at[3]).start()
        events(ORDERS[1 + part])

    def to_y(owner, h, step, index):
        piece = landing.at[owner, h]
        return pltpu.make_async_remote_copy(
            src_ref=piece, dst_ref=piece, send_sem=g_send.at[h, index],
            recv_sem=g_recv.at[owner, h], device_id={"head": lax.rem(y + step, 4)}, device_id_type=MESH,
        )

    def gathers(h):
        owner, step = (3, 1) if h < 3 else (1, 3)
        return (
            to_y(y, h, 1, 0), to_y(y, h, 3, 1), to_y(lax.rem(y + owner, 4), h, step, 2),
        )

    for h in range(HEADS):
        mine = is_me(*workers[h])

        @pl.when(mine)
        def _():
            pltpu.make_async_copy(part_ref.at[0], landing.at[y, h], local_sems.at[3]).wait()

        @pl.when(jnp.logical_not(mine))
        def _():
            pltpu.make_async_copy(part_ref.at[0], landing.at[y, h], back_recv.at[h]).wait()
        for copy in gathers(h)[0:2]:
            copy.start()

    events(ORDERS[3])
    weights.arrive()
    for zq in range(4):
        for parity in range(2):
            for half in range(2):
                for quarter in range(4):
                    for side in range(2):
                        row = quarter * 160 + side * 80
                        rest[parity, half, row:row + 80, zq * 64:(zq + 1) * 64] = packed[
                            zq, parity, half, quarter * 80:(quarter + 1) * 80, side * 64:(side + 1) * 64
                        ]

    def gathered(step, h):
        other = lax.rem(y + step, 4)
        pltpu.make_async_copy(part_ref.at[0], landing.at[other, h], g_recv.at[other, h]).wait()

    for turn, step in enumerate((0, 1, 3, 2)):
        other = lax.rem(y + step, 4)
        if turn == 1:
            for h in range(HEADS):
                gathered(1, h)
                if h < 3:
                    gathered(3, h)
                gathers(h)[2].start()
        for h in range(HEADS):
            if step == 2 or (step == 3 and h >= 3):
                gathered(step, h)
            for kind in range(2):
                rows_ref[kind * ROWS:(kind + 1) * ROWS, h * HD:(h + 1) * HD] = landing[other, h, kind]
        parity, half = lax.rem(other, 2), other // 2
        for zq in range(5):
            weight = main[zq, parity, half] if zq < 4 else rest[parity, half]
            term = jnp.dot(rows_ref[...], weight, preferred_element_type=jnp.float32)
            total_ref[zq] = term if turn == 0 else total_ref[zq] + term

    for zq in range(4):
        for kind in range(2):
            rows = slice(kind * ROWS, (kind + 1) * ROWS)
            both_ref[kind, :, zq * 320:zq * 320 + 256] = total_ref[zq, rows].astype(jnp.bfloat16)
            both_ref[kind, :, zq * 320 + 256:(zq + 1) * 320] = (
                total_ref[4, rows, zq * 64:(zq + 1) * 64].astype(jnp.bfloat16)
            )

    for direct in (True, False):
        for step in range(8):
            block = (x_lo if direct else 1 - x_lo) * 8 + lax.rem(z + step, 8)
            for live, copy in forwards(direct, block):
                pl.when(live)(copy.wait_send)
    @pl.when(role == 3)
    def _():
        for step in chain:
            for other_x in range(2):
                on(other_x * 8 + lax.rem(z + step, 8), step).wait_send()
    for live, copy in sends:
        pl.when(live)(copy.wait_send)
    for slot in range(SLOTS):
        own, live, far, dst = back(slot)
        pl.when(live)(far.wait_send)
    for h in range(HEADS):
        for copy in gathers(h):
            copy.wait_send()
    weights.finish()


def local(qkv, tangent, segments, out_weight):
    vmem = pl.BlockSpec(memory_space=pltpu.VMEM)
    dma = pltpu.SemaphoreType.DMA
    bf16, f32 = jnp.bfloat16, jnp.float32
    hbm = pl.BlockSpec(memory_space=pl.ANY)
    both = pl.pallas_call(
        layer,
        out_shape=jax.ShapeDtypeStruct((2, ROWS, 1280), bf16),
        in_specs=[hbm, hbm, vmem, hbm],
        out_specs=vmem,
        scratch_shapes=[
            pltpu.VMEM((3, ROWS, HEADS * HD), bf16),
            pltpu.VMEM((3, ROWS, HEADS * HD), bf16),
            pltpu.VMEM((320, 640), bf16),
            pltpu.VMEM((640, 320), bf16),
            pltpu.VMEM((8, 128), jnp.int32),
            dma((3,)),
            pltpu.VMEM((HEADS, 3, ROWS, 2 * HD), bf16),
            pltpu.VMEM((2, SEQ, 2 * HD), bf16),
            pltpu.VMEM((SLOTS * ROWS, 2 * HD), bf16),
            pltpu.VMEM((BLOCKS, 8, 128), jnp.int32),
            pltpu.VMEM((KTILES, 2 * HD, TILE), bf16),
            pltpu.VMEM((KTILES, PART, TILE), f32),
            pltpu.VMEM((KTILES, PART, TILE), f32),
            pltpu.VMEM((PART, 128), f32),
            pltpu.VMEM((2, PART, 128), f32),
            pltpu.VMEM((PART, 3 * HD), f32),
            pltpu.VMEM((SLOTS, 2, ROWS, HD), bf16),
            pltpu.VMEM((320, 128), bf16),
            pltpu.VMEM((4, 2, 2, 640, 256), bf16),
            pltpu.VMEM((4, 2, 2, 320, 128), bf16),
            pltpu.VMEM((2, 2, 640, 256), bf16),
            pltpu.VMEM((4, HEADS, 2, ROWS, HD), bf16),
            pltpu.VMEM((2 * ROWS, HEADS * HD), bf16),
            pltpu.VMEM((5, 2 * ROWS, 256), f32),
            dma((6,)), dma((2, 4)), dma((BLOCKS,)), dma((HEADS,)), dma((SLOTS,)),
            dma((2, 4, 2)), dma((BLOCKS,)), dma((BLOCKS, 2)),
            dma((2, 2)), dma((2, 2)), dma((3, 2, 2)), dma((4, 2)),
            dma((3, 4, 2)), dma((4, 4, 2)), dma((4, 4, 2)), dma((4, 4, 2)),
            dma((SLOTS,)), dma((HEADS,)), dma((HEADS, 3)), dma((4, HEADS)),
        ],
        compiler_params=pltpu.CompilerParams(
            collective_id=0, has_side_effects=True, vmem_limit_bytes=56 * 2**20
        ),
        name="layer",
    )(qkv, tangent, segments.reshape(1, ROWS), out_weight.T)
    return both[0], both[1]


def solution(mesh):
    return jax.shard_map(
        local,
        mesh=mesh,
        in_specs=(
            P(None, ("dp", "ctx"), "head"),
            P(None, ("dp", "ctx"), "head"),
            P(("dp", "ctx")),
            P("head", "ctx"),
        ),
        out_specs=(P(("dp", "ctx"), "head"), P(("dp", "ctx"), "head")),
        check_vma=False,
    )
```

```python
import functools
import math

import jax
import jax.numpy as jnp
from jax import lax
from jax.experimental import pallas as pl
from jax.experimental.pallas import tpu as pltpu
from jax.sharding import PartitionSpec as P

HD = 128
HEADS = 5
BLOCKS = 16
ROWS = 160
SEQ = BLOCKS * ROWS
SLOTS = 6
SEGS = 4
TILE = 512
PART = 480


def several(kind, first, last):
    return [(kind, turn) for turn in range(first, last)]


ORDERS = (
    several("X", 0, 1) + several("K", 0, 2) + several("X", 1, 3) + several("K", 2, 4) + several("D", 0, 2)
    + several("X", 3, 4) + several("D", 2, 5) + several("I", 0, 4) + several("D", 5, 8) + several("R", 0, 8),
    several("O", 0, 4),
    several("F", 0, 4),
    [],
)
KTILES = SEQ // TILE
MESH = pl.DeviceIdType.MESH


def role_of(x_lo, core):
    return x_lo * 2 + core


def chunk_of(block):
    return (block >= 6).astype(jnp.int32) + (block >= 11).astype(jnp.int32)


def chunk_start(chunk):
    return chunk * 5 + jnp.minimum(chunk, 1)


def work_of(x_lo, z, core):
    role = role_of(x_lo, core)
    first = jnp.where(role == 3, 4 * (z // 2), chunk_start(role))
    count = jnp.where(role == 3, 4, 5 + (role == 0).astype(jnp.int32))
    return first, count


def worker_of(head, block, core):
    if head == HEADS - 1:
        return 1, 2 * (block // 4) + core, 1
    role = chunk_of(block)
    return role // 2, 2 * head + core, lax.rem(role, 2)


def fold(op, values):
    parts = [values[:, i:i + 128] for i in range(0, values.shape[1], 128)]
    while len(parts) > 1:
        parts = [op(a, b) for a, b in zip(parts[0::2], parts[1::2])]
    return parts[0]


def signal_if(condition, semaphore, device):
    @pl.when(condition)
    def _():
        pl.semaphore_signal(semaphore, inc=1, device_id=device, device_id_type=MESH)


class Both:
    def __init__(self, copies):
        self.copies = copies

    def start(self):
        for copy in self.copies:
            copy.start()

    def wait_send(self):
        for copy in self.copies:
            copy.wait_send()


class Weights:
    def __init__(self, shard_ref, tail_ref, main_ref, packed_ref, local_sems, *sems):
        self.shard, self.tail, self.local_sems = shard_ref, tail_ref, local_sems
        self.main, self.packed = main_ref, packed_ref
        (self.y_send, self.y_recv, self.z_send, self.z_recv,
         self.x_send, self.x_recv, self.c_send, self.c_recv) = sems
        self.ctx, self.y, dp = lax.axis_index("ctx"), lax.axis_index("head"), lax.axis_index("dp")
        self.x_lo, self.z = self.ctx // 8, lax.rem(self.ctx, 8)
        self.x_hi, self.core = dp // 2, lax.rem(dp, 2)
        self.x = self.x_hi * 2 + self.x_lo
        self.inner = self.x_hi * 2 + 1 - self.x_lo
        self.outer = lax.rem(self.x + 3 + 2 * self.x_lo, 4)
        self.far = lax.rem(self.x + 2, 4)
        self.active = lax.rem(self.z, 2) == self.core
        self.parity = lax.rem(self.z // 4 + self.y, 2)

    def prepare(self):
        for quarter in range(4):
            for side in range(2):
                row = quarter * 160 + side * 80
                self.tail[quarter * 80:(quarter + 1) * 80, side * 64:(side + 1) * 64] = (
                    self.shard[row:row + 80, 256:320]
                )

    def device(self, x=None, z=None, y=None, core=None):
        x = self.x if x is None else x
        z = self.z if z is None else z
        y = self.y if y is None else y
        core = self.core if core is None else core
        return {"ctx": lax.rem(x, 2) * 8 + z, "head": y, "dp": (x // 2) * 2 + core}

    def first_target(self, same):
        y = self.x_lo * 2 + self.z // 4
        x = self.x if same else self.x_hi * 2 + 1 - self.x_lo
        z = lax.rem(self.z + 4 * lax.rem(self.y, 2), 8)
        is_me = (x == self.x) & (y == self.y) & (z == self.z)
        return x, z, y, is_me

    def first_source(self, half):
        y = 2 * half + self.parity
        x = self.x_hi * 2 + self.y // 2
        z = lax.rem(self.z + 4 * self.parity, 8)
        is_me = (x == self.x) & (y == self.y) & (z == self.z)
        return x, z, y, is_me

    def greet(self, barrier):
        for half in range(2):
            x, z, y, is_me = self.first_source(half)
            signal_if(self.active & jnp.logical_not(is_me), barrier, self.device(x, z, y))
        for x in (self.inner, self.outer):
            signal_if(True, barrier, self.device(x=x))
        signal_if(True, barrier, self.device(core=1 - self.core))
        for step in (1, 7):
            signal_if(True, barrier, self.device(z=lax.rem(self.z + step, 8)))

    def greetings(self):
        count = jnp.int32(5)
        for same in (True, False):
            is_me = self.first_target(same)[3]
            count = count + (self.active & jnp.logical_not(is_me)).astype(jnp.int32)
        return count

    def rows(self, quarter):
        return (
            pl.ds(pl.multiple_of(quarter * 160, 160), 160),
            pl.ds(pl.multiple_of(quarter * 80, 80), 80),
        )

    def piece(self, zq, parity, x):
        wide, narrow = self.rows(x)
        return self.main.at[zq, parity, :, wide], self.packed.at[zq, parity, :, narrow]

    def landed(self, refs, sems):
        for i, ref in enumerate(refs):
            pltpu.make_async_copy(ref, ref, sems.at[i]).wait()

    def remote(self, srcs, dsts, send, recv, device):
        return Both([
            pltpu.make_async_remote_copy(
                src_ref=src, dst_ref=dst, send_sem=send.at[i], recv_sem=recv.at[i],
                device_id=device, device_id_type=MESH,
            ) for i, (src, dst) in enumerate(zip(srcs, dsts))
        ])

    def first(self, index):
        x, z, y, is_me = self.first_target(index == 0)
        wide, narrow = self.rows(x)
        zq, parity, half = lax.rem(self.z, 4), lax.rem(self.y, 2), self.y // 2
        srcs = self.shard.at[wide, 0:256], self.tail.at[narrow]
        dsts = self.main.at[zq, parity, half, wide], self.packed.at[zq, parity, half, narrow]
        far = self.remote(
            srcs, dsts, self.y_send.at[index], self.y_recv.at[half], self.device(x, z, y)
        )
        return is_me, far, srcs, dsts

    def over_y(self):
        for index in range(2):
            is_me, far, srcs, dsts = self.first(index)
            pl.when(self.active & jnp.logical_not(is_me))(far.start)

            @pl.when(self.active & is_me)
            def _():
                for i in range(2):
                    pltpu.make_async_copy(srcs[i], dsts[i], self.local_sems.at[i]).start()

    def second(self, turn, back):
        z, zq, parity = self.from_z(self.order(turn))
        mine = self.piece(zq, parity, self.x)
        return self.remote(
            mine, mine, self.z_send.at[turn, int(back)], self.z_recv.at[z // 2],
            self.device(z=lax.rem(self.z + (7 if back else 1), 8)),
        )

    def seconds(self):
        passive = jnp.logical_not(self.active)
        return (
            (0, True, self.second(0, False)), (0, self.active, self.second(0, True)),
            (1, self.active, self.second(1, False)), (1, passive, self.second(1, True)),
            (2, passive, self.second(2, False)), (2, self.active, self.second(2, True)),
        )

    def over_z(self):
        @pl.when(self.active)
        def _():
            for index in range(2):
                is_me, far, srcs, dsts = self.first(index)
                pl.when(jnp.logical_not(is_me))(far.wait_send)
            for half in range(2):
                is_me = self.first_source(half)[3]
                wide, narrow = self.rows(self.x)
                zq = lax.rem(self.z, 4)
                dst = (
                    self.main.at[zq, self.parity, half, wide],
                    self.packed.at[zq, self.parity, half, narrow],
                )

                @pl.when(is_me)
                def _():
                    self.landed(dst, self.local_sems)

                @pl.when(jnp.logical_not(is_me))
                def _():
                    self.landed(dst, self.y_recv.at[half])

    def from_z(self, index):
        z = 2 * index + self.core
        return z, lax.rem(z, 4), lax.rem(z // 4 + self.y, 2)

    def order(self, turn):
        step = jnp.where(self.active, (0, 6, 2, 4)[turn], (7, 1, 5, 3)[turn])
        return lax.rem(self.z + step, 8) // 2

    def third(self, index, hop):
        z, zq, parity = self.from_z(index)
        owner = self.inner if hop == 2 else self.x
        mine = self.piece(zq, parity, owner)
        return self.remote(
            mine, mine, self.x_send.at[hop, index], self.x_recv.at[owner, index],
            self.device(x=self.outer if hop else self.inner),
        )

    def fourth(self, index, x):
        z, zq, parity = self.from_z(index)
        mine = self.piece(zq, parity, x)
        return self.remote(
            mine, mine, self.c_send.at[x, index], self.c_recv.at[x, index],
            self.device(core=1 - self.core),
        )

    def start_x(self, turn):
        index = self.order(turn)
        z, zq, parity = self.from_z(index)

        @pl.when(z != self.z)
        def _():
            self.landed(self.piece(zq, parity, self.x), self.z_recv.at[index])
        for other, live, copy in self.seconds():
            if other == turn:
                pl.when(live)(copy.start)
        self.third(index, 0).start()
        self.third(index, 1).start()
        self.fourth(index, self.x).start()

    def pass_on(self, x, turn):
        index = self.order(turn)
        z, zq, parity = self.from_z(index)
        self.landed(self.piece(zq, parity, x), self.x_recv.at[x, index])
        if x is self.inner:
            self.third(index, 2).start()
        self.fourth(index, x).start()

    def arrive(self):
        for x in range(4):
            for index in range(4):
                z = 2 * index + 1 - self.core
                other = self.piece(lax.rem(z, 4), lax.rem(z // 4 + self.y, 2), x)
                self.landed(other, self.c_recv.at[x, index])

    def finish(self):
        for turn, live, copy in self.seconds():
            pl.when(live)(copy.wait_send)
        for index in range(4):
            for hop in range(3):
                self.third(index, hop).wait_send()
        for x in range(4):
            for index in range(4):
                self.fourth(index, x).wait_send()


def layer(
    qkv_hbm, tan_hbm, seg_ref, turned_hbm, both_ref,
    qkv_ref, tan_ref, turned_ref, shard_ref, count_ref, in_sems, stage, kv_ref, q_ref, counts_ref, kt_ref, s_ref, st_ref, top_ref, sum_ref, acc_ref, part_ref,
    tail, main, packed, rest, landing, rows_ref, total_ref,
    local_sems, kv_send, kv_recv, q_send, q_recv, n_send, n_recv, f_send,
    y_send, y_recv, z_send, z_recv, x_send, x_recv, c_send, c_recv,
    back_send, back_recv, g_send, g_recv,
):
    ctx, dp, y = lax.axis_index("ctx"), lax.axis_index("dp"), lax.axis_index("head")
    x_lo, z, x_hi, core = ctx // 8, lax.rem(ctx, 8), dp // 2, lax.rem(dp, 2)
    sample = lax.rem(z, 2)
    role = role_of(x_lo, core)
    first, count = work_of(x_lo, z, core)
    weights = Weights(
        shard_ref, tail, main, packed, local_sems.at[pl.ds(4, 2)],
        y_send, y_recv, z_send, z_recv, x_send, x_recv, c_send, c_recv,
    )

    def at(other_x, other_z, other_core):
        return {"ctx": other_x * 8 + other_z, "dp": x_hi * 2 + other_core}

    def is_me(other_x, other_z, other_core):
        return (other_x == x_lo) & (other_z == z) & (other_core == core)

    def remote(src, dst, send, recv, device):
        return pltpu.make_async_remote_copy(
            src_ref=src, dst_ref=dst, send_sem=send, recv_sem=recv, device_id=at(*device),
            device_id_type=MESH,
        )

    def rows_of(block):
        return pl.ds(pl.multiple_of(block * ROWS, ROWS), ROWS)

    loads = [
        pltpu.make_async_copy(src, dst, in_sems.at[i]) for i, (src, dst) in enumerate(
            ((qkv_hbm, qkv_ref), (tan_hbm, tan_ref), (turned_hbm, turned_ref))
        )
    ]
    for load in loads:
        load.start()
    barrier = pltpu.get_barrier_semaphore()
    for other_x in range(2):
        for step in range(8):
            source = (other_x, lax.rem(z + step, 8), sample)
            signal_if(jnp.logical_not(is_me(*source)), barrier, at(*source))
    for mate in ((1 - x_lo, z, core), (x_lo, z, 1 - core), (1 - x_lo, z, 1 - core)):
        signal_if(True, barrier, at(*mate))
    weights.greet(barrier)
    workers = [worker_of(h, ctx, core) for h in range(HEADS)]
    for worker in workers:
        signal_if(jnp.logical_not(is_me(*worker)), barrier, at(*worker))
    for step in range(1, 4):
        signal_if(True, barrier, {"head": lax.rem(y + step, 4)})
    for step in (2, 6):
        signal_if(role == 3, barrier, at(1, lax.rem(z + step, 8), 1))
    own_block = (core == sample) & (first <= ctx) & (ctx < first + count)
    lane = lax.broadcasted_iota(jnp.int32, (8, 128), 1)
    tally = jnp.zeros((8, 128), jnp.int32)
    for v in range(SEGS - 1):
        below = jnp.sum((seg_ref[...] <= v).astype(jnp.int32), axis=1, keepdims=True)
        tally = jnp.where(lane == v, below, tally)
    count_ref[...] = tally
    for load in loads:
        load.wait()
    shard_ref[...] = turned_ref[...].T
    weights.prepare()
    for slot in (4, 5):
        @pl.when(slot >= count)
        def _():
            q_ref[slot * ROWS:(slot + 1) * ROWS] = jnp.zeros((ROWS, 2 * HD), jnp.bfloat16)
    for head in range(HEADS):
        cols = slice(head * HD, (head + 1) * HD)
        stage[head, 0, :, 0:HD] = qkv_ref[1, :, cols]
        stage[head, 0, :, HD:] = tan_ref[1, :, cols]
        stage[head, 1, :, 0:HD] = qkv_ref[2, :, cols]
        stage[head, 1, :, HD:] = tan_ref[2, :, cols]
        stage[head, 2, :, 0:HD] = tan_ref[0, :, cols]
        stage[head, 2, :, HD:] = qkv_ref[0, :, cols]
    pl.semaphore_wait(
        barrier,
        22 - (core == sample).astype(jnp.int32) + weights.greetings()
        + count - own_block.astype(jnp.int32) + 2 * (role == 3).astype(jnp.int32),
    )
    weights.over_y()

    sends = []

    def send(device, src, dst, send_sem, recv_sem, local_sem, live=True):
        mine = is_me(*device)
        far = remote(src, dst, send_sem, recv_sem, device)
        away = live & jnp.logical_not(mine)
        pl.when(away)(far.start)

        @pl.when(mine)
        def _():
            pltpu.make_async_copy(src, dst, local_sem).start()
        sends.append((away, far))

    for other_x in range(2):
        for step in range(4):
            device = (other_x, 2 * lax.rem(z // 2 + step, 4) + core)
            for other_core in range(2):
                send(
                    device + (other_core,), count_ref, counts_ref.at[ctx],
                    n_send.at[other_x, step, other_core], n_recv.at[ctx], local_sems.at[0],
                )
    for head in range(HEADS):
        slot = lax.rem(ctx, 4) if head == 4 else ctx - chunk_start(chunk_of(ctx))
        send(
            worker_of(head, ctx, core), stage.at[head, 2], q_ref.at[rows_of(slot)],
            q_send.at[head], q_recv.at[slot], local_sems.at[2],
        )
    weights.over_z()
    def send_keys(step):
        turn = lax.rem(z // 2 + (0, 1, 3, 2)[step], 4)
        slice_z = 2 * turn + core
        send(
            (x_lo, slice_z, jnp.where(x_lo == 0, core, 0)), stage.at[turn, 0:2],
            kv_ref.at[:, rows_of(ctx)], kv_send.at[0, step], kv_recv.at[ctx], local_sems.at[1],
        )
        steps = lax.rem(slice_z - z + 8, 8)
        send(
            (1, slice_z, 1), stage.at[HEADS - 1, 0:2], kv_ref.at[:, rows_of(ctx)],
            kv_send.at[1, step], kv_recv.at[ctx], local_sems.at[1], (steps <= 2) | (steps >= 6),
        )

    entry = (x_lo == 0) & (core == sample)
    third = role == 2

    def forward(block, mate, index):
        dst = kv_ref.at[:, rows_of(block)]
        return remote(dst, dst, f_send.at[block, index], kv_recv.at[block], mate)

    def forwards(direct, block):
        to_core = (entry, forward(block, (0, z, 1 - core), 0))
        if direct:
            to_x = forward(block, (1 - x_lo, z, jnp.where(entry, 0, sample)), 1)
            return [to_core, (entry | third, to_x)]
        return [to_core]

    def arrived(block, ref, own_sem, sem):
        mine = (block == ctx) & (core == sample)

        @pl.when(mine)
        def _():
            pltpu.make_async_copy(ref, ref, own_sem).wait()

        @pl.when(jnp.logical_not(mine))
        def _():
            pltpu.make_async_copy(ref, ref, sem).wait()

    chain = {6: 2, 7: 2, 1: 6}

    def on(block, step):
        dst = kv_ref.at[:, rows_of(block)]
        return remote(
            dst, dst, f_send.at[block, 0], kv_recv.at[block], (1, lax.rem(z + chain[step], 8), 1)
        )

    def pass_keys(direct, step):
        block = (x_lo if direct else 1 - x_lo) * 8 + lax.rem(z + step, 8)

        @pl.when(role != 3)
        def _():
            arrived(block, kv_ref.at[:, rows_of(block)], local_sems.at[1], kv_recv.at[block])
            for live, copy in forwards(direct, block):
                pl.when(live)(copy.start)

        if direct:
            @pl.when(role == 3)
            def _():
                for other_x in range(2):
                    block = other_x * 8 + lax.rem(z + step, 8)
                    ref = kv_ref.at[:, rows_of(block)]
                    arrived(block, ref, local_sems.at[1], kv_recv.at[block])
                    if step in chain:
                        on(block, step).start()

    near = (0, 1, 7, 2, 6, 3, 5, 4)

    def events(order):
        for kind, turn in order:
            if kind in "DR":
                pass_keys(kind == "D", near[turn])
            elif kind == "X":
                weights.start_x(turn)
            elif kind == "K":
                send_keys(turn)
            else:
                x = {"I": weights.inner, "O": weights.outer, "F": weights.far}[kind]
                weights.pass_on(x, turn)

    events(ORDERS[0])
    for direct in (True, False):
        for step in range(8):
            block = (x_lo if direct else 1 - x_lo) * 8 + lax.rem(z + step, 8)
            arrived(block, counts_ref.at[block], local_sems.at[0], n_recv.at[block])
    for slot in range(SLOTS):
        @pl.when(slot < count)
        def _():
            arrived(first + slot, q_ref.at[rows_of(slot)], local_sems.at[2], q_recv.at[slot])

    def back(slot):
        block = lax.min(first + slot, BLOCKS - 1)
        head = jnp.where(role == 3, HEADS - 1, z // 2)
        own = (block == ctx) & (core == sample)
        dst = landing.at[y, head]
        far = pltpu.make_async_remote_copy(
            src_ref=part_ref.at[slot], dst_ref=dst, send_sem=back_send.at[slot],
            recv_sem=back_recv.at[head], device_id={"ctx": block, "dp": x_hi * 2 + sample},
            device_id_type=MESH,
        )
        return (slot < count) & own, (slot < count) & jnp.logical_not(own), far, dst

    scale = 1.0 / math.sqrt(HD)
    power = scale / math.log(2.0)
    below = jnp.sum(counts_ref[...], axis=0)
    bounds = [below[0:1, v:v + 1] for v in range(SEGS - 1)]

    def of_position(position, values):
        result = values[SEGS - 1]
        for v in range(SEGS - 2, -1, -1):
            result = jnp.where(position < bounds[v], values[v], result)
        return result

    starts = [jnp.zeros((1, 1), jnp.int32)] + bounds
    ends = bounds + [jnp.full((1, 1), SEQ, jnp.int32)]

    @pl.loop(0, KTILES)
    def _(tile):
        keys = pl.ds(pl.multiple_of(tile * TILE, TILE), TILE)
        kt_ref[tile] = kv_ref[0, keys].T

    for part in range(2):
        position = (first + 3 * part) * ROWS + lax.broadcasted_iota(jnp.int32, (PART, 1), 0)
        start = of_position(position, starts)
        end = of_position(position, ends)
        column = lax.broadcasted_iota(jnp.int32, (1, TILE), 1)
        rows = slice(part * PART, (part + 1) * PART)
        top_ref[...] = jnp.full_like(top_ref, -1e30)
        sum_ref[...] = jnp.zeros_like(sum_ref)
        acc_ref[...] = jnp.zeros_like(acc_ref)

        @pl.loop(0, KTILES)
        def _(tile):
            s = jnp.dot(
                q_ref[rows, HD:], kt_ref[tile, 0:HD], preferred_element_type=jnp.float32
            )
            place = column + tile * TILE
            s = jnp.where((place >= start) & (place < end), s, -1e30)
            s_ref[tile] = s
            st_ref[tile] = jnp.dot(
                q_ref[rows, :], kt_ref[tile], preferred_element_type=jnp.float32
            )
            top_ref[...] = jnp.maximum(top_ref[...], fold(jnp.maximum, s))

        top = jnp.max(top_ref[...], axis=1, keepdims=True)

        @pl.loop(0, KTILES)
        def _(tile):
            keys = pl.ds(pl.multiple_of(tile * TILE, TILE), TILE)
            prob = jnp.exp2((s_ref[tile] - top) * power)
            weighted = prob * st_ref[tile]
            sum_ref[0] += fold(jnp.add, prob)
            sum_ref[1] += fold(jnp.add, weighted)
            acc_ref[:, 0:2 * HD] += jnp.dot(
                prob.astype(jnp.bfloat16), kv_ref[1, keys], preferred_element_type=jnp.float32
            )
            acc_ref[:, 2 * HD:] += jnp.dot(
                weighted.astype(jnp.bfloat16), kv_ref[1, keys, 0:HD],
                preferred_element_type=jnp.float32,
            )

        inverse = 1.0 / jnp.sum(sum_ref[0], axis=1, keepdims=True)
        drift = jnp.sum(sum_ref[1], axis=1, keepdims=True) * scale
        plain = acc_ref[:, 0:HD] * inverse
        turned = (acc_ref[:, HD:2 * HD] + acc_ref[:, 2 * HD:] * scale - drift * plain) * inverse
        for slot in range(3):
            piece = slice(slot * ROWS, (slot + 1) * ROWS)
            part_ref[part * 3 + slot, 0] = plain[piece].astype(jnp.bfloat16)
            part_ref[part * 3 + slot, 1] = turned[piece].astype(jnp.bfloat16)
        for slot in range(part * 3, part * 3 + 3):
            own, live, far, dst = back(slot)
            pl.when(live)(far.start)

            @pl.when(own)
            def _():
                pltpu.make_async_copy(part_ref.at[slot], dst, local_sems.at[3]).start()
        events(ORDERS[1 + part])

    def to_y(owner, h, step, index):
        piece = landing.at[owner, h]
        return pltpu.make_async_remote_copy(
            src_ref=piece, dst_ref=piece, send_sem=g_send.at[h, index],
            recv_sem=g_recv.at[owner, h], device_id={"head": lax.rem(y + step, 4)}, device_id_type=MESH,
        )

    def gathers(h):
        owner, step = (3, 1) if h < 3 else (1, 3)
        return (
            to_y(y, h, 1, 0), to_y(y, h, 3, 1), to_y(lax.rem(y + owner, 4), h, step, 2),
        )

    for h in range(HEADS):
        mine = is_me(*workers[h])

        @pl.when(mine)
        def _():
            pltpu.make_async_copy(part_ref.at[0], landing.at[y, h], local_sems.at[3]).wait()

        @pl.when(jnp.logical_not(mine))
        def _():
            pltpu.make_async_copy(part_ref.at[0], landing.at[y, h], back_recv.at[h]).wait()
        for copy in gathers(h)[0:2]:
            copy.start()

    events(ORDERS[3])
    weights.arrive()
    for zq in range(4):
        for parity in range(2):
            for half in range(2):
                for quarter in range(4):
                    for side in range(2):
                        row = quarter * 160 + side * 80
                        rest[parity, half, row:row + 80, zq * 64:(zq + 1) * 64] = packed[
                            zq, parity, half, quarter * 80:(quarter + 1) * 80, side * 64:(side + 1) * 64
                        ]

    def gathered(step, h):
        other = lax.rem(y + step, 4)
        pltpu.make_async_copy(part_ref.at[0], landing.at[other, h], g_recv.at[other, h]).wait()

    for turn, step in enumerate((0, 1, 3, 2)):
        other = lax.rem(y + step, 4)
        if turn == 1:
            for h in range(HEADS):
                gathered(1, h)
                if h < 3:
                    gathered(3, h)
                gathers(h)[2].start()
        for h in range(HEADS):
            if step == 2 or (step == 3 and h >= 3):
                gathered(step, h)
            for kind in range(2):
                rows_ref[kind * ROWS:(kind + 1) * ROWS, h * HD:(h + 1) * HD] = landing[other, h, kind]
        parity, half = lax.rem(other, 2), other // 2
        for zq in range(5):
            weight = main[zq, parity, half] if zq < 4 else rest[parity, half]
            term = jnp.dot(rows_ref[...], weight, preferred_element_type=jnp.float32)
            total_ref[zq] = term if turn == 0 else total_ref[zq] + term

    for zq in range(4):
        for kind in range(2):
            rows = slice(kind * ROWS, (kind + 1) * ROWS)
            both_ref[kind, :, zq * 320:zq * 320 + 256] = total_ref[zq, rows].astype(jnp.bfloat16)
            both_ref[kind, :, zq * 320 + 256:(zq + 1) * 320] = (
                total_ref[4, rows, zq * 64:(zq + 1) * 64].astype(jnp.bfloat16)
            )

    for direct in (True, False):
        for step in range(8):
            block = (x_lo if direct else 1 - x_lo) * 8 + lax.rem(z + step, 8)
            for live, copy in forwards(direct, block):
                pl.when(live)(copy.wait_send)
    @pl.when(role == 3)
    def _():
        for step in chain:
            for other_x in range(2):
                on(other_x * 8 + lax.rem(z + step, 8), step).wait_send()
    for live, copy in sends:
        pl.when(live)(copy.wait_send)
    for slot in range(SLOTS):
        own, live, far, dst = back(slot)
        pl.when(live)(far.wait_send)
    for h in range(HEADS):
        for copy in gathers(h):
            copy.wait_send()
    weights.finish()


def local(qkv, tangent, segments, out_weight):
    vmem = pl.BlockSpec(memory_space=pltpu.VMEM)
    dma = pltpu.SemaphoreType.DMA
    bf16, f32 = jnp.bfloat16, jnp.float32
    hbm = pl.BlockSpec(memory_space=pl.ANY)
    both = pl.pallas_call(
        layer,
        out_shape=jax.ShapeDtypeStruct((2, ROWS, 1280), bf16),
        in_specs=[hbm, hbm, vmem, hbm],
        out_specs=vmem,
        scratch_shapes=[
            pltpu.VMEM((3, ROWS, HEADS * HD), bf16),
            pltpu.VMEM((3, ROWS, HEADS * HD), bf16),
            pltpu.VMEM((320, 640), bf16),
            pltpu.VMEM((640, 320), bf16),
            pltpu.VMEM((8, 128), jnp.int32),
            dma((3,)),
            pltpu.VMEM((HEADS, 3, ROWS, 2 * HD), bf16),
            pltpu.VMEM((2, SEQ, 2 * HD), bf16),
            pltpu.VMEM((SLOTS * ROWS, 2 * HD), bf16),
            pltpu.VMEM((BLOCKS, 8, 128), jnp.int32),
            pltpu.VMEM((KTILES, 2 * HD, TILE), bf16),
            pltpu.VMEM((KTILES, PART, TILE), f32),
            pltpu.VMEM((KTILES, PART, TILE), f32),
            pltpu.VMEM((PART, 128), f32),
            pltpu.VMEM((2, PART, 128), f32),
            pltpu.VMEM((PART, 3 * HD), f32),
            pltpu.VMEM((SLOTS, 2, ROWS, HD), bf16),
            pltpu.VMEM((320, 128), bf16),
            pltpu.VMEM((4, 2, 2, 640, 256), bf16),
            pltpu.VMEM((4, 2, 2, 320, 128), bf16),
            pltpu.VMEM((2, 2, 640, 256), bf16),
            pltpu.VMEM((4, HEADS, 2, ROWS, HD), bf16),
            pltpu.VMEM((2 * ROWS, HEADS * HD), bf16),
            pltpu.VMEM((5, 2 * ROWS, 256), f32),
            dma((6,)), dma((2, 4)), dma((BLOCKS,)), dma((HEADS,)), dma((SLOTS,)),
            dma((2, 4, 2)), dma((BLOCKS,)), dma((BLOCKS, 2)),
            dma((2, 2)), dma((2, 2)), dma((3, 2, 2)), dma((4, 2)),
            dma((3, 4, 2)), dma((4, 4, 2)), dma((4, 4, 2)), dma((4, 4, 2)),
            dma((SLOTS,)), dma((HEADS,)), dma((HEADS, 3)), dma((4, HEADS)),
        ],
        compiler_params=pltpu.CompilerParams(
            collective_id=0, has_side_effects=True, vmem_limit_bytes=56 * 2**20
        ),
        name="layer",
    )(qkv, tangent, segments.reshape(1, ROWS), out_weight.T)
    return both[0], both[1]


def solution(mesh):
    return jax.shard_map(
        local,
        mesh=mesh,
        in_specs=(
            P(None, ("dp", "ctx"), "head"),
            P(None, ("dp", "ctx"), "head"),
            P(("dp", "ctx")),
            P("head", "ctx"),
        ),
        out_specs=(P(("dp", "ctx"), "head"), P(("dp", "ctx"), "head")),
        check_vma=False,
    )
```

```python
import functools
import math

import jax
import jax.numpy as jnp
from jax import lax
from jax.experimental import pallas as pl
from jax.experimental.pallas import tpu as pltpu
from jax.sharding import PartitionSpec as P

HD = 128
HEADS = 5
BLOCKS = 16
ROWS = 160
SEQ = BLOCKS * ROWS
SLOTS = 6
SEGS = 4
TILE = 512
PART = 480


def several(kind, first, last):
    return [(kind, turn) for turn in range(first, last)]


ORDERS = (
    several("X", 0, 1) + several("K", 0, 2) + several("X", 1, 3) + several("K", 2, 4) + several("D", 0, 2)
    + several("X", 3, 4) + several("D", 2, 5) + several("I", 0, 4) + several("D", 5, 8) + several("R", 0, 8),
    several("O", 0, 4),
    [],
    several("F", 0, 4),
)
KTILES = SEQ // TILE
MESH = pl.DeviceIdType.MESH


def role_of(x_lo, core):
    return x_lo * 2 + core


def chunk_of(block):
    return (block >= 6).astype(jnp.int32) + (block >= 11).astype(jnp.int32)


def chunk_start(chunk):
    return chunk * 5 + jnp.minimum(chunk, 1)


def work_of(x_lo, z, core):
    role = role_of(x_lo, core)
    first = jnp.where(role == 3, 4 * (z // 2), chunk_start(role))
    count = jnp.where(role == 3, 4, 5 + (role == 0).astype(jnp.int32))
    return first, count


def worker_of(head, block, core):
    if head == HEADS - 1:
        return 1, 2 * (block // 4) + core, 1
    role = chunk_of(block)
    return role // 2, 2 * head + core, lax.rem(role, 2)


def fold(op, values):
    parts = [values[:, i:i + 128] for i in range(0, values.shape[1], 128)]
    while len(parts) > 1:
        parts = [op(a, b) for a, b in zip(parts[0::2], parts[1::2])]
    return parts[0]


def signal_if(condition, semaphore, device):
    @pl.when(condition)
    def _():
        pl.semaphore_signal(semaphore, inc=1, device_id=device, device_id_type=MESH)


class Both:
    def __init__(self, copies):
        self.copies = copies

    def start(self):
        for copy in self.copies:
            copy.start()

    def wait_send(self):
        for copy in self.copies:
            copy.wait_send()


class Weights:
    def __init__(self, shard_ref, tail_ref, main_ref, packed_ref, local_sems, *sems):
        self.shard, self.tail, self.local_sems = shard_ref, tail_ref, local_sems
        self.main, self.packed = main_ref, packed_ref
        (self.y_send, self.y_recv, self.z_send, self.z_recv,
         self.x_send, self.x_recv, self.c_send, self.c_recv) = sems
        self.ctx, self.y, dp = lax.axis_index("ctx"), lax.axis_index("head"), lax.axis_index("dp")
        self.x_lo, self.z = self.ctx // 8, lax.rem(self.ctx, 8)
        self.x_hi, self.core = dp // 2, lax.rem(dp, 2)
        self.x = self.x_hi * 2 + self.x_lo
        self.inner = self.x_hi * 2 + 1 - self.x_lo
        self.outer = lax.rem(self.x + 3 + 2 * self.x_lo, 4)
        self.far = lax.rem(self.x + 2, 4)
        self.active = lax.rem(self.z, 2) == self.core
        self.parity = lax.rem(self.z // 4 + self.y, 2)

    def prepare(self):
        for quarter in range(4):
            for side in range(2):
                row = quarter * 160 + side * 80
                self.tail[quarter * 80:(quarter + 1) * 80, side * 64:(side + 1) * 64] = (
                    self.shard[row:row + 80, 256:320]
                )

    def device(self, x=None, z=None, y=None, core=None):
        x = self.x if x is None else x
        z = self.z if z is None else z
        y = self.y if y is None else y
        core = self.core if core is None else core
        return {"ctx": lax.rem(x, 2) * 8 + z, "head": y, "dp": (x // 2) * 2 + core}

    def first_target(self, same):
        y = self.x_lo * 2 + self.z // 4
        x = self.x if same else self.x_hi * 2 + 1 - self.x_lo
        z = lax.rem(self.z + 4 * lax.rem(self.y, 2), 8)
        is_me = (x == self.x) & (y == self.y) & (z == self.z)
        return x, z, y, is_me

    def first_source(self, half):
        y = 2 * half + self.parity
        x = self.x_hi * 2 + self.y // 2
        z = lax.rem(self.z + 4 * self.parity, 8)
        is_me = (x == self.x) & (y == self.y) & (z == self.z)
        return x, z, y, is_me

    def greet(self, barrier):
        for half in range(2):
            x, z, y, is_me = self.first_source(half)
            signal_if(self.active & jnp.logical_not(is_me), barrier, self.device(x, z, y))
        for x in (self.inner, self.outer):
            signal_if(True, barrier, self.device(x=x))
        signal_if(True, barrier, self.device(core=1 - self.core))
        for step in (1, 7):
            signal_if(True, barrier, self.device(z=lax.rem(self.z + step, 8)))

    def greetings(self):
        count = jnp.int32(5)
        for same in (True, False):
            is_me = self.first_target(same)[3]
            count = count + (self.active & jnp.logical_not(is_me)).astype(jnp.int32)
        return count

    def rows(self, quarter):
        return (
            pl.ds(pl.multiple_of(quarter * 160, 160), 160),
            pl.ds(pl.multiple_of(quarter * 80, 80), 80),
        )

    def piece(self, zq, parity, x):
        wide, narrow = self.rows(x)
        return self.main.at[zq, parity, :, wide], self.packed.at[zq, parity, :, narrow]

    def landed(self, refs, sems):
        for i, ref in enumerate(refs):
            pltpu.make_async_copy(ref, ref, sems.at[i]).wait()

    def remote(self, srcs, dsts, send, recv, device):
        return Both([
            pltpu.make_async_remote_copy(
                src_ref=src, dst_ref=dst, send_sem=send.at[i], recv_sem=recv.at[i],
                device_id=device, device_id_type=MESH,
            ) for i, (src, dst) in enumerate(zip(srcs, dsts))
        ])

    def first(self, index):
        x, z, y, is_me = self.first_target(index == 0)
        wide, narrow = self.rows(x)
        zq, parity, half = lax.rem(self.z, 4), lax.rem(self.y, 2), self.y // 2
        srcs = self.shard.at[wide, 0:256], self.tail.at[narrow]
        dsts = self.main.at[zq, parity, half, wide], self.packed.at[zq, parity, half, narrow]
        far = self.remote(
            srcs, dsts, self.y_send.at[index], self.y_recv.at[half], self.device(x, z, y)
        )
        return is_me, far, srcs, dsts

    def over_y(self):
        for index in range(2):
            is_me, far, srcs, dsts = self.first(index)
            pl.when(self.active & jnp.logical_not(is_me))(far.start)

            @pl.when(self.active & is_me)
            def _():
                for i in range(2):
                    pltpu.make_async_copy(srcs[i], dsts[i], self.local_sems.at[i]).start()

    def second(self, turn, back):
        z, zq, parity = self.from_z(self.order(turn))
        mine = self.piece(zq, parity, self.x)
        return self.remote(
            mine, mine, self.z_send.at[turn, int(back)], self.z_recv.at[z // 2],
            self.device(z=lax.rem(self.z + (7 if back else 1), 8)),
        )

    def seconds(self):
        passive = jnp.logical_not(self.active)
        return (
            (0, True, self.second(0, False)), (0, self.active, self.second(0, True)),
            (1, self.active, self.second(1, False)), (1, passive, self.second(1, True)),
            (2, passive, self.second(2, False)), (2, self.active, self.second(2, True)),
        )

    def over_z(self):
        @pl.when(self.active)
        def _():
            for index in range(2):
                is_me, far, srcs, dsts = self.first(index)
                pl.when(jnp.logical_not(is_me))(far.wait_send)
            for half in range(2):
                is_me = self.first_source(half)[3]
                wide, narrow = self.rows(self.x)
                zq = lax.rem(self.z, 4)
                dst = (
                    self.main.at[zq, self.parity, half, wide],
                    self.packed.at[zq, self.parity, half, narrow],
                )

                @pl.when(is_me)
                def _():
                    self.landed(dst, self.local_sems)

                @pl.when(jnp.logical_not(is_me))
                def _():
                    self.landed(dst, self.y_recv.at[half])

    def from_z(self, index):
        z = 2 * index + self.core
        return z, lax.rem(z, 4), lax.rem(z // 4 + self.y, 2)

    def order(self, turn):
        step = jnp.where(self.active, (0, 6, 2, 4)[turn], (7, 1, 5, 3)[turn])
        return lax.rem(self.z + step, 8) // 2

    def third(self, index, hop):
        z, zq, parity = self.from_z(index)
        owner = self.inner if hop == 2 else self.x
        mine = self.piece(zq, parity, owner)
        return self.remote(
            mine, mine, self.x_send.at[hop, index], self.x_recv.at[owner, index],
            self.device(x=self.outer if hop else self.inner),
        )

    def fourth(self, index, x):
        z, zq, parity = self.from_z(index)
        mine = self.piece(zq, parity, x)
        return self.remote(
            mine, mine, self.c_send.at[x, index], self.c_recv.at[x, index],
            self.device(core=1 - self.core),
        )

    def start_x(self, turn):
        index = self.order(turn)
        z, zq, parity = self.from_z(index)

        @pl.when(z != self.z)
        def _():
            self.landed(self.piece(zq, parity, self.x), self.z_recv.at[index])
        for other, live, copy in self.seconds():
            if other == turn:
                pl.when(live)(copy.start)
        self.third(index, 0).start()
        self.third(index, 1).start()
        self.fourth(index, self.x).start()

    def pass_on(self, x, turn):
        index = self.order(turn)
        z, zq, parity = self.from_z(index)
        self.landed(self.piece(zq, parity, x), self.x_recv.at[x, index])
        if x is self.inner:
            self.third(index, 2).start()
        self.fourth(index, x).start()

    def arrive(self):
        for x in range(4):
            for index in range(4):
                z = 2 * index + 1 - self.core
                other = self.piece(lax.rem(z, 4), lax.rem(z // 4 + self.y, 2), x)
                self.landed(other, self.c_recv.at[x, index])

    def finish(self):
        for turn, live, copy in self.seconds():
            pl.when(live)(copy.wait_send)
        for index in range(4):
            for hop in range(3):
                self.third(index, hop).wait_send()
        for x in range(4):
            for index in range(4):
                self.fourth(index, x).wait_send()


def layer(
    qkv_hbm, tan_hbm, seg_ref, turned_hbm, both_ref,
    qkv_ref, tan_ref, turned_ref, shard_ref, count_ref, in_sems, stage, kv_ref, q_ref, counts_ref, kt_ref, s_ref, st_ref, top_ref, sum_ref, acc_ref, part_ref,
    tail, main, packed, rest, landing, rows_ref, total_ref,
    local_sems, kv_send, kv_recv, q_send, q_recv, n_send, n_recv, f_send,
    y_send, y_recv, z_send, z_recv, x_send, x_recv, c_send, c_recv,
    back_send, back_recv, g_send, g_recv,
):
    ctx, dp, y = lax.axis_index("ctx"), lax.axis_index("dp"), lax.axis_index("head")
    x_lo, z, x_hi, core = ctx // 8, lax.rem(ctx, 8), dp // 2, lax.rem(dp, 2)
    sample = lax.rem(z, 2)
    role = role_of(x_lo, core)
    first, count = work_of(x_lo, z, core)
    weights = Weights(
        shard_ref, tail, main, packed, local_sems.at[pl.ds(4, 2)],
        y_send, y_recv, z_send, z_recv, x_send, x_recv, c_send, c_recv,
    )

    def at(other_x, other_z, other_core):
        return {"ctx": other_x * 8 + other_z, "dp": x_hi * 2 + other_core}

    def is_me(other_x, other_z, other_core):
        return (other_x == x_lo) & (other_z == z) & (other_core == core)

    def remote(src, dst, send, recv, device):
        return pltpu.make_async_remote_copy(
            src_ref=src, dst_ref=dst, send_sem=send, recv_sem=recv, device_id=at(*device),
            device_id_type=MESH,
        )

    def rows_of(block):
        return pl.ds(pl.multiple_of(block * ROWS, ROWS), ROWS)

    loads = [
        pltpu.make_async_copy(src, dst, in_sems.at[i]) for i, (src, dst) in enumerate(
            ((qkv_hbm, qkv_ref), (tan_hbm, tan_ref), (turned_hbm, turned_ref))
        )
    ]
    for load in loads:
        load.start()
    barrier = pltpu.get_barrier_semaphore()
    for other_x in range(2):
        for step in range(8):
            source = (other_x, lax.rem(z + step, 8), sample)
            signal_if(jnp.logical_not(is_me(*source)), barrier, at(*source))
    for mate in ((1 - x_lo, z, core), (x_lo, z, 1 - core), (1 - x_lo, z, 1 - core)):
        signal_if(True, barrier, at(*mate))
    weights.greet(barrier)
    workers = [worker_of(h, ctx, core) for h in range(HEADS)]
    for worker in workers:
        signal_if(jnp.logical_not(is_me(*worker)), barrier, at(*worker))
    for step in range(1, 4):
        signal_if(True, barrier, {"head": lax.rem(y + step, 4)})
    for step in (2, 6):
        signal_if(role == 3, barrier, at(1, lax.rem(z + step, 8), 1))
    own_block = (core == sample) & (first <= ctx) & (ctx < first + count)
    lane = lax.broadcasted_iota(jnp.int32, (8, 128), 1)
    tally = jnp.zeros((8, 128), jnp.int32)
    for v in range(SEGS - 1):
        below = jnp.sum((seg_ref[...] <= v).astype(jnp.int32), axis=1, keepdims=True)
        tally = jnp.where(lane == v, below, tally)
    count_ref[...] = tally
    for load in loads:
        load.wait()
    shard_ref[...] = turned_ref[...].T
    weights.prepare()
    for slot in (4, 5):
        @pl.when(slot >= count)
        def _():
            q_ref[slot * ROWS:(slot + 1) * ROWS] = jnp.zeros((ROWS, 2 * HD), jnp.bfloat16)
    for head in range(HEADS):
        cols = slice(head * HD, (head + 1) * HD)
        stage[head, 0, :, 0:HD] = qkv_ref[1, :, cols]
        stage[head, 0, :, HD:] = tan_ref[1, :, cols]
        stage[head, 1, :, 0:HD] = qkv_ref[2, :, cols]
        stage[head, 1, :, HD:] = tan_ref[2, :, cols]
        stage[head, 2, :, 0:HD] = tan_ref[0, :, cols]
        stage[head, 2, :, HD:] = qkv_ref[0, :, cols]
    pl.semaphore_wait(
        barrier,
        22 - (core == sample).astype(jnp.int32) + weights.greetings()
        + count - own_block.astype(jnp.int32) + 2 * (role == 3).astype(jnp.int32),
    )
    weights.over_y()

    sends = []

    def send(device, src, dst, send_sem, recv_sem, local_sem, live=True):
        mine = is_me(*device)
        far = remote(src, dst, send_sem, recv_sem, device)
        away = live & jnp.logical_not(mine)
        pl.when(away)(far.start)

        @pl.when(mine)
        def _():
            pltpu.make_async_copy(src, dst, local_sem).start()
        sends.append((away, far))

    for other_x in range(2):
        for step in range(4):
            device = (other_x, 2 * lax.rem(z // 2 + step, 4) + core)
            for other_core in range(2):
                send(
                    device + (other_core,), count_ref, counts_ref.at[ctx],
                    n_send.at[other_x, step, other_core], n_recv.at[ctx], local_sems.at[0],
                )
    for head in range(HEADS):
        slot = lax.rem(ctx, 4) if head == 4 else ctx - chunk_start(chunk_of(ctx))
        send(
            worker_of(head, ctx, core), stage.at[head, 2], q_ref.at[rows_of(slot)],
            q_send.at[head], q_recv.at[slot], local_sems.at[2],
        )
    weights.over_z()
    def send_keys(step):
        turn = lax.rem(z // 2 + (0, 1, 3, 2)[step], 4)
        slice_z = 2 * turn + core
        send(
            (x_lo, slice_z, jnp.where(x_lo == 0, core, 0)), stage.at[turn, 0:2],
            kv_ref.at[:, rows_of(ctx)], kv_send.at[0, step], kv_recv.at[ctx], local_sems.at[1],
        )
        steps = lax.rem(slice_z - z + 8, 8)
        send(
            (1, slice_z, 1), stage.at[HEADS - 1, 0:2], kv_ref.at[:, rows_of(ctx)],
            kv_send.at[1, step], kv_recv.at[ctx], local_sems.at[1], (steps <= 2) | (steps >= 6),
        )

    entry = (x_lo == 0) & (core == sample)
    third = role == 2

    def forward(block, mate, index):
        dst = kv_ref.at[:, rows_of(block)]
        return remote(dst, dst, f_send.at[block, index], kv_recv.at[block], mate)

    def forwards(direct, block):
        to_core = (entry, forward(block, (0, z, 1 - core), 0))
        if direct:
            to_x = forward(block, (1 - x_lo, z, jnp.where(entry, 0, sample)), 1)
            return [to_core, (entry | third, to_x)]
        return [to_core]

    def arrived(block, ref, own_sem, sem):
        mine = (block == ctx) & (core == sample)

        @pl.when(mine)
        def _():
            pltpu.make_async_copy(ref, ref, own_sem).wait()

        @pl.when(jnp.logical_not(mine))
        def _():
            pltpu.make_async_copy(ref, ref, sem).wait()

    chain = {6: 2, 7: 2, 1: 6}

    def on(block, step):
        dst = kv_ref.at[:, rows_of(block)]
        return remote(
            dst, dst, f_send.at[block, 0], kv_recv.at[block], (1, lax.rem(z + chain[step], 8), 1)
        )

    def pass_keys(direct, step):
        block = (x_lo if direct else 1 - x_lo) * 8 + lax.rem(z + step, 8)

        @pl.when(role != 3)
        def _():
            arrived(block, kv_ref.at[:, rows_of(block)], local_sems.at[1], kv_recv.at[block])
            for live, copy in forwards(direct, block):
                pl.when(live)(copy.start)

        if direct:
            @pl.when(role == 3)
            def _():
                for other_x in range(2):
                    block = other_x * 8 + lax.rem(z + step, 8)
                    ref = kv_ref.at[:, rows_of(block)]
                    arrived(block, ref, local_sems.at[1], kv_recv.at[block])
                    if step in chain:
                        on(block, step).start()

    near = (0, 1, 7, 2, 6, 3, 5, 4)

    def events(order):
        for kind, turn in order:
            if kind in "DR":
                pass_keys(kind == "D", near[turn])
            elif kind == "X":
                weights.start_x(turn)
            elif kind == "K":
                send_keys(turn)
            else:
                x = {"I": weights.inner, "O": weights.outer, "F": weights.far}[kind]
                weights.pass_on(x, turn)

    events(ORDERS[0])
    for direct in (True, False):
        for step in range(8):
            block = (x_lo if direct else 1 - x_lo) * 8 + lax.rem(z + step, 8)
            arrived(block, counts_ref.at[block], local_sems.at[0], n_recv.at[block])
    for slot in range(SLOTS):
        @pl.when(slot < count)
        def _():
            arrived(first + slot, q_ref.at[rows_of(slot)], local_sems.at[2], q_recv.at[slot])

    def back(slot):
        block = lax.min(first + slot, BLOCKS - 1)
        head = jnp.where(role == 3, HEADS - 1, z // 2)
        own = (block == ctx) & (core == sample)
        dst = landing.at[y, head]
        far = pltpu.make_async_remote_copy(
            src_ref=part_ref.at[slot], dst_ref=dst, send_sem=back_send.at[slot],
            recv_sem=back_recv.at[head], device_id={"ctx": block, "dp": x_hi * 2 + sample},
            device_id_type=MESH,
        )
        return (slot < count) & own, (slot < count) & jnp.logical_not(own), far, dst

    scale = 1.0 / math.sqrt(HD)
    power = scale / math.log(2.0)
    below = jnp.sum(counts_ref[...], axis=0)
    bounds = [below[0:1, v:v + 1] for v in range(SEGS - 1)]

    def of_position(position, values):
        result = values[SEGS - 1]
        for v in range(SEGS - 2, -1, -1):
            result = jnp.where(position < bounds[v], values[v], result)
        return result

    starts = [jnp.zeros((1, 1), jnp.int32)] + bounds
    ends = bounds + [jnp.full((1, 1), SEQ, jnp.int32)]

    @pl.loop(0, KTILES)
    def _(tile):
        keys = pl.ds(pl.multiple_of(tile * TILE, TILE), TILE)
        kt_ref[tile] = kv_ref[0, keys].T

    for part in range(2):
        position = (first + 3 * part) * ROWS + lax.broadcasted_iota(jnp.int32, (PART, 1), 0)
        start = of_position(position, starts)
        end = of_position(position, ends)
        column = lax.broadcasted_iota(jnp.int32, (1, TILE), 1)
        rows = slice(part * PART, (part + 1) * PART)
        top_ref[...] = jnp.full_like(top_ref, -1e30)
        sum_ref[...] = jnp.zeros_like(sum_ref)
        acc_ref[...] = jnp.zeros_like(acc_ref)

        @pl.loop(0, KTILES)
        def _(tile):
            s = jnp.dot(
                q_ref[rows, HD:], kt_ref[tile, 0:HD], preferred_element_type=jnp.float32
            )
            place = column + tile * TILE
            s = jnp.where((place >= start) & (place < end), s, -1e30)
            s_ref[tile] = s
            st_ref[tile] = jnp.dot(
                q_ref[rows, :], kt_ref[tile], preferred_element_type=jnp.float32
            )
            top_ref[...] = jnp.maximum(top_ref[...], fold(jnp.maximum, s))

        top = jnp.max(top_ref[...], axis=1, keepdims=True)

        @pl.loop(0, KTILES)
        def _(tile):
            keys = pl.ds(pl.multiple_of(tile * TILE, TILE), TILE)
            prob = jnp.exp2((s_ref[tile] - top) * power)
            weighted = prob * st_ref[tile]
            sum_ref[0] += fold(jnp.add, prob)
            sum_ref[1] += fold(jnp.add, weighted)
            acc_ref[:, 0:2 * HD] += jnp.dot(
                prob.astype(jnp.bfloat16), kv_ref[1, keys], preferred_element_type=jnp.float32
            )
            acc_ref[:, 2 * HD:] += jnp.dot(
                weighted.astype(jnp.bfloat16), kv_ref[1, keys, 0:HD],
                preferred_element_type=jnp.float32,
            )

        inverse = 1.0 / jnp.sum(sum_ref[0], axis=1, keepdims=True)
        drift = jnp.sum(sum_ref[1], axis=1, keepdims=True) * scale
        plain = acc_ref[:, 0:HD] * inverse
        turned = (acc_ref[:, HD:2 * HD] + acc_ref[:, 2 * HD:] * scale - drift * plain) * inverse
        for slot in range(3):
            piece = slice(slot * ROWS, (slot + 1) * ROWS)
            part_ref[part * 3 + slot, 0] = plain[piece].astype(jnp.bfloat16)
            part_ref[part * 3 + slot, 1] = turned[piece].astype(jnp.bfloat16)
        for slot in range(part * 3, part * 3 + 3):
            own, live, far, dst = back(slot)
            pl.when(live)(far.start)

            @pl.when(own)
            def _():
                pltpu.make_async_copy(part_ref.at[slot], dst, local_sems.at[3]).start()
        events(ORDERS[1 + part])

    def to_y(owner, h, step, index):
        piece = landing.at[owner, h]
        return pltpu.make_async_remote_copy(
            src_ref=piece, dst_ref=piece, send_sem=g_send.at[h, index],
            recv_sem=g_recv.at[owner, h], device_id={"head": lax.rem(y + step, 4)}, device_id_type=MESH,
        )

    def gathers(h):
        owner, step = (3, 1) if h < 3 else (1, 3)
        return (
            to_y(y, h, 1, 0), to_y(y, h, 3, 1), to_y(lax.rem(y + owner, 4), h, step, 2),
        )

    for h in range(HEADS):
        mine = is_me(*workers[h])

        @pl.when(mine)
        def _():
            pltpu.make_async_copy(part_ref.at[0], landing.at[y, h], local_sems.at[3]).wait()

        @pl.when(jnp.logical_not(mine))
        def _():
            pltpu.make_async_copy(part_ref.at[0], landing.at[y, h], back_recv.at[h]).wait()
        for copy in gathers(h)[0:2]:
            copy.start()

    events(ORDERS[3])
    weights.arrive()
    for zq in range(4):
        for parity in range(2):
            for half in range(2):
                for quarter in range(4):
                    for side in range(2):
                        row = quarter * 160 + side * 80
                        rest[parity, half, row:row + 80, zq * 64:(zq + 1) * 64] = packed[
                            zq, parity, half, quarter * 80:(quarter + 1) * 80, side * 64:(side + 1) * 64
                        ]

    def gathered(step, h):
        other = lax.rem(y + step, 4)
        pltpu.make_async_copy(part_ref.at[0], landing.at[other, h], g_recv.at[other, h]).wait()

    for turn, step in enumerate((0, 1, 3, 2)):
        other = lax.rem(y + step, 4)
        if turn == 1:
            for h in range(HEADS):
                gathered(1, h)
                if h < 3:
                    gathered(3, h)
                gathers(h)[2].start()
        for h in range(HEADS):
            if step == 2 or (step == 3 and h >= 3):
                gathered(step, h)
            for kind in range(2):
                rows_ref[kind * ROWS:(kind + 1) * ROWS, h * HD:(h + 1) * HD] = landing[other, h, kind]
        parity, half = lax.rem(other, 2), other // 2
        for zq in range(5):
            weight = main[zq, parity, half] if zq < 4 else rest[parity, half]
            term = jnp.dot(rows_ref[...], weight, preferred_element_type=jnp.float32)
            total_ref[zq] = term if turn == 0 else total_ref[zq] + term

    for zq in range(4):
        for kind in range(2):
            rows = slice(kind * ROWS, (kind + 1) * ROWS)
            both_ref[kind, :, zq * 320:zq * 320 + 256] = total_ref[zq, rows].astype(jnp.bfloat16)
            both_ref[kind, :, zq * 320 + 256:(zq + 1) * 320] = (
                total_ref[4, rows, zq * 64:(zq + 1) * 64].astype(jnp.bfloat16)
            )

    for direct in (True, False):
        for step in range(8):
            block = (x_lo if direct else 1 - x_lo) * 8 + lax.rem(z + step, 8)
            for live, copy in forwards(direct, block):
                pl.when(live)(copy.wait_send)
    @pl.when(role == 3)
    def _():
        for step in chain:
            for other_x in range(2):
                on(other_x * 8 + lax.rem(z + step, 8), step).wait_send()
    for live, copy in sends:
        pl.when(live)(copy.wait_send)
    for slot in range(SLOTS):
        own, live, far, dst = back(slot)
        pl.when(live)(far.wait_send)
    for h in range(HEADS):
        for copy in gathers(h):
            copy.wait_send()
    weights.finish()


def local(qkv, tangent, segments, out_weight):
    vmem = pl.BlockSpec(memory_space=pltpu.VMEM)
    dma = pltpu.SemaphoreType.DMA
    bf16, f32 = jnp.bfloat16, jnp.float32
    hbm = pl.BlockSpec(memory_space=pl.ANY)
    both = pl.pallas_call(
        layer,
        out_shape=jax.ShapeDtypeStruct((2, ROWS, 1280), bf16),
        in_specs=[hbm, hbm, vmem, hbm],
        out_specs=vmem,
        scratch_shapes=[
            pltpu.VMEM((3, ROWS, HEADS * HD), bf16),
            pltpu.VMEM((3, ROWS, HEADS * HD), bf16),
            pltpu.VMEM((320, 640), bf16),
            pltpu.VMEM((640, 320), bf16),
            pltpu.VMEM((8, 128), jnp.int32),
            dma((3,)),
            pltpu.VMEM((HEADS, 3, ROWS, 2 * HD), bf16),
            pltpu.VMEM((2, SEQ, 2 * HD), bf16),
            pltpu.VMEM((SLOTS * ROWS, 2 * HD), bf16),
            pltpu.VMEM((BLOCKS, 8, 128), jnp.int32),
            pltpu.VMEM((KTILES, 2 * HD, TILE), bf16),
            pltpu.VMEM((KTILES, PART, TILE), f32),
            pltpu.VMEM((KTILES, PART, TILE), f32),
            pltpu.VMEM((PART, 128), f32),
            pltpu.VMEM((2, PART, 128), f32),
            pltpu.VMEM((PART, 3 * HD), f32),
            pltpu.VMEM((SLOTS, 2, ROWS, HD), bf16),
            pltpu.VMEM((320, 128), bf16),
            pltpu.VMEM((4, 2, 2, 640, 256), bf16),
            pltpu.VMEM((4, 2, 2, 320, 128), bf16),
            pltpu.VMEM((2, 2, 640, 256), bf16),
            pltpu.VMEM((4, HEADS, 2, ROWS, HD), bf16),
            pltpu.VMEM((2 * ROWS, HEADS * HD), bf16),
            pltpu.VMEM((5, 2 * ROWS, 256), f32),
            dma((6,)), dma((2, 4)), dma((BLOCKS,)), dma((HEADS,)), dma((SLOTS,)),
            dma((2, 4, 2)), dma((BLOCKS,)), dma((BLOCKS, 2)),
            dma((2, 2)), dma((2, 2)), dma((3, 2, 2)), dma((4, 2)),
            dma((3, 4, 2)), dma((4, 4, 2)), dma((4, 4, 2)), dma((4, 4, 2)),
            dma((SLOTS,)), dma((HEADS,)), dma((HEADS, 3)), dma((4, HEADS)),
        ],
        compiler_params=pltpu.CompilerParams(
            collective_id=0, has_side_effects=True, vmem_limit_bytes=56 * 2**20
        ),
        name="layer",
    )(qkv, tangent, segments.reshape(1, ROWS), out_weight.T)
    return both[0], both[1]


def solution(mesh):
    return jax.shard_map(
        local,
        mesh=mesh,
        in_specs=(
            P(None, ("dp", "ctx"), "head"),
            P(None, ("dp", "ctx"), "head"),
            P(("dp", "ctx")),
            P("head", "ctx"),
        ),
        out_specs=(P(("dp", "ctx"), "head"), P(("dp", "ctx"), "head")),
        check_vma=False,
    )
```
